256 devices in a mesh: seq: 64 (over y, z, core), head: 4 (over x).
Axes of the slice: x: 4, y: 4, z: 8, core: 2. Of those that a mesh axis runs over, the one named last changes fastest.
Arguments:
- activations: bfloat16 [8192, 4096], P('seq', 'head'), may hold values from -6 to 6
- grad_out: bfloat16 [8192, 4096], P('seq', 'head'), may hold values from -0.125 to 0.125
- write_proj: bfloat16 [8192, 128], P('seq'), may hold values from -1.75 to 1.75
- read_proj: bfloat16 [8192, 128], P('seq'), may hold values from -1.75 to 1.75
- step_raw: float32 [8192, 64], P('seq', 'head'), may hold values from -2 to 0
- step_table: float32 [1000, 64], P(None, 'head'), may hold values from -0.7 to 0.7
- decay_rate: float32 [64], P('head'), may hold values from 0 to 1, as said below
- frame_step: int32 [4], replicated, may hold values from 0 to 999
- scan_order: int32 [8192], P('seq'), may hold values from 0 to 127, as said below
Outputs:
- grad_act: bfloat16 [8192, 4096], P('seq', 'head')
- grad_write: bfloat16 [8192, 128], P('seq')
- grad_read: bfloat16 [8192, 128], P('seq')
- grad_pre: float32 [8192, 64], P('seq', 'head')
- grad_table: float32 [1000, 64], P(None, 'head')
The draws below stay inside these ranges and needn't reach their ends.
Inputs may be any that keep to these rules, and one draw needn't show every extreme that they name: `scan_order`: within each device's block of 128 entries: a permutation of 0 to 127 in which each aligned run of 2 entries is one run r * 2 to r * 2 + 1, ascending or descending. `decay_rate`: Positive.
All inputs are finite; a program needn't handle non-finite values.
Results may differ from the reference program's by a relative error of at most 0.005.
Values may be sent and summed in bfloat16 or wider, within the bound.
No kernel may reach another device: no remote copies, remote signals or barrier semaphores. Data moves between devices by JAX's collectives and lax.ppermute only.
A program may use at most 192 MiB of HBM per device.

```python
import math
import jax
import jax.numpy as jnp
from jax import lax

HEADS = 64
HEAD_DIM = 64
STATE = 128
SPAN = 128
TSTEPS = 1000
FRAME_TOK = 2048
TOK_DEV = 128
TOKENS = 8192
PIECE = 2
FRAMES = 4


def draw_decay_rate(key, part):
    key = jax.random.fold_in(key, 11)
    levels = jax.random.uniform(key, (HEADS,), jnp.float32)
    floor_log = math.log(0.3 / TOKENS)
    top_log = math.log(0.2)
    return jnp.exp(floor_log + levels * (top_log - floor_log))


def draw_scan_order(key, part):
    key = jax.random.fold_in(key, 23)
    device_count = TOKENS // TOK_DEV
    row_count = TOK_DEV // PIECE
    row_keys = jax.random.split(key, device_count)
    row_order = jax.vmap(lambda sub_key: jax.random.permutation(sub_key, row_count))(row_keys)
    reversed_rows = jax.random.randint(jax.random.fold_in(key, 5), (device_count, row_count), 0, 2)
    offsets = jnp.arange(PIECE, dtype=jnp.int32)
    placed = jnp.where(reversed_rows[:, :, None] == 1, PIECE - 1 - offsets[None, None, :], offsets[None, None, :])
    local_index = row_order[:, :, None].astype(jnp.int32) * PIECE + placed
    return local_index.reshape(TOKENS).astype(jnp.int32)


def touch_ends(values, stream_key, least, high):
    longest = values.shape.index(max(values.shape))
    spots = []
    for shift in (0, 1):
        where = [jax.random.randint(jax.random.fold_in(stream_key, axis), (), 0, length) for axis, length in enumerate(values.shape)]
        where[longest] = (where[longest] + shift) % values.shape[longest]
        spots.append(tuple(where))
    return values.at[spots[0]].set(least).at[spots[1]].set(high)


def shard_levels(own_key, extent, cuts, low, largest):
    gain = 1.0
    for axis_at, blocks in cuts:
        steps = jax.random.uniform(jax.random.fold_in(jax.random.fold_in(own_key, 6), axis_at), (blocks,), jnp.float32, low / len(cuts), largest / len(cuts))
        gain = gain * jnp.repeat(jnp.exp(steps), extent[axis_at] // blocks).reshape((-1,) + (1,) * (len(extent) - 1 - axis_at))
    return gain


def bell_draw(own_key, extent, scale, bound, shards=(), kind=jnp.bfloat16):
    gain = shard_levels(own_key, extent, shards, -0.22, 0.18) if shards else 1.0
    entries = jax.random.normal(own_key, extent, jnp.float32) * scale * gain
    return jnp.minimum(jnp.maximum(entries, -bound), bound).astype(kind)


def setup_inputs(seed: int = 0) -> dict:
    streams_of = jax.random.split(jax.random.key(seed), 10)
    activations = bell_draw(streams_of[0], (TOKENS, HEADS * HEAD_DIM), 1.0, 6.0, ((0, 64), (1, 4)))
    grad_out = bell_draw(streams_of[1], (TOKENS, HEADS * HEAD_DIM), (2 * TOKENS ** -0.5), 0.125, ((0, 64), (1, 4)))
    write_proj = bell_draw(streams_of[2], (TOKENS, STATE), 0.3, 1.75, ((0, 64),))
    read_proj = bell_draw(streams_of[3], (TOKENS, STATE), 0.3, 1.75, ((0, 64),))
    step_raw = jnp.clip(-2.0 + 2.0 * jax.random.uniform(streams_of[4], (TOKENS, HEADS), jnp.float32) ** shard_levels(streams_of[4], (TOKENS, HEADS), ((0, 64), (1, 4)), -0.2, 0.2), -2.0, 0.0)
    step_table = jnp.clip(jax.random.uniform(streams_of[5], (TSTEPS, HEADS), jnp.float32, -0.7, 0.7) * shard_levels(streams_of[5], (TSTEPS, HEADS), ((1, 4),), -0.4, 0.0), -0.7, 0.7)
    decay_rate = draw_decay_rate(jax.random.fold_in(streams_of[9], 71), 0)
    frame_step = touch_ends(jax.random.randint(streams_of[7], (FRAMES,), 0, TSTEPS), jax.random.fold_in(streams_of[7], 1), 0, TSTEPS - 1).astype(jnp.int32)
    scan_order = draw_scan_order(jax.random.fold_in(streams_of[9], 71), 0)
    return dict(activations=activations, grad_out=grad_out, write_proj=write_proj, read_proj=read_proj, step_raw=step_raw, step_table=step_table, decay_rate=decay_rate, frame_step=frame_step, scan_order=scan_order)


precise = lax.Precision.HIGHEST


def state_part(signal, writer, deltas, slopes):
    running = jnp.cumsum(deltas * slopes[None, :], axis=0)
    totals = running[-1]
    to_end = jnp.exp(totals[None, :] - running)
    contrib = jnp.einsum('jhp,jn->hpn', signal * (deltas * to_end)[:, :, None], writer, precision=precise)
    return totals, contrib


def adjoint_part(upstream, reader, deltas, slopes):
    running = jnp.cumsum(deltas * slopes[None, :], axis=0)
    totals = running[-1]
    contrib = jnp.einsum('khp,kn->hpn', upstream * jnp.exp(running)[:, :, None], reader, precision=precise)
    return totals, contrib


def block_grads(signal, upstream, writer, reader, deltas, slopes, state_in, adjoint_in):
    length = signal.shape[0]
    running = jnp.cumsum(deltas * slopes[None, :], axis=0)
    totals = running[-1]
    order_idx = jnp.arange(length)
    lower_mask = order_idx[:, None] >= order_idx[None, :]
    lower_ones = lower_mask.astype(jnp.float32)
    upper_ones = lower_ones.T
    transposed = running.T
    spread = transposed[:, :, None] - transposed[:, None, :]
    decay_low = jnp.exp(jnp.where(lower_mask[None], spread, -jnp.inf))
    scaled = signal * deltas[:, :, None]
    to_end = jnp.exp(totals[None, :] - running)
    head_exp = jnp.exp(running)
    intersection = jnp.dot(reader, writer.T, precision=precise)
    weights = decay_low * intersection[None]
    carried = jnp.einsum('hpn,jn->jhp', adjoint_in, writer, precision=precise)
    upward = jnp.einsum('hki,khp->ihp', weights, upstream, precision=precise) + to_end[:, :, None] * carried
    grad_act = deltas[:, :, None] * upward
    mixing = decay_low * jnp.einsum('ihp,jhp->hij', upstream, scaled, precision=precise)
    grad_read = jnp.einsum('hij,jn->in', mixing, writer, precision=precise) + jnp.einsum(
        'ihp,hpn->in', upstream * head_exp[:, :, None], state_in, precision=precise)
    grad_write = jnp.einsum('hkj,kn->jn', mixing, reader, precision=precise) + jnp.einsum(
        'jhp,hpn->jn', scaled * to_end[:, :, None], adjoint_in, precision=precise)
    crossed = jnp.einsum('ik,hkj->hij', upper_ones, mixing * intersection[None], precision=precise)
    term_one = jnp.sum(crossed * lower_ones[None], axis=2).T
    state_read = jnp.einsum('hpn,kn->khp', state_in, reader, precision=precise)
    term_two = jnp.dot(upper_ones, head_exp * jnp.sum(upstream * state_read, axis=-1), precision=precise)
    term_three = jnp.dot(lower_ones, to_end * jnp.sum(scaled * carried, axis=-1), precision=precise)
    term_four = jnp.exp(totals) * jnp.sum(adjoint_in * state_in, axis=(1, 2))
    direct = jnp.sum(scaled * upward, axis=-1)
    log_grad = term_one + term_two + term_three + term_four[None, :] - direct
    grad_step = jnp.sum(signal * upward, axis=-1) + slopes[None, :] * log_grad
    return grad_act, grad_write, grad_read, grad_step


def reference(activations, grad_out, write_proj, read_proj, step_raw, step_table, decay_rate, frame_step, scan_order):
    position = jnp.arange(TOKENS).astype(jnp.int32)
    frame_idx = frame_step[position // FRAME_TOK]
    pre_step = step_raw + step_table[frame_idx]
    deltas_bf = jax.nn.softplus(pre_step).astype(jnp.bfloat16)
    source = (scan_order // PIECE) * TOK_DEV + (position // TOK_DEV) * PIECE + scan_order % PIECE
    blocks = TOKENS // SPAN
    signal = activations[source].astype(jnp.float32).reshape(blocks, SPAN, HEADS, HEAD_DIM)
    upstream = grad_out[source].astype(jnp.float32).reshape(blocks, SPAN, HEADS, HEAD_DIM)
    writer = write_proj[source].astype(jnp.float32).reshape(blocks, SPAN, STATE)
    reader = read_proj[source].astype(jnp.float32).reshape(blocks, SPAN, STATE)
    deltas = deltas_bf[source].astype(jnp.float32).reshape(blocks, SPAN, HEADS)
    slopes = -decay_rate
    zero_state = jnp.zeros((HEADS, HEAD_DIM, STATE), jnp.float32)

    def backward_step(running, inputs):
        totals, contrib = adjoint_part(inputs[0], inputs[1], inputs[2], slopes)
        return jnp.exp(totals)[:, None, None] * running + contrib, running

    unused, adjoints = lax.scan(backward_step, zero_state, (upstream, reader, deltas), reverse=True)

    def forward_step(running, inputs):
        grads = block_grads(inputs[0], inputs[1], inputs[2], inputs[3], inputs[4], slopes, running, inputs[5])
        totals, contrib = state_part(inputs[0], inputs[2], inputs[4], slopes)
        return jnp.exp(totals)[:, None, None] * running + contrib, grads

    unused_state, results = lax.scan(forward_step, zero_state, (signal, upstream, writer, reader, deltas, adjoints))
    scan_act = results[0].reshape(TOKENS, HEADS * HEAD_DIM).astype(jnp.bfloat16)
    scan_write = results[1].reshape(TOKENS, STATE).astype(jnp.bfloat16)
    scan_read = results[2].reshape(TOKENS, STATE).astype(jnp.bfloat16)
    scan_step = results[3].reshape(TOKENS, HEADS).astype(jnp.bfloat16)
    grad_act = jnp.zeros_like(scan_act).at[source].set(scan_act)
    grad_write = jnp.zeros_like(scan_write).at[source].set(scan_write)
    grad_read = jnp.zeros_like(scan_read).at[source].set(scan_read)
    grad_delta = jnp.zeros_like(scan_step).at[source].set(scan_step)
    grad_pre = grad_delta.astype(jnp.float32) * jax.nn.sigmoid(pre_step)
    grad_table = jax.ops.segment_sum(grad_pre, frame_idx, num_segments=TSTEPS)
    return grad_act, grad_write, grad_read, grad_pre, grad_table
```

```python
import functools

import jax
import jax.numpy as jnp
import numpy as np
from jax import lax
from jax.experimental import pallas as pl
from jax.experimental.pallas import tpu as pltpu
from jax.sharding import PartitionSpec as P

F32 = jnp.float32
BF16 = jnp.bfloat16
FRAME_TOK = 2048
TOK = 128
LANES = 128
SEQ = 64
PARTS = 8
PAIRS = 8
BLOCKS = 8
SLOT_IN = 56
SLOT_STATE = 136
SLOT_OUT = 40
LOCAL = BLOCKS * TOK
PARAMS = pltpu.CompilerParams(vmem_limit_bytes=48 * 1024 * 1024)


def place(part, pair):
    y, low = part // 2, part % 2
    high, core = pair // 2, pair % 2
    return y * 16 + (high * 2 + low) * 2 + core


def my_place():
    me = lax.axis_index("seq")
    part = (me // 16) * 2 + (me // 2) % 2
    pair = ((me // 4) % 4) * 2 + me % 2
    return part, pair, me % 2


STATE_GROUPS = [[place(part, pair) for part in range(PARTS)] for pair in range(PAIRS)]


def nn(a, b):
    return lax.dot_general(a, b, (((1,), (0,)), ((), ())), preferred_element_type=F32)


def nt(a, b):
    return lax.dot_general(a, b, (((1,), (1,)), ((), ())), preferred_element_type=F32)


def split(value):
    high = value.astype(BF16)
    return high, (value - high.astype(F32)).astype(BF16)


def lane_iota(rows):
    return lax.broadcasted_iota(jnp.int32, (rows, LANES), 1)


def heads_over_lanes(first, second, rows):
    return jnp.where(lane_iota(rows) < 64, first, second)


def softplus(value):
    return jnp.maximum(value, 0.0) + jnp.log1p(jnp.exp(-jnp.abs(value)))


def sigmoid(value):
    return 1.0 / (1.0 + jnp.exp(-value))


def shifted_steps(frame_ref, raw_ref, table_ref):
    frame_here = lax.axis_index("seq") * TOK // FRAME_TOK
    index = frame_ref[frame_here]
    return raw_ref[...] + table_ref[pl.ds(index, 1), :]


def pack_kernel(frame_ref, order_ref, x_ref, dy_ref, b_ref, c_ref, raw_ref, table_ref, out_ref):
    heads = raw_ref.shape[1]
    pre = shifted_steps(frame_ref, raw_ref, table_ref)
    pre = jnp.concatenate([pre, jnp.zeros((TOK, LANES - heads), F32)], axis=1)
    pre = pre.T[:heads]
    delta = softplus(pre).astype(BF16).astype(F32)
    gate = sigmoid(pre)
    gate_high = gate.astype(BF16).astype(F32)
    gate_low = gate - gate_high
    order = jnp.broadcast_to(order_ref[...].astype(F32), (TOK, TOK)).T
    lane = lane_iota(TOK)
    token = ((lane % 64) * 2 + lane // 64).astype(F32)
    steps = lax.broadcasted_iota(jnp.int32, (TOK, TOK), 0).astype(F32)
    position = jnp.sum(jnp.where(order == token, steps, 0.0), axis=0, keepdims=True)
    for pair in range(PAIRS):
        own = slice(2 * pair, 2 * pair + 2)
        rows = jnp.concatenate(
            [position, delta[own], gate_high[own], gate_low[own], jnp.zeros((1, LANES), F32)], axis=0
        ).astype(BF16)
        proj_ref = c_ref if pair % 2 else b_ref
        columns = slice(LANES * pair, LANES * pair + LANES)
        for part in range(PARTS):
            slot = place(part, pair)
            tokens = slice(16 * part, 16 * part + 16)
            out_ref[slot, 0:16, :] = x_ref[tokens, columns]
            out_ref[slot, 16:32, :] = dy_ref[tokens, columns]
            out_ref[slot, 32:48, :] = proj_ref[tokens, :]
            out_ref[slot, 48:56, :] = rows


def to_columns(first, second):
    head_one = jnp.concatenate([first, pltpu.roll(first, LANES - 1, 1)], axis=0)
    head_two = jnp.concatenate([pltpu.roll(second, 1, 1), second], axis=0)
    return jnp.where(lane_iota(TOK) % 2 == 0, head_one, head_two)


def slope_lanes(decay_ref, pair, rows):
    first, second = -decay_ref[2 * pair], -decay_ref[2 * pair + 1]
    return first, second, jnp.where(lane_iota(rows) % 2 == 0, first, second)


def unpack_kernel(
    decay_ref, recv_ref, swap_ref,
    x_ref, dy_ref, b_ref, c_ref, send_ref, s_ref, r_ref, stat_ref,
    wide, misc,
):
    part, pair, core = my_place()

    def spread(value, target_ref):
        wide[...] = value.reshape(SEQ * 16, LANES)
        for row in range(16):
            target_ref[row * 64 : row * 64 + 64, :] = wide[pl.ds(row, 64, stride=16), :].astype(BF16)

    spread(recv_ref[:, 0:16, :].astype(F32), x_ref)
    spread(recv_ref[:, 16:32, :].astype(F32), dy_ref)
    mine = recv_ref[:, 32:48, :].astype(F32)
    other = swap_ref[:, 32:48, :].astype(F32)
    spread(jnp.where(core == 0, mine, other), b_ref)
    spread(jnp.where(core == 0, other, mine), c_ref)

    misc[...] = recv_ref[:, 48:56, :].astype(F32).reshape(SEQ * 8, LANES)
    shift = (LANES - 16 * part) % LANES

    def own_lanes(row):
        return pltpu.roll(misc[pl.ds(row, 64, stride=8), :], shift, 1)

    steps = to_columns(own_lanes(1), own_lanes(2))
    gates = to_columns(own_lanes(3) + own_lanes(5), own_lanes(4) + own_lanes(6))
    pos_rows = jnp.concatenate(
        [misc[pl.ds(part * 64 + 8 * block, 1), :] for block in range(BLOCKS)], axis=0
    )
    pos_cols = jnp.concatenate([pos_rows, jnp.zeros((LANES - BLOCKS, LANES), F32)], axis=0).T
    lane = lane_iota(TOK)
    steps_bf = steps.astype(BF16)
    sums = jnp.zeros((TOK, LANES), F32)
    for block in range(BLOCKS):
        later = (pos_cols[:, block : block + 1] >= pos_rows[block : block + 1, :]).astype(F32).astype(BF16)
        sums = jnp.where(lane // 2 == block, nn(later, steps_bf), sums)
    slope_one, slope_two, slopes = slope_lanes(decay_ref, pair, TOK)
    logs = sums * slopes
    totals = jnp.sum(steps, axis=0, keepdims=True) * slopes[:1]
    stat_ref[0] = steps
    stat_ref[1] = logs
    stat_ref[2] = gates
    stat_ref[3] = pos_cols
    stat_ref[4] = jnp.concatenate(
        [pos_rows, jnp.broadcast_to(totals, (8, LANES)), jnp.zeros((LANES - 16, LANES), F32)], axis=0
    )
    weights = steps * jnp.exp(totals - logs)
    starts = jnp.exp(logs)
    state = jnp.zeros((LANES, LANES), F32)
    for block in range(BLOCKS):
        rows = slice(block * TOK, block * TOK + TOK)
        j = 2 * block
        keep = jnp.exp(heads_over_lanes(totals[:, j : j + 1], totals[:, j + 1 : j + 2], 1))
        write_t = b_ref[rows, :].astype(F32).T.astype(BF16)
        read_t = c_ref[rows, :].astype(F32).T.astype(BF16)
        wx = heads_over_lanes(weights[:, j : j + 1], weights[:, j + 1 : j + 2], TOK)
        high, low = split(x_ref[rows, :].astype(F32) * wx)
        gained = nn(write_t, high) + nn(write_t, low)
        s_ref[block] = gained
        state = state * keep + gained
        wd = heads_over_lanes(starts[:, j : j + 1], starts[:, j + 1 : j + 2], TOK)
        high, low = split(dy_ref[rows, :].astype(F32) * wd)
        r_ref[block] = nn(read_t, high) + nn(read_t, low)
    adjoint = jnp.zeros((LANES, LANES), F32)
    whole = jnp.zeros((1, LANES), F32)
    for block in reversed(range(BLOCKS)):
        j = 2 * block
        total = heads_over_lanes(totals[:, j : j + 1], totals[:, j + 1 : j + 2], 1)
        adjoint = adjoint * jnp.exp(total) + r_ref[block]
        whole = whole + total
    top = whole.astype(BF16).astype(F32)
    middle = (whole - top).astype(BF16).astype(F32)
    bottom = whole - top - middle
    tail = jnp.concatenate([top, middle, bottom, jnp.zeros((5, LANES), F32)], axis=0).astype(BF16)
    state = state.astype(BF16)
    adjoint = adjoint.astype(BF16)
    for slot in range(PARTS):
        after = slot > part

        @pl.when(after)
        def _():
            send_ref[slot, 0:128, :] = state

        @pl.when(jnp.logical_not(after))
        def _():
            send_ref[slot, 0:128, :] = adjoint

        send_ref[slot, 128:136, :] = tail


def inner_kernel(x_ref, dy_ref, b_ref, c_ref, stat_ref, u_ref, gw_ref, gr_ref, t_ref):
    steps = stat_ref[0]
    logs = stat_ref[1]
    log_rows = logs.T
    pos_cols = stat_ref[3]
    pos_rows = stat_ref[4][:8]
    lane = lane_iota(TOK)
    t_ref[...] = jnp.zeros((LANES, LANES), F32)
    for block in range(BLOCKS):
        rows = slice(block * TOK, block * TOK + TOK)
        x = x_ref[rows, :]
        dy = dy_ref[rows, :]
        write = b_ref[rows, :]
        read = c_ref[rows, :]
        pos_col = pos_cols[:, block : block + 1]
        pos_row = pos_rows[block : block + 1, :]
        ahead = pos_row >= pos_col
        behind = (pos_col >= pos_row).astype(F32).astype(BF16)
        cross = nt(write, read)
        zero = jnp.zeros_like(dy)
        x_heads = (jnp.where(lane < 64, x, zero), jnp.where(lane < 64, zero, x))
        dy_stack = jnp.concatenate(
            [jnp.where(lane < 64, dy, zero), jnp.where(lane < 64, zero, dy)], axis=0
        )
        carry, mixed = [], []
        for head in range(2):
            j = 2 * block + head
            gap = log_rows[j : j + 1, :] - logs[:, j : j + 1]
            decay = jnp.exp(jnp.where(ahead, gap, -1e30))
            carry.append(decay * cross)
            mixed.append(decay * (nt(x_heads[head], dy) * steps[:, j : j + 1]))
            high, low = split(mixed[head] * cross)
            crossed = nn(high, behind) + nn(low, behind)
            t_ref[j : j + 1, :] = jnp.sum(jnp.where(ahead, crossed, 0.0), axis=0, keepdims=True)
        high, low = split(jnp.concatenate(carry, axis=1))
        u_ref[rows, :] = nn(high, dy_stack) + nn(low, dy_stack)
        both = mixed[0] + mixed[1]
        high, low = split(both)
        gw_ref[rows, :] = nn(high, read) + nn(low, read)
        high, low = split(both.T)
        gr_ref[rows, :] = nn(high, write) + nn(low, write)


def outer_kernel(
    decay_ref, recv_ref, x_ref, dy_ref, b_ref, c_ref, s_ref, r_ref, stat_ref,
    u_ref, gw_ref, gr_ref, t_ref,
    out_ref, keep_ref, give_ref,
    adj, wide, wide_w, wide_r,
):
    part, pair, core = my_place()
    slope_one, slope_two, slopes = slope_lanes(decay_ref, pair, TOK)

    def arrive(slot, state):
        tail = recv_ref[slot, 128:136, :].astype(F32)
        total = tail[0:1] + tail[1:2] + tail[2:3]
        return state * jnp.exp(total) + recv_ref[slot, 0:128, :].astype(F32)

    zero = jnp.zeros((LANES, LANES), F32)
    state = lax.fori_loop(0, part, arrive, zero)
    adjoint = lax.fori_loop(0, PARTS - 1 - part, lambda k, a: arrive(PARTS - 1 - k, a), zero)

    steps = stat_ref[0]
    logs = stat_ref[1]
    gates = stat_ref[2]
    pos_cols = stat_ref[3]
    pos_rows = stat_ref[4][:8]
    totals = stat_ref[4][8:9]
    starts = jnp.exp(logs)
    ends = jnp.exp(totals - logs)
    lane = lane_iota(TOK)
    sub = lax.broadcasted_iota(jnp.int32, (LANES, LANES), 0)

    def total_of(block):
        j = 2 * block
        return heads_over_lanes(totals[:, j : j + 1], totals[:, j + 1 : j + 2], 1)

    for block in reversed(range(BLOCKS)):
        adj[block] = adjoint
        adjoint = adjoint * jnp.exp(total_of(block)) + r_ref[block]

    direct = jnp.zeros((TOK, LANES), F32)
    log_grad = t_ref[...].T
    for block in range(BLOCKS):
        rows = slice(block * TOK, block * TOK + TOK)
        j = 2 * block
        x = x_ref[rows, :].astype(F32)
        dy = dy_ref[rows, :].astype(F32)
        write = b_ref[rows, :]
        read = c_ref[rows, :]
        adjoint = adj[block]
        state_high, state_low = split(state)
        adj_high, adj_low = split(adjoint)
        step = heads_over_lanes(steps[:, j : j + 1], steps[:, j + 1 : j + 2], TOK)
        start = heads_over_lanes(starts[:, j : j + 1], starts[:, j + 1 : j + 2], TOK)
        end = heads_over_lanes(ends[:, j : j + 1], ends[:, j + 1 : j + 2], TOK)
        keep = jnp.exp(total_of(block))
        carried = end * (nn(write, adj_high) + nn(write, adj_low))
        recalled = nn(read, state_high) + nn(read, state_low)
        u = u_ref[rows, :] + carried
        act = step * u
        out_rows = (pl.ds(2 * block, 64, stride=16), pl.ds(2 * block + 1, 64, stride=16))
        wide[out_rows[0], :] = act[:64]
        wide[out_rows[1], :] = act[64:]
        dy_start = start * dy
        x_end = (end * step) * x
        high, low = split(dy_start)
        gr = gr_ref[rows, :] + (nt(high, state_high) + (nt(high, state_low) + nt(low, state_high)))
        high, low = split(x_end)
        gw = gw_ref[rows, :] + (nt(high, adj_high) + (nt(high, adj_low) + nt(low, adj_high)))
        for half in range(2):
            wide_w[out_rows[half], :] = gw[64 * half : 64 * half + 64]
            wide_r[out_rows[half], :] = gr[64 * half : 64 * half + 64]
        pick = (lane == 2 * block + sub // 64).astype(F32).astype(BF16)

        def per_head(value):
            high, low = split(value)
            return nn(high, pick) + nn(low, pick)

        mine = lane // 2 == block
        read_part = per_head(dy_start * recalled)
        write_part = per_head(step * x * carried)
        direct = direct + per_head(x * u)
        ahead = (pos_rows[block : block + 1, :] >= pos_cols[:, block : block + 1]).astype(F32).astype(BF16)
        behind = (pos_cols[:, block : block + 1] >= pos_rows[block : block + 1, :]).astype(F32).astype(BF16)
        high, low = split(read_part)
        added = nn(ahead, high) + nn(ahead, low)
        high, low = split(write_part)
        added = added + (nn(behind, high) + nn(behind, low))
        overlap = jnp.sum(adjoint * state, axis=0, keepdims=True) * keep
        first = jnp.sum(jnp.where(lane_iota(1) < 64, overlap, 0.0), axis=1, keepdims=True)
        second = jnp.sum(jnp.where(lane_iota(1) < 64, 0.0, overlap), axis=1, keepdims=True)
        added = added + jnp.where(lane % 2 == 0, first, second)
        log_grad = log_grad + jnp.where(mine, added, 0.0)
        state = state * keep + s_ref[block]

    log_grad = log_grad - steps * direct
    grad_step = (direct + slopes * log_grad).astype(BF16).astype(F32)
    grad_step = jnp.where(lane < 2 * BLOCKS, grad_step, 0.0)
    grad_pre = grad_step * gates
    frames = []
    for frame in range(4):
        low_rows = slice(16 * frame, 16 * frame + 16)
        high_rows = slice(64 + 16 * frame, 80 + 16 * frame)
        frames.append(jnp.sum(grad_pre[low_rows] + grad_pre[high_rows], axis=0, keepdims=True))
    frames = jnp.concatenate(frames + [jnp.zeros((4, LANES), F32)], axis=0)
    frames_high = frames.astype(BF16).astype(F32)
    frames = frames_high + pltpu.roll(frames - frames_high, 64, 1)

    even = lane_iota(64) % 2 == 0
    top, bottom = grad_step[:64], grad_step[64:]
    shift = 16 * part
    row_one = pltpu.roll(jnp.where(even, top, pltpu.roll(bottom, 1, 1)), shift, 1)
    row_two = pltpu.roll(jnp.where(even, pltpu.roll(top, LANES - 1, 1), bottom), shift, 1)
    misc = jnp.concatenate(
        [
            row_one[:, None, :],
            row_two[:, None, :],
            jnp.broadcast_to(frames[None, :4, :], (SEQ, 4, LANES)),
            jnp.zeros((SEQ, 2, LANES), F32),
        ],
        axis=1,
    )
    out_ref[:, 0:16, :] = wide[...].reshape(SEQ, 16, LANES).astype(BF16)
    out_ref[:, 32:40, :] = misc.astype(BF16)

    @pl.when(core == 0)
    def _():
        keep_ref[...] = wide_w[...]
        give_ref[...] = wide_r[...]

    @pl.when(core == 1)
    def _():
        keep_ref[...] = wide_r[...]
        give_ref[...] = wide_w[...]


def join_kernel(in_ref, keep_ref, got_ref, out_ref):
    out_ref[:, 0:16, :] = in_ref[:, 0:16, :]
    out_ref[:, 16:32, :] = (keep_ref[...] + got_ref[...]).reshape(SEQ, 16, LANES).astype(BF16)
    out_ref[:, 32:40, :] = in_ref[:, 32:40, :]


def finish_kernel(frame_ref, recv_ref, raw_ref, table_ref, act_ref, proj_ref, pre_ref, grad_ref, rows_ref):
    heads = raw_ref.shape[1]
    for pair in range(PAIRS):
        columns = slice(LANES * pair, LANES * pair + LANES)
        for part in range(PARTS):
            act_ref[16 * part : 16 * part + 16, columns] = recv_ref[place(part, pair), 0:16, :]
    for part in range(PARTS):
        for core in range(2):
            total = recv_ref[place(part, core), 16:32, :].astype(F32)
            for high in range(1, 4):
                total = total + recv_ref[place(part, 2 * high + core), 16:32, :].astype(F32)
            proj_ref[16 * part : 16 * part + 16, LANES * core : LANES * core + LANES] = total.astype(BF16)
    lane = lane_iota(8)
    sub = lax.broadcasted_iota(jnp.int32, (8, LANES), 0)
    rows_ref[...] = jnp.zeros((LANES, LANES), F32)
    per_frame = jnp.zeros((8, LANES), F32)
    for pair in range(PAIRS):
        rows = recv_ref[place(0, pair), 32:40, :].astype(F32)
        for part in range(1, PARTS):
            rows = rows + recv_ref[place(part, pair), 32:40, :].astype(F32)
        rows_ref[2 * pair : 2 * pair + 2, :] = rows[0:2]
        rows = rows + pltpu.roll(rows, 64, 1)
        for head in range(2):
            inside = (lane < 2 * BLOCKS) & (lane % 2 == head)
            total = jnp.sum(jnp.where(inside, rows, 0.0), axis=1, keepdims=True)
            per_frame = jnp.where(lane == 2 * pair + head, total, per_frame)
    pre = shifted_steps(frame_ref, raw_ref, table_ref)
    pre_ref[...] = rows_ref[...].T[:, :heads] * sigmoid(pre)
    steps = lax.broadcasted_iota(jnp.int32, grad_ref.shape, 0)
    grad = jnp.zeros(grad_ref.shape, F32)
    for frame in range(4):
        grad = grad + jnp.where(steps == frame_ref[frame], per_frame[2 + frame : 3 + frame, :heads], 0.0)
    grad_ref[...] = grad


def total_kernel(own_ref, one_ref, two_ref, three_ref, write_ref, read_ref):
    even = own_ref[...].astype(F32) + two_ref[...].astype(F32)
    odd = one_ref[...].astype(F32) + three_ref[...].astype(F32)
    total = (even + odd).astype(BF16)
    write_ref[...] = total[:, :LANES]
    read_ref[...] = total[:, LANES:]


VMEM = pl.BlockSpec(memory_space=pltpu.VMEM)
SMEM = pl.BlockSpec(memory_space=pltpu.SMEM)


def call(kernel, name, in_specs, out_shape, scratch=(), cost=None):
    shapes = [jax.ShapeDtypeStruct(shape, dtype) for shape, dtype in out_shape]
    return pl.pallas_call(
        kernel,
        out_shape=shapes,
        in_specs=in_specs,
        out_specs=[VMEM] * len(shapes),
        scratch_shapes=list(scratch),
        compiler_params=PARAMS,
        cost_estimate=cost,
        name=name,
    )


def shards(
    activations, grad_out, write_proj, read_proj, step_raw, step_table, decay_rate, frame_step, scan_order
):
    heads = step_raw.shape[1]
    swap_core = [(i, i ^ 1) for i in range(SEQ)]
    (send,) = call(
        pack_kernel, "pack", [SMEM] + [VMEM] * 7, [((SEQ, SLOT_IN, LANES), BF16)]
    )(
        frame_step, scan_order.reshape(1, TOK), activations, grad_out, write_proj, read_proj,
        step_raw, step_table,
    )
    recv = lax.all_to_all(send, "seq", 0, 0, tiled=True)
    swap = lax.ppermute(recv, "seq", swap_core)
    tokens = ((LOCAL, LANES), BF16)
    sums = ((LOCAL, LANES), F32)
    blocks = ((BLOCKS, LANES, LANES), F32)
    x, dy, write, read, states, s_part, r_part, stat = call(
        unpack_kernel, "unpack", [SMEM, VMEM, VMEM],
        [tokens] * 4 + [((PARTS, SLOT_STATE, LANES), BF16), blocks, blocks, ((5, LANES, LANES), F32)],
        [pltpu.VMEM((LOCAL, LANES), F32), pltpu.VMEM((SEQ * 8, LANES), F32)],
    )(decay_rate, recv, swap)
    states = lax.all_to_all(states, "seq", 0, 0, tiled=True, axis_index_groups=STATE_GROUPS)
    u, gw, gr, t = call(
        inner_kernel, "inner", [VMEM] * 5, [sums] * 3 + [((LANES, LANES), F32)],
        cost=pl.CostEstimate(flops=10**9, bytes_accessed=4 * 2**20, transcendentals=2**18),
    )(x, dy, write, read, stat)
    out, keep, give = call(
        outer_kernel, "outer", [SMEM] + [VMEM] * 12,
        [((SEQ, SLOT_OUT, LANES), BF16), sums, sums],
        [pltpu.VMEM((BLOCKS, LANES, LANES), F32)] + [pltpu.VMEM((LOCAL, LANES), F32)] * 3,
    )(decay_rate, states, x, dy, write, read, s_part, r_part, stat, u, gw, gr, t)
    got = lax.ppermute(give, "seq", swap_core)
    (out,) = call(join_kernel, "join", [VMEM] * 3, [((SEQ, SLOT_OUT, LANES), BF16)])(out, keep, got)
    back = lax.all_to_all(out, "seq", 0, 0, tiled=True)
    act, proj, grad_pre, grad_table = call(
        finish_kernel, "finish", [SMEM] + [VMEM] * 3,
        [
            (activations.shape, BF16),
            ((TOK, 2 * LANES), BF16),
            (step_raw.shape, F32),
            (step_table.shape, F32),
        ],
        [pltpu.VMEM((LANES, LANES), F32)],
    )(frame_step, back, step_raw, step_table)
    ring = [lax.ppermute(proj, "head", [(i, (i + k) % 4) for i in range(4)]) for k in (1, 2, 3)]
    grad_write, grad_read = call(
        total_kernel, "total", [VMEM] * 4, [(write_proj.shape, BF16), (read_proj.shape, BF16)]
    )(proj, *ring)
    return (act, grad_write, grad_read, grad_pre, grad_table)


def solution(mesh):
    in_specs = (
        P("seq", "head"),
        P("seq", "head"),
        P("seq", None),
        P("seq", None),
        P("seq", "head"),
        P(None, "head"),
        P("head"),
        P(),
        P("seq"),
    )
    out_specs = (
        P("seq", "head"),
        P("seq", None),
        P("seq", None),
        P("seq", "head"),
        P(None, "head"),
    )
    return jax.shard_map(shards, mesh=mesh, in_specs=in_specs, out_specs=out_specs, check_vma=False)
```

```python
import jax
import jax.numpy as jnp
from jax import lax
from jax.experimental import pallas as pl
from jax.experimental.pallas import tpu as pltpu
from jax.sharding import PartitionSpec as P

F32 = jnp.float32
BF16 = jnp.bfloat16
FRAME_TOK = 2048
TOK = 128
LANES = 128
SEQ = 64
PARTS = 8
PAIRS = 8
BLOCKS = 8
SLOT_IN = 56
SLOT_STATE = 136
SLOT_OUT = 40
LOCAL = BLOCKS * TOK
PARAMS = pltpu.CompilerParams(vmem_limit_bytes=32 * 1024 * 1024)


def place(part, pair):
    y, low = part // 2, part % 2
    high, core = pair // 2, pair % 2
    return y * 16 + (high * 2 + low) * 2 + core


def my_place():
    me = lax.axis_index("seq")
    part = (me // 16) * 2 + (me // 2) % 2
    pair = ((me // 4) % 4) * 2 + me % 2
    return part, pair, me % 2


STATE_GROUPS = [[place(part, pair) for part in range(PARTS)] for pair in range(PAIRS)]


def nn(a, b):
    return lax.dot_general(a, b, (((1,), (0,)), ((), ())), preferred_element_type=F32)


def nt(a, b):
    return lax.dot_general(a, b, (((1,), (1,)), ((), ())), preferred_element_type=F32)


def split(value):
    high = value.astype(BF16)
    return high, (value - high.astype(F32)).astype(BF16)


def lane_iota(rows):
    return lax.broadcasted_iota(jnp.int32, (rows, LANES), 1)


def heads_over_lanes(first, second, rows):
    return jnp.where(lane_iota(rows) < 64, first, second)


def softplus(value):
    return jnp.maximum(value, 0.0) + jnp.log1p(jnp.exp(-jnp.abs(value)))


def sigmoid(value):
    return 1.0 / (1.0 + jnp.exp(-value))


def shifted_steps(frame_ref, raw, table):
    frame_here = lax.axis_index("seq") * TOK // FRAME_TOK
    index = frame_ref[frame_here]
    columns = lax.broadcasted_iota(jnp.int32, table.shape, 1)
    shift = jnp.sum(jnp.where(columns == index, table, 0.0), axis=1, keepdims=True)
    return raw + shift


def pack_kernel(frame_ref, order_ref, *refs):
    sources, out_ref, targets, sems = refs[:6], refs[6], refs[7:13], refs[13]
    copies = [
        pltpu.make_async_copy(source, target, sems.at[i])
        for i, (source, target) in enumerate(zip(sources, targets))
    ]
    for copy in copies:
        copy.start()
    raw_ref, table_ref, b_ref, c_ref, x_ref, dy_ref = targets
    order = jnp.broadcast_to(order_ref[...].astype(F32), (TOK, TOK)).T
    lane = lane_iota(TOK)
    token = ((lane % 64) * 2 + lane // 64).astype(F32)
    steps = lax.broadcasted_iota(jnp.int32, (TOK, TOK), 0).astype(F32)
    position = jnp.sum(jnp.where(order == token, steps, 0.0), axis=0, keepdims=True)
    copies[0].wait()
    copies[1].wait()
    pre = shifted_steps(frame_ref, raw_ref[...], table_ref[...])
    delta = softplus(pre).astype(BF16).astype(F32)
    gate = sigmoid(pre)
    gate_high = gate.astype(BF16).astype(F32)
    gate_low = gate - gate_high
    for copy in copies[2:]:
        copy.wait()
    for pair in range(PAIRS):
        own = slice(2 * pair, 2 * pair + 2)
        rows = jnp.concatenate(
            [position, delta[own], gate_high[own], gate_low[own], jnp.zeros((1, LANES), F32)], axis=0
        ).astype(BF16)
        proj_ref = c_ref if pair % 2 else b_ref
        columns = slice(LANES * pair, LANES * pair + LANES)
        for part in range(PARTS):
            slot = place(part, pair)
            tokens = slice(16 * part, 16 * part + 16)
            out_ref[slot, 0:16, :] = x_ref[tokens, columns]
            out_ref[slot, 16:32, :] = dy_ref[tokens, columns]
            out_ref[slot, 32:48, :] = proj_ref[tokens, :]
            out_ref[slot, 48:56, :] = rows


def to_columns(first, second):
    head_one = jnp.concatenate([first, pltpu.roll(first, LANES - 1, 1)], axis=0)
    head_two = jnp.concatenate([pltpu.roll(second, 1, 1), second], axis=0)
    return jnp.where(lane_iota(TOK) % 2 == 0, head_one, head_two)


def slope_lanes(decay_ref, pair, rows):
    return jnp.where(lane_iota(rows) % 2 == 0, -decay_ref[2 * pair], -decay_ref[2 * pair + 1])


def block_lanes(columns, block, rows):
    j = 2 * block
    return heads_over_lanes(columns[:, j : j + 1], columns[:, j + 1 : j + 2], rows)


def block_rows(block):
    return slice(block * TOK, block * TOK + TOK)


def stack(value):
    return jnp.concatenate(split(value), axis=0)


def twice(value):
    return jnp.concatenate([value, value], axis=1)


def turned(value):
    return value.astype(F32).T.astype(BF16)


def twice_split(value):
    return jnp.concatenate(split(value), axis=1)


def spread(value, wide, target_ref, base):
    wide[...] = value.reshape(SEQ * 16, LANES)
    for row in range(16):
        start = base + row * 64
        target_ref[start : start + 64, :] = wide[pl.ds(row, 64, stride=16), :].astype(BF16)


def unpack_kernel(
    decay_ref, recv_ref, data_ref, proj_ref, weight_ref, wide, wide_two, wide_three, misc
):
    part, pair, core = my_place()
    spread(recv_ref[:, 0:16, :].astype(F32), wide, data_ref, 0)
    spread(recv_ref[:, 16:32, :].astype(F32), wide_two, data_ref, LOCAL)
    spread(recv_ref[:, 32:48, :].astype(F32), wide_three, proj_ref, 0)
    misc[...] = recv_ref[:, 48:56, :].astype(F32).reshape(SEQ * 8, LANES)
    shift = (LANES - 16 * part) % LANES

    def own_lanes(row):
        return pltpu.roll(misc[pl.ds(row, 64, stride=8), :], shift, 1)

    steps = to_columns(own_lanes(1), own_lanes(2))
    gates_high = to_columns(own_lanes(3), own_lanes(4))
    gates_low = to_columns(own_lanes(5), own_lanes(6))
    pos_rows = jnp.concatenate(
        [misc[pl.ds(part * 64 + 8 * block, 1), :] for block in range(BLOCKS)], axis=0
    )
    pos_cols = jnp.concatenate([pos_rows, jnp.zeros((LANES - BLOCKS, LANES), F32)], axis=0).T
    lane = lane_iota(TOK)
    steps_bf = steps.astype(BF16)
    sums = jnp.zeros((TOK, LANES), F32)
    for block in range(BLOCKS):
        later = (pos_cols[:, block : block + 1] >= pos_rows[block : block + 1, :]).astype(F32).astype(BF16)
        sums = jnp.where(lane // 2 == block, nn(later, steps_bf), sums)
    slopes = slope_lanes(decay_ref, pair, TOK)
    logs = sums * slopes
    totals = jnp.sum(steps, axis=0, keepdims=True) * slopes[:1]
    short = jnp.where(lane_iota(1) < 2 * BLOCKS, totals, 0.0)
    onward = short
    until = pltpu.roll(short, 2, 1)
    for reach in (2, 4, 8):
        onward = onward + pltpu.roll(onward, LANES - reach, 1)
        until = until + pltpu.roll(until, reach, 1)
    base = 2 * LOCAL
    data_ref[base : base + TOK, :] = steps_bf
    data_ref[base + TOK : base + 2 * TOK, :] = gates_high.astype(BF16)
    data_ref[base + 2 * TOK : base + 3 * TOK, :] = gates_low.astype(BF16)
    data_ref[base + 3 * TOK : base + 4 * TOK, :] = pos_cols.astype(BF16)
    whole = heads_over_lanes(onward[:, 0:1], onward[:, 1:2], 1)
    top = whole.astype(BF16).astype(F32)
    middle = (whole - top).astype(BF16).astype(F32)
    bottom = whole - top - middle
    tail = jnp.concatenate([top, middle, bottom, jnp.zeros((13, LANES), F32)], axis=0).astype(BF16)
    weight_ref[4 * LOCAL : 4 * LOCAL + 16, :] = tail
    weights = steps * jnp.exp(jnp.minimum(onward - logs, 0.0))
    starts = jnp.exp(jnp.minimum(logs + until, 0.0))
    for block in range(BLOCKS):
        rows = block_rows(block)
        later_rows = slice(LOCAL + block * TOK, LOCAL + block * TOK + TOK)
        first = block * 2 * TOK
        weight_ref[first : first + 2 * TOK, :] = stack(
            data_ref[rows, :].astype(F32) * block_lanes(weights, block, TOK)
        )
        first = 2 * LOCAL + block * 2 * TOK
        weight_ref[first : first + 2 * TOK, :] = stack(
            data_ref[later_rows, :].astype(F32) * block_lanes(starts, block, TOK)
        )


def states_kernel(mine_ref, swap_ref, weight_ref, data_ref, all_ref, send_ref, wide):
    part, pair, core = my_place()
    all_ref[0 : 2 * LOCAL, :] = data_ref[0 : 2 * LOCAL, :]
    all_ref[4 * LOCAL : 4 * LOCAL + 4 * TOK, :] = data_ref[2 * LOCAL : 2 * LOCAL + 4 * TOK, :]
    spread(swap_ref[:, 32:48, :].astype(F32), wide, all_ref, 3 * LOCAL)

    @pl.when(core == 0)
    def _():
        all_ref[2 * LOCAL : 3 * LOCAL, :] = mine_ref[...]

    @pl.when(core == 1)
    def _():
        all_ref[2 * LOCAL : 3 * LOCAL, :] = all_ref[3 * LOCAL : 4 * LOCAL, :]
        all_ref[3 * LOCAL : 4 * LOCAL, :] = mine_ref[...]

    state = jnp.zeros((LANES, LANES), F32)
    adjoint = jnp.zeros((LANES, LANES), F32)
    for block in range(BLOCKS):
        write = all_ref[2 * LOCAL + block * TOK : 2 * LOCAL + block * TOK + TOK, :]
        read = all_ref[3 * LOCAL + block * TOK : 3 * LOCAL + block * TOK + TOK, :]
        first = block * 2 * TOK
        state = state + nn(twice(turned(write)), weight_ref[first : first + 2 * TOK, :])
        first = 2 * LOCAL + block * 2 * TOK
        adjoint = adjoint + nn(twice(turned(read)), weight_ref[first : first + 2 * TOK, :])
    state = state.astype(BF16)
    adjoint = adjoint.astype(BF16)
    for slot in range(PARTS):
        after = slot > part

        @pl.when(after)
        def _():
            send_ref[slot, 0:128, :] = state

        @pl.when(jnp.logical_not(after))
        def _():
            send_ref[slot, 0:128, :] = adjoint

        send_ref[slot, 128:136, :] = weight_ref[4 * LOCAL : 4 * LOCAL + 16, :][:8]


def inner_kernel(decay_ref, all_ref, sums_ref, grad_ref, data_ref):
    part, pair, core = my_place()
    base = 4 * LOCAL
    steps_bf = all_ref[base : base + TOK, :]
    steps = steps_bf.astype(F32)
    pos_cols = all_ref[base + 3 * TOK : base + 4 * TOK, :].astype(F32)
    pos_rows = pos_cols.T[:8]
    grad_ref[2 * LOCAL : 2 * LOCAL + TOK, :] = steps
    grad_ref[2 * LOCAL + TOK : 2 * LOCAL + 2 * TOK, :] = (
        all_ref[base + TOK : base + 2 * TOK, :].astype(F32) + all_ref[base + 2 * TOK : base + 3 * TOK, :].astype(F32)
    )
    grad_ref[2 * LOCAL + 2 * TOK : 2 * LOCAL + 3 * TOK, :] = jnp.zeros((TOK, LANES), F32)
    lane = lane_iota(TOK)
    sums = jnp.zeros((TOK, LANES), F32)
    masks = 3 * LOCAL
    for block in range(BLOCKS):
        pos_col = pos_cols[:, block : block + 1]
        pos_row = pos_rows[block : block + 1, :]
        behind = (pos_col >= pos_row).astype(F32).astype(BF16)
        first = masks + block * 2 * TOK
        data_ref[first : first + TOK, :] = (pos_row >= pos_col).astype(F32).astype(BF16)
        data_ref[first + TOK : first + 2 * TOK, :] = behind
        sums = jnp.where(lane // 2 == block, nn(behind, steps_bf), sums)
    slopes = slope_lanes(decay_ref, pair, TOK)
    logs = sums * slopes
    log_rows = logs.T
    totals = jnp.sum(steps, axis=0, keepdims=True) * slopes[:1]
    starts = jnp.exp(logs)
    ends = steps * jnp.exp(totals - logs)
    data_ref[0:LOCAL, :] = all_ref[0:LOCAL, :]
    data_ref[LOCAL : 3 * LOCAL, :] = all_ref[2 * LOCAL : 4 * LOCAL, :]
    for block in range(BLOCKS):
        rows = block_rows(block)

        def piece(number):
            return all_ref[number * LOCAL + block * TOK : number * LOCAL + block * TOK + TOK, :]

        def sums_rows(number):
            return slice(number * LOCAL + block * TOK, number * LOCAL + block * TOK + TOK)

        x, dy, write, read = piece(0), piece(1), piece(2), piece(3)
        sums_ref[6 * LOCAL + block : 6 * LOCAL + block + 1, :] = block_lanes(totals, block, 1)
        end = block_lanes(ends, block, TOK)
        grad_ref[LOCAL + block * TOK : LOCAL + block * TOK + TOK, :] = end
        xe = x.astype(F32) * end
        ds = dy.astype(F32) * block_lanes(starts, block, TOK)
        first = block * 2 * TOK
        sums_ref[sums_rows(4), :] = ds
        sums_ref[sums_rows(5), :] = xe
        sums_ref[sums_rows(2), :] = nn(twice(turned(write)), stack(xe))
        sums_ref[sums_rows(3), :] = nn(twice(turned(read)), stack(ds))
        ahead = pos_rows[block : block + 1, :] >= pos_cols[:, block : block + 1]
        behind = data_ref[masks + first + TOK : masks + first + 2 * TOK, :]
        cross = nt(write, read)
        zero = jnp.zeros_like(dy)
        x_heads = (jnp.where(lane < 64, x, zero), jnp.where(lane < 64, zero, x))
        dy_stack = jnp.concatenate(
            [jnp.where(lane < 64, dy, zero), jnp.where(lane < 64, zero, dy)], axis=0
        )
        carry, mixed, seen = [], [], []
        for head in range(2):
            j = 2 * block + head
            gap = log_rows[j : j + 1, :] - logs[:, j : j + 1]
            decay = jnp.exp(jnp.where(ahead, gap, -1e30))
            carry.append(decay * cross)
            mixed.append(decay * (nt(x_heads[head], dy) * steps[:, j : j + 1]))
            seen.append(twice_split(mixed[head] * cross))
        crossed = nn(jnp.concatenate(seen, axis=0), jnp.concatenate([behind, behind], axis=0))
        for head in range(2):
            j = 2 * LOCAL + 2 * TOK + 2 * block + head
            own = jnp.where(ahead, crossed[head * TOK : head * TOK + TOK], 0.0)
            grad_ref[j : j + 1, :] = jnp.sum(own, axis=0, keepdims=True)
        high, low = split(jnp.concatenate(carry, axis=1))
        grad_ref[rows, :] = block_lanes(steps, block, TOK) * (nn(high, dy_stack) + nn(low, dy_stack))
        both = mixed[0] + mixed[1]
        sums_ref[sums_rows(0), :] = nn(twice_split(both), jnp.concatenate([read, read], axis=0))
        sums_ref[sums_rows(1), :] = nn(twice_split(both.T), jnp.concatenate([write, write], axis=0))


def outer_kernel(recv_ref, sums_ref, keep_ref, give_ref, all_ref, adj, wide_w, wide_r):
    part, pair, core = my_place()

    def arrive(slot, state):
        tail = recv_ref[slot, 128:136, :].astype(F32)
        total = tail[0:1] + tail[1:2] + tail[2:3]
        return state * jnp.exp(total) + recv_ref[slot, 0:128, :].astype(F32)

    zero = jnp.zeros((LANES, LANES), F32)
    state = lax.fori_loop(0, part, arrive, zero)
    adjoint = lax.fori_loop(0, PARTS - 1 - part, lambda k, a: arrive(PARTS - 1 - k, a), zero)
    keeps = jnp.exp(sums_ref[6 * LOCAL : 6 * LOCAL + 8, :])

    def sums_rows(number, block):
        return slice(number * LOCAL + block * TOK, number * LOCAL + block * TOK + TOK)

    for block in reversed(range(BLOCKS)):
        adj[block] = adjoint
        adjoint = adjoint * keeps[block : block + 1] + sums_ref[sums_rows(3, block), :]
    overlaps = []
    for block in range(BLOCKS):
        adjoint = adj[block]
        state_high, state_low = split(state)
        adj_high, adj_low = split(adjoint)
        first = block * 2 * TOK
        all_ref[4 * LOCAL + first : 4 * LOCAL + first + TOK, :] = state_high
        all_ref[4 * LOCAL + first + TOK : 4 * LOCAL + first + 2 * TOK, :] = state_low
        all_ref[6 * LOCAL + first : 6 * LOCAL + first + TOK, :] = adj_high
        all_ref[6 * LOCAL + first + TOK : 6 * LOCAL + first + 2 * TOK, :] = adj_low
        keep = keeps[block : block + 1]
        overlaps.append(jnp.sum(adjoint * state, axis=0, keepdims=True) * keep)
        ds_high, ds_low = split(sums_ref[sums_rows(4, block), :])
        xe_high, xe_low = split(sums_ref[sums_rows(5, block), :])
        all_ref[first : first + TOK, :] = ds_high
        all_ref[first + TOK : first + 2 * TOK, :] = ds_low
        all_ref[2 * LOCAL + first : 2 * LOCAL + first + TOK, :] = xe_high
        all_ref[2 * LOCAL + first + TOK : 2 * LOCAL + first + 2 * TOK, :] = xe_low
        gr = sums_ref[sums_rows(1, block), :] + (
            nt(jnp.concatenate([ds_high, ds_low], axis=1), twice(state_high)) + nt(ds_high, state_low)
        )
        gw = sums_ref[sums_rows(0, block), :] + (
            nt(jnp.concatenate([xe_high, xe_low], axis=1), twice(adj_high)) + nt(xe_high, adj_low)
        )
        for half in range(2):
            out_rows = pl.ds(2 * block + half, 64, stride=16)
            wide_w[out_rows, :] = gw[64 * half : 64 * half + 64]
            wide_r[out_rows, :] = gr[64 * half : 64 * half + 64]
        state = state * keep + sums_ref[sums_rows(2, block), :]
    overlaps = jnp.concatenate(overlaps, axis=0)
    top = overlaps.astype(BF16).astype(F32)
    middle = (overlaps - top).astype(BF16).astype(F32)
    bottom = overlaps - top - middle
    all_ref[8 * LOCAL : 8 * LOCAL + 32, :] = jnp.concatenate(
        [top, middle, bottom, jnp.zeros((8, LANES), F32)], axis=0
    ).astype(BF16)

    @pl.when(core == 0)
    def _():
        keep_ref[...] = wide_w[...]
        give_ref[...] = wide_r[...]

    @pl.when(core == 1)
    def _():
        keep_ref[...] = wide_r[...]
        give_ref[...] = wide_w[...]


def grads_kernel(decay_ref, data_ref, all_ref, grad_ref, out_ref, wide):
    part, pair, core = my_place()
    slopes = slope_lanes(decay_ref, pair, TOK)
    base = 2 * LOCAL
    steps = grad_ref[base : base + TOK, :]
    gates = grad_ref[base + TOK : base + 2 * TOK, :]
    lane = lane_iota(TOK)
    tail = all_ref[8 * LOCAL : 8 * LOCAL + 32, :].astype(F32)
    overlaps = tail[0:8] + tail[8:16] + tail[16:24]
    row_lane = lane_iota(8)
    row = lax.broadcasted_iota(jnp.int32, (8, LANES), 0)
    first = jnp.sum(jnp.where(row_lane < 64, overlaps, 0.0), axis=1, keepdims=True)
    second = jnp.sum(jnp.where(row_lane < 64, 0.0, overlaps), axis=1, keepdims=True)
    kept = jnp.where(row_lane == 2 * row, first, jnp.where(row_lane == 2 * row + 1, second, 0.0))
    log_grad = grad_ref[base + 2 * TOK : base + 3 * TOK, :].T + jnp.sum(kept, axis=0, keepdims=True)
    sub = lax.broadcasted_iota(jnp.int32, (2 * LANES, LANES), 0) % LANES // 64
    pick_lane = lax.broadcasted_iota(jnp.int32, (2 * LANES, LANES), 1)
    direct = jnp.zeros((TOK, LANES), F32)
    for block in range(BLOCKS):
        rows = block_rows(block)
        lo = block * 2 * TOK

        def both(number):
            start = number * LOCAL + lo
            return all_ref[start : start + TOK, :].astype(F32) + all_ref[start + TOK : start + 2 * TOK, :].astype(F32)

        x = data_ref[rows, :].astype(F32)
        write = data_ref[LOCAL + block * TOK : LOCAL + block * TOK + TOK, :]
        read = data_ref[2 * LOCAL + block * TOK : 2 * LOCAL + block * TOK + TOK, :]
        carried = nn(twice(write), all_ref[6 * LOCAL + lo : 6 * LOCAL + lo + 2 * TOK, :])
        recalled = nn(twice(read), all_ref[4 * LOCAL + lo : 4 * LOCAL + lo + 2 * TOK, :])
        act = grad_ref[rows, :] + grad_ref[LOCAL + block * TOK : LOCAL + block * TOK + TOK, :] * carried
        wide[pl.ds(2 * block, 64, stride=16), :] = act[:64]
        wide[pl.ds(2 * block + 1, 64, stride=16), :] = act[64:]
        products = jnp.concatenate([both(0) * recalled, both(2) * carried, x * act], axis=0)
        pick = (pick_lane == 2 * block + sub).astype(F32).astype(BF16)
        sums = nn(twice_split(products), pick)
        direct = direct + sums[2 * TOK :]
        ahead = data_ref[3 * LOCAL + lo : 3 * LOCAL + lo + TOK, :]
        behind = data_ref[3 * LOCAL + lo + TOK : 3 * LOCAL + lo + 2 * TOK, :]
        added = nn(twice(ahead), stack(sums[:TOK])) + nn(twice(behind), stack(sums[TOK : 2 * TOK]))
        log_grad = log_grad + jnp.where(lane // 2 == block, added, 0.0)

    grad_step = direct / steps + slopes * (log_grad - direct)
    grad_step = jnp.where(lane < 2 * BLOCKS, grad_step, 0.0).astype(BF16).astype(F32)
    grad_pre = grad_step * gates
    frames = []
    for frame in range(4):
        low_rows = slice(16 * frame, 16 * frame + 16)
        high_rows = slice(64 + 16 * frame, 80 + 16 * frame)
        frames.append(jnp.sum(grad_pre[low_rows] + grad_pre[high_rows], axis=0, keepdims=True))
    frames = jnp.concatenate(frames + [jnp.zeros((4, LANES), F32)], axis=0)
    frames_high = frames.astype(BF16).astype(F32)
    frames = frames_high + pltpu.roll(frames - frames_high, 64, 1)

    even = lane_iota(64) % 2 == 0
    top, bottom = grad_step[:64], grad_step[64:]
    shift = 16 * part
    row_one = pltpu.roll(jnp.where(even, top, pltpu.roll(bottom, 1, 1)), shift, 1)
    row_two = pltpu.roll(jnp.where(even, pltpu.roll(top, LANES - 1, 1), bottom), shift, 1)
    misc = jnp.concatenate(
        [
            row_one[:, None, :],
            row_two[:, None, :],
            jnp.broadcast_to(frames[None, :4, :], (SEQ, 4, LANES)),
            jnp.zeros((SEQ, 2, LANES), F32),
        ],
        axis=1,
    )
    out_ref[:, 0:16, :] = wide[...].reshape(SEQ, 16, LANES).astype(BF16)
    out_ref[:, 16:32, :] = jnp.zeros((SEQ, 16, LANES), BF16)
    out_ref[:, 32:40, :] = misc.astype(BF16)


def join_kernel(in_ref, keep_ref, got_ref, out_ref):
    out_ref[:, 0:16, :] = in_ref[:, 0:16, :]
    out_ref[:, 16:32, :] = (keep_ref[...] + got_ref[...]).reshape(SEQ, 16, LANES).astype(BF16)
    out_ref[:, 32:40, :] = in_ref[:, 32:40, :]


def proj_kernel(recv_ref, proj_ref, rest_ref):
    for part in range(PARTS):
        for core in range(2):
            total = recv_ref[place(part, core), 16:32, :].astype(F32)
            for high in range(1, 4):
                total = total + recv_ref[place(part, 2 * high + core), 16:32, :].astype(F32)
            proj_ref[16 * part : 16 * part + 16, LANES * core : LANES * core + LANES] = total.astype(BF16)
    rest_ref[:, 0:16, :] = recv_ref[:, 0:16, :]
    rest_ref[:, 16:24, :] = recv_ref[:, 32:40, :]


def finish_kernel(frame_ref, recv_ref, raw_ref, table_ref, act_ref, pre_ref, grad_ref, rows_ref):
    heads = raw_ref.shape[0]
    for pair in range(PAIRS):
        columns = slice(LANES * pair, LANES * pair + LANES)
        for part in range(PARTS):
            act_ref[16 * part : 16 * part + 16, columns] = recv_ref[place(part, pair), 0:16, :]
    lane = lane_iota(8)
    per_frame = jnp.zeros((8, LANES), F32)
    for pair in range(PAIRS):
        rows = recv_ref[place(0, pair), 16:24, :].astype(F32)
        for part in range(1, PARTS):
            rows = rows + recv_ref[place(part, pair), 16:24, :].astype(F32)
        rows_ref[2 * pair : 2 * pair + 2, :] = rows[0:2]
        rows = rows + pltpu.roll(rows, 64, 1)
        for head in range(2):
            inside = (lane < 2 * BLOCKS) & (lane % 2 == head)
            total = jnp.sum(jnp.where(inside, rows, 0.0), axis=1, keepdims=True)
            per_frame = jnp.where(lane == 2 * pair + head, total, per_frame)
    pre = shifted_steps(frame_ref, raw_ref[...], table_ref[...])
    pre_ref[...] = rows_ref[...] * sigmoid(pre)
    per_head = jnp.concatenate([per_frame, jnp.zeros((LANES - 8, LANES), F32)], axis=0).T
    steps = lax.broadcasted_iota(jnp.int32, grad_ref.shape, 1)
    grad = jnp.zeros(grad_ref.shape, F32)
    for frame in range(4):
        grad = grad + jnp.where(steps == frame_ref[frame], per_head[:heads, 2 + frame : 3 + frame], 0.0)
    grad_ref[...] = grad


def total_kernel(own_ref, one_ref, two_ref, three_ref, write_ref, read_ref):
    even = own_ref[...].astype(F32) + two_ref[...].astype(F32)
    odd = one_ref[...].astype(F32) + three_ref[...].astype(F32)
    total = (even + odd).astype(BF16)
    write_ref[...] = total[:, :LANES]
    read_ref[...] = total[:, LANES:]


VMEM = pl.BlockSpec(memory_space=pltpu.VMEM)
SMEM = pl.BlockSpec(memory_space=pltpu.SMEM)


def call(kernel, name, in_specs, out_shape, scratch=(), params=PARAMS):
    shapes = [jax.ShapeDtypeStruct(shape, dtype) for shape, dtype in out_shape]
    return pl.pallas_call(
        kernel,
        out_shape=shapes,
        in_specs=in_specs,
        out_specs=[VMEM] * len(shapes),
        scratch_shapes=list(scratch),
        compiler_params=params,
        name=name,
    )


def shards(
    activations, grad_out, write_proj, read_proj, step_raw, step_table, decay_rate, frame_step, scan_order
):
    raw, table = step_raw.T, step_table.T
    swap_core = [(i, i ^ 1) for i in range(SEQ)]
    hbm = pl.BlockSpec(memory_space=pltpu.HBM)
    sources = (raw, table, write_proj, read_proj, activations, grad_out)
    (send,) = call(
        pack_kernel, "pack", [SMEM, VMEM] + [hbm] * 6, [((SEQ, SLOT_IN, LANES), BF16)],
        [pltpu.VMEM(a.shape, a.dtype) for a in sources] + [pltpu.SemaphoreType.DMA((6,))],
        pltpu.CompilerParams(vmem_limit_bytes=62 * 1024 * 1024),
    )(frame_step, scan_order.reshape(1, TOK), *sources)
    recv = lax.all_to_all(send, "seq", 0, 0, tiled=True)
    swap = lax.ppermute(recv, "seq", swap_core)
    wide = pltpu.VMEM((LOCAL, LANES), F32)
    data, mine, weight = call(
        unpack_kernel, "unpack", [SMEM, VMEM],
        [((2 * LOCAL + 4 * TOK, LANES), BF16), ((LOCAL, LANES), BF16), ((4 * LOCAL + 16, LANES), BF16)],
        [wide] * 3 + [pltpu.VMEM((SEQ * 8, LANES), F32)],
    )(decay_rate, recv)
    data, states = call(
        states_kernel, "states", [VMEM] * 4,
        [((4 * LOCAL + 4 * TOK, LANES), BF16), ((PARTS, SLOT_STATE, LANES), BF16)], [wide],
    )(mine, swap, weight, data)
    states = lax.all_to_all(states, "seq", 0, 0, tiled=True, axis_index_groups=STATE_GROUPS)
    sums, grad, data = call(
        inner_kernel, "inner", [SMEM, VMEM],
        [
            ((6 * LOCAL + 8, LANES), F32),
            ((2 * LOCAL + 3 * TOK, LANES), F32),
            ((5 * LOCAL, LANES), BF16),
        ],
    )(decay_rate, data)
    keep, give, pairs = call(
        outer_kernel, "outer", [VMEM] * 2,
        [((LOCAL, LANES), F32)] * 2 + [((8 * LOCAL + 32, LANES), BF16)],
        [pltpu.VMEM((BLOCKS, LANES, LANES), F32)] + [wide] * 2,
    )(states, sums)
    got = lax.ppermute(give, "seq", swap_core)
    (out,) = call(
        grads_kernel, "grads", [SMEM] + [VMEM] * 3, [((SEQ, SLOT_OUT, LANES), BF16)], [wide]
    )(decay_rate, data, pairs, grad)
    (out,) = call(join_kernel, "join", [VMEM] * 3, [((SEQ, SLOT_OUT, LANES), BF16)])(out, keep, got)
    back = lax.all_to_all(out, "seq", 0, 0, tiled=True)
    proj, rest = call(
        proj_kernel, "proj", [VMEM], [((TOK, 2 * LANES), BF16), ((SEQ, 24, LANES), BF16)]
    )(back)
    ring = [lax.ppermute(proj, "head", [(i, (i + k) % 4) for i in range(4)]) for k in (1, 2, 3)]
    act, grad_pre, grad_table = call(
        finish_kernel, "finish", [SMEM] + [VMEM] * 3,
        [(activations.shape, BF16), (raw.shape, F32), (table.shape, F32)],
        [pltpu.VMEM((2 * PAIRS, LANES), F32)],
    )(frame_step, rest, raw, table)
    grad_write, grad_read = call(
        total_kernel, "total", [VMEM] * 4, [(write_proj.shape, BF16), (read_proj.shape, BF16)]
    )(proj, *ring)
    return (act, grad_write, grad_read, grad_pre.T, grad_table.T)


def solution(mesh):
    in_specs = (
        P("seq", "head"),
        P("seq", "head"),
        P("seq", None),
        P("seq", None),
        P("seq", "head"),
        P(None, "head"),
        P("head"),
        P(),
        P("seq"),
    )
    out_specs = (
        P("seq", "head"),
        P("seq", None),
        P("seq", None),
        P("seq", "head"),
        P(None, "head"),
    )
    return jax.shard_map(shards, mesh=mesh, in_specs=in_specs, out_specs=out_specs, check_vma=False)
```

```python
import jax
import jax.numpy as jnp
from jax import lax
from jax.experimental import pallas as pl
from jax.experimental.pallas import tpu as pltpu
from jax.sharding import PartitionSpec as P

F32 = jnp.float32
BF16 = jnp.bfloat16
FRAME_TOK = 2048
TOK = 128
LANES = 128
SEQ = 64
PARTS = 8
PAIRS = 8
BLOCKS = 8
SLOT_IN = 56
SLOT_STATE = 136
SLOT_OUT = 40
LOCAL = BLOCKS * TOK
PARAMS = pltpu.CompilerParams(vmem_limit_bytes=32 * 1024 * 1024)


def place(part, pair):
    y, low = part // 2, part % 2
    high, core = pair // 2, pair % 2
    return y * 16 + (high * 2 + low) * 2 + core


def my_place():
    me = lax.axis_index("seq")
    part = (me // 16) * 2 + (me // 2) % 2
    pair = ((me // 4) % 4) * 2 + me % 2
    return part, pair, me % 2


STATE_GROUPS = [[place(part, pair) for part in range(PARTS)] for pair in range(PAIRS)]


def nn(a, b):
    return lax.dot_general(a, b, (((1,), (0,)), ((), ())), preferred_element_type=F32)


def nt(a, b):
    return lax.dot_general(a, b, (((1,), (1,)), ((), ())), preferred_element_type=F32)


def split(value):
    high = value.astype(BF16)
    return high, (value - high.astype(F32)).astype(BF16)


def lane_iota(rows):
    return lax.broadcasted_iota(jnp.int32, (rows, LANES), 1)


def heads_over_lanes(first, second, rows):
    return jnp.where(lane_iota(rows) < 64, first, second)


def softplus(value):
    return jnp.maximum(value, 0.0) + jnp.log1p(jnp.exp(-jnp.abs(value)))


def sigmoid(value):
    return 1.0 / (1.0 + jnp.exp(-value))


def shifted_steps(frame_ref, raw, table):
    frame_here = lax.axis_index("seq") * TOK // FRAME_TOK
    index = frame_ref[frame_here]
    columns = lax.broadcasted_iota(jnp.int32, table.shape, 1)
    shift = jnp.sum(jnp.where(columns == index, table, 0.0), axis=1, keepdims=True)
    return raw + shift


def pack_kernel(frame_ref, order_ref, *refs):
    sources, out_ref, targets, sems = refs[:6], refs[6], refs[7:13], refs[13]
    copies = [
        pltpu.make_async_copy(source, target, sems.at[i])
        for i, (source, target) in enumerate(zip(sources, targets))
    ]
    for copy in copies:
        copy.start()
    raw_ref, table_ref, b_ref, c_ref, x_ref, dy_ref = targets
    order = jnp.broadcast_to(order_ref[...].astype(F32), (TOK, TOK)).T
    lane = lane_iota(TOK)
    token = ((lane % 64) * 2 + lane // 64).astype(F32)
    steps = lax.broadcasted_iota(jnp.int32, (TOK, TOK), 0).astype(F32)
    position = jnp.sum(jnp.where(order == token, steps, 0.0), axis=0, keepdims=True)
    copies[0].wait()
    copies[1].wait()
    pre = shifted_steps(frame_ref, raw_ref[...], table_ref[...])
    delta = softplus(pre).astype(BF16).astype(F32)
    gate = sigmoid(pre)
    gate_high = gate.astype(BF16).astype(F32)
    gate_low = gate - gate_high
    for copy in copies[2:]:
        copy.wait()
    for pair in range(PAIRS):
        own = slice(2 * pair, 2 * pair + 2)
        rows = jnp.concatenate(
            [position, delta[own], gate_high[own], gate_low[own], jnp.zeros((1, LANES), F32)], axis=0
        ).astype(BF16)
        proj_ref = c_ref if pair % 2 else b_ref
        columns = slice(LANES * pair, LANES * pair + LANES)
        for part in range(PARTS):
            slot = place(part, pair)
            tokens = slice(16 * part, 16 * part + 16)
            out_ref[slot, 0:16, :] = x_ref[tokens, columns]
            out_ref[slot, 16:32, :] = dy_ref[tokens, columns]
            out_ref[slot, 32:48, :] = proj_ref[tokens, :]
            out_ref[slot, 48:56, :] = rows


def to_columns(first, second):
    head_one = jnp.concatenate([first, pltpu.roll(first, LANES - 1, 1)], axis=0)
    head_two = jnp.concatenate([pltpu.roll(second, 1, 1), second], axis=0)
    return jnp.where(lane_iota(TOK) % 2 == 0, head_one, head_two)


def slope_lanes(decay_ref, pair, rows):
    return jnp.where(lane_iota(rows) % 2 == 0, -decay_ref[2 * pair], -decay_ref[2 * pair + 1])


def block_lanes(columns, block, rows):
    j = 2 * block
    return heads_over_lanes(columns[:, j : j + 1], columns[:, j + 1 : j + 2], rows)


def block_rows(block):
    return slice(block * TOK, block * TOK + TOK)


def stack(value):
    return jnp.concatenate(split(value), axis=0)


def twice(value):
    return jnp.concatenate([value, value], axis=1)


def turned(value):
    return value.astype(F32).T.astype(BF16)


def twice_split(value):
    return jnp.concatenate(split(value), axis=1)


def spread(value, wide, target_ref, base):
    wide[...] = value.reshape(SEQ * 16, LANES)
    for row in range(16):
        start = base + row * 64
        target_ref[start : start + 64, :] = wide[pl.ds(row, 64, stride=16), :].astype(BF16)


def unpack_kernel(
    decay_ref, recv_ref, data_ref, proj_ref, weight_ref, wide, wide_two, wide_three, misc
):
    part, pair, core = my_place()
    spread(recv_ref[:, 0:16, :].astype(F32), wide, data_ref, 0)
    spread(recv_ref[:, 16:32, :].astype(F32), wide_two, data_ref, LOCAL)
    spread(recv_ref[:, 32:48, :].astype(F32), wide_three, proj_ref, 0)
    misc[...] = recv_ref[:, 48:56, :].astype(F32).reshape(SEQ * 8, LANES)
    shift = (LANES - 16 * part) % LANES

    def own_lanes(row):
        return pltpu.roll(misc[pl.ds(row, 64, stride=8), :], shift, 1)

    steps = to_columns(own_lanes(1), own_lanes(2))
    gates_high = to_columns(own_lanes(3), own_lanes(4))
    gates_low = to_columns(own_lanes(5), own_lanes(6))
    pos_rows = jnp.concatenate(
        [misc[pl.ds(part * 64 + 8 * block, 1), :] for block in range(BLOCKS)], axis=0
    )
    pos_cols = jnp.concatenate([pos_rows, jnp.zeros((LANES - BLOCKS, LANES), F32)], axis=0).T
    lane = lane_iota(TOK)
    steps_bf = steps.astype(BF16)
    sums = jnp.zeros((TOK, LANES), F32)
    for block in range(BLOCKS):
        later = (pos_cols[:, block : block + 1] >= pos_rows[block : block + 1, :]).astype(F32).astype(BF16)
        sums = jnp.where(lane // 2 == block, nn(later, steps_bf), sums)
    slopes = slope_lanes(decay_ref, pair, TOK)
    logs = sums * slopes
    totals = jnp.sum(steps, axis=0, keepdims=True) * slopes[:1]
    short = jnp.where(lane_iota(1) < 2 * BLOCKS, totals, 0.0)
    onward = short
    until = pltpu.roll(short, 2, 1)
    for reach in (2, 4, 8):
        onward = onward + pltpu.roll(onward, LANES - reach, 1)
        until = until + pltpu.roll(until, reach, 1)
    base = 2 * LOCAL
    data_ref[base : base + TOK, :] = steps_bf
    data_ref[base + TOK : base + 2 * TOK, :] = gates_high.astype(BF16)
    data_ref[base + 2 * TOK : base + 3 * TOK, :] = gates_low.astype(BF16)
    data_ref[base + 3 * TOK : base + 4 * TOK, :] = pos_cols.astype(BF16)
    whole = heads_over_lanes(onward[:, 0:1], onward[:, 1:2], 1)
    top = whole.astype(BF16).astype(F32)
    middle = (whole - top).astype(BF16).astype(F32)
    bottom = whole - top - middle
    tail = jnp.concatenate([top, middle, bottom, jnp.zeros((13, LANES), F32)], axis=0).astype(BF16)
    weight_ref[2 * LOCAL : 2 * LOCAL + 16, :] = tail
    weights = steps * jnp.exp(jnp.minimum(onward - logs, 0.0))
    starts = jnp.exp(jnp.minimum(logs + until, 0.0))
    for block in range(BLOCKS):
        rows = block_rows(block)
        later_rows = slice(LOCAL + block * TOK, LOCAL + block * TOK + TOK)
        weight_ref[rows, :] = (
            data_ref[rows, :].astype(F32) * block_lanes(weights, block, TOK)
        ).astype(BF16)
        weight_ref[later_rows, :] = (
            data_ref[later_rows, :].astype(F32) * block_lanes(starts, block, TOK)
        ).astype(BF16)


def gather_kernel(mine_ref, swap_ref, data_ref, all_ref, wide):
    part, pair, core = my_place()
    all_ref[0 : 2 * LOCAL, :] = data_ref[0 : 2 * LOCAL, :]
    all_ref[4 * LOCAL : 4 * LOCAL + 4 * TOK, :] = data_ref[2 * LOCAL : 2 * LOCAL + 4 * TOK, :]

    @pl.when(core == 0)
    def _():
        all_ref[2 * LOCAL : 3 * LOCAL, :] = mine_ref[...]
        spread(swap_ref[:, 32:48, :].astype(F32), wide, all_ref, 3 * LOCAL)

    @pl.when(core == 1)
    def _():
        all_ref[3 * LOCAL : 4 * LOCAL, :] = mine_ref[...]
        spread(swap_ref[:, 32:48, :].astype(F32), wide, all_ref, 2 * LOCAL)


def states_kernel(all_ref, weight_ref, send_ref):
    part, pair, core = my_place()
    state = jnp.zeros((LANES, LANES), F32)
    adjoint = jnp.zeros((LANES, LANES), F32)
    for block in range(0, BLOCKS, 2):
        rows = slice(block * TOK, block * TOK + 2 * TOK)
        later_rows = slice(LOCAL + block * TOK, LOCAL + block * TOK + 2 * TOK)
        write = all_ref[2 * LOCAL + block * TOK : 2 * LOCAL + block * TOK + 2 * TOK, :]
        read = all_ref[3 * LOCAL + block * TOK : 3 * LOCAL + block * TOK + 2 * TOK, :]
        state = state + nn(turned(write), weight_ref[rows, :])
        adjoint = adjoint + nn(turned(read), weight_ref[later_rows, :])
    state = state.astype(BF16)
    adjoint = adjoint.astype(BF16)
    for slot in range(PARTS):
        after = slot > part

        @pl.when(after)
        def _():
            send_ref[slot, 0:128, :] = state

        @pl.when(jnp.logical_not(after))
        def _():
            send_ref[slot, 0:128, :] = adjoint

        send_ref[slot, 128:136, :] = weight_ref[2 * LOCAL : 2 * LOCAL + 16, :][:8]


def inner_kernel(decay_ref, all_ref, sums_ref, grad_ref):
    part, pair, core = my_place()
    base = 4 * LOCAL
    steps_bf = all_ref[base : base + TOK, :]
    steps = steps_bf.astype(F32)
    pos_cols = all_ref[base + 3 * TOK : base + 4 * TOK, :].astype(F32)
    pos_rows = pos_cols.T[:8]
    grad_ref[LOCAL + 2 * TOK : LOCAL + 3 * TOK, :] = jnp.zeros((TOK, LANES), F32)
    lane = lane_iota(TOK)
    sums = jnp.zeros((TOK, LANES), F32)
    masks = []
    for block in range(BLOCKS):
        behind = pos_cols[:, block : block + 1] >= pos_rows[block : block + 1, :]
        masks.append(behind.astype(F32).astype(BF16))
        sums = jnp.where(lane // 2 == block, nn(masks[block], steps_bf), sums)
    slopes = slope_lanes(decay_ref, pair, TOK)
    logs = sums * slopes
    log_rows = logs.T
    totals = jnp.sum(steps, axis=0, keepdims=True) * slopes[:1]
    starts = jnp.exp(logs)
    ends = steps * jnp.exp(totals - logs)
    grad_ref[LOCAL : LOCAL + TOK, :] = ends
    grad_ref[LOCAL + TOK : LOCAL + 2 * TOK, :] = starts
    for block in range(BLOCKS):
        rows = block_rows(block)

        def piece(number):
            return all_ref[number * LOCAL + block * TOK : number * LOCAL + block * TOK + TOK, :]

        def sums_rows(number):
            return slice(number * LOCAL + block * TOK, number * LOCAL + block * TOK + TOK)

        x, dy, write, read = piece(0), piece(1), piece(2), piece(3)
        sums_ref[2 * LOCAL + block : 2 * LOCAL + block + 1, :] = block_lanes(totals, block, 1)
        ahead = pos_rows[block : block + 1, :] >= pos_cols[:, block : block + 1]
        behind = masks[block]
        cross = nt(write, read)
        zero = jnp.zeros_like(dy)
        x_heads = (jnp.where(lane < 64, x, zero), jnp.where(lane < 64, zero, x))
        dy_stack = jnp.concatenate(
            [jnp.where(lane < 64, dy, zero), jnp.where(lane < 64, zero, dy)], axis=0
        )
        carry, mixed, seen = [], [], []
        for head in range(2):
            j = 2 * block + head
            gap = log_rows[j : j + 1, :] - logs[:, j : j + 1]
            decay = jnp.exp(jnp.where(ahead, gap, -1e30))
            carry.append(decay * cross)
            mixed.append(decay * (nt(x_heads[head], dy) * steps[:, j : j + 1]))
            seen.append(twice_split(mixed[head] * cross))
        crossed = nn(jnp.concatenate(seen, axis=0), jnp.concatenate([behind, behind], axis=0))
        for head in range(2):
            j = LOCAL + 2 * TOK + 2 * block + head
            own = jnp.where(ahead, crossed[head * TOK : head * TOK + TOK], 0.0)
            grad_ref[j : j + 1, :] = jnp.sum(own, axis=0, keepdims=True)
        high, low = split(jnp.concatenate(carry, axis=1))
        grad_ref[rows, :] = block_lanes(steps, block, TOK) * (nn(high, dy_stack) + nn(low, dy_stack))
        both = mixed[0] + mixed[1]
        sums_ref[sums_rows(0), :] = nn(twice_split(both), jnp.concatenate([read, read], axis=0))
        sums_ref[sums_rows(1), :] = nn(twice_split(both.T), jnp.concatenate([write, write], axis=0))


def outer_kernel(recv_ref, sums_ref, data_ref, grad_ref, keep_ref, give_ref, all_ref, adj, wide_w, wide_r):
    part, pair, core = my_place()

    def arrive(slot, state):
        tail = recv_ref[slot, 128:136, :].astype(F32)
        total = tail[0:1] + tail[1:2] + tail[2:3]
        return state * jnp.exp(total) + recv_ref[slot, 0:128, :].astype(F32)

    zero = jnp.zeros((LANES, LANES), F32)
    state = lax.fori_loop(0, part, arrive, zero)
    adjoint = lax.fori_loop(0, PARTS - 1 - part, lambda k, a: arrive(PARTS - 1 - k, a), zero)
    keeps = jnp.exp(sums_ref[2 * LOCAL : 2 * LOCAL + 8, :])

    def sums_rows(number, block):
        return slice(number * LOCAL + block * TOK, number * LOCAL + block * TOK + TOK)

    ends = grad_ref[LOCAL : LOCAL + TOK, :]
    starts = grad_ref[LOCAL + TOK : LOCAL + 2 * TOK, :]

    def data_rows(number, block):
        return slice(number * LOCAL + block * TOK, number * LOCAL + block * TOK + TOK)

    gains, ds, xe = [], [], []
    for block in range(BLOCKS):
        xe.append(split(data_ref[data_rows(0, block), :].astype(F32) * block_lanes(ends, block, TOK)))
        ds.append(split(data_ref[data_rows(1, block), :].astype(F32) * block_lanes(starts, block, TOK)))
        write = twice(turned(data_ref[data_rows(2, block), :]))
        read = twice(turned(data_ref[data_rows(3, block), :]))
        gains.append((nn(write, jnp.concatenate(xe[block], axis=0)), nn(read, jnp.concatenate(ds[block], axis=0))))
    for block in reversed(range(BLOCKS)):
        adj[block] = adjoint
        adjoint = adjoint * keeps[block : block + 1] + gains[block][1]
    overlaps = []
    for block in range(BLOCKS):
        adjoint = adj[block]
        state_high, state_low = split(state)
        adj_high, adj_low = split(adjoint)
        first = block * 2 * TOK
        all_ref[4 * LOCAL + first : 4 * LOCAL + first + TOK, :] = state_high
        all_ref[4 * LOCAL + first + TOK : 4 * LOCAL + first + 2 * TOK, :] = state_low
        all_ref[6 * LOCAL + first : 6 * LOCAL + first + TOK, :] = adj_high
        all_ref[6 * LOCAL + first + TOK : 6 * LOCAL + first + 2 * TOK, :] = adj_low
        keep = keeps[block : block + 1]
        overlaps.append(jnp.sum(adjoint * state, axis=0, keepdims=True) * keep)
        ds_high, ds_low = ds[block]
        xe_high, xe_low = xe[block]
        all_ref[first : first + TOK, :] = ds_high
        all_ref[first + TOK : first + 2 * TOK, :] = ds_low
        all_ref[2 * LOCAL + first : 2 * LOCAL + first + TOK, :] = xe_high
        all_ref[2 * LOCAL + first + TOK : 2 * LOCAL + first + 2 * TOK, :] = xe_low
        gr = sums_ref[sums_rows(1, block), :] + (
            nt(jnp.concatenate([ds_high, ds_low], axis=1), twice(state_high)) + nt(ds_high, state_low)
        )
        gw = sums_ref[sums_rows(0, block), :] + (
            nt(jnp.concatenate([xe_high, xe_low], axis=1), twice(adj_high)) + nt(xe_high, adj_low)
        )
        for half in range(2):
            out_rows = pl.ds(2 * block + half, 64, stride=16)
            wide_w[out_rows, :] = gw[64 * half : 64 * half + 64]
            wide_r[out_rows, :] = gr[64 * half : 64 * half + 64]
        state = state * keep + gains[block][0]
    overlaps = jnp.concatenate(overlaps, axis=0)
    top = overlaps.astype(BF16).astype(F32)
    middle = (overlaps - top).astype(BF16).astype(F32)
    bottom = overlaps - top - middle
    all_ref[8 * LOCAL : 8 * LOCAL + 32, :] = jnp.concatenate(
        [top, middle, bottom, jnp.zeros((8, LANES), F32)], axis=0
    ).astype(BF16)

    @pl.when(core == 0)
    def _():
        keep_ref[...] = wide_w[...]
        give_ref[...] = wide_r[...]

    @pl.when(core == 1)
    def _():
        keep_ref[...] = wide_r[...]
        give_ref[...] = wide_w[...]


def grads_kernel(decay_ref, data_ref, all_ref, grad_ref, out_ref, wide, misc):
    part, pair, core = my_place()
    slopes = slope_lanes(decay_ref, pair, TOK)
    base = 4 * LOCAL
    steps = data_ref[base : base + TOK, :].astype(F32)
    gates = data_ref[base + TOK : base + 2 * TOK, :].astype(F32) + data_ref[base + 2 * TOK : base + 3 * TOK, :].astype(F32)
    pos_cols = data_ref[base + 3 * TOK : base + 4 * TOK, :].astype(F32)
    pos_rows = pos_cols.T[:8]
    ends = grad_ref[LOCAL : LOCAL + TOK, :]
    lane = lane_iota(TOK)
    tail = all_ref[8 * LOCAL : 8 * LOCAL + 32, :].astype(F32)
    overlaps = tail[0:8] + tail[8:16] + tail[16:24]
    row_lane = lane_iota(8)
    row = lax.broadcasted_iota(jnp.int32, (8, LANES), 0)
    first = jnp.sum(jnp.where(row_lane < 64, overlaps, 0.0), axis=1, keepdims=True)
    second = jnp.sum(jnp.where(row_lane < 64, 0.0, overlaps), axis=1, keepdims=True)
    kept = jnp.where(row_lane == 2 * row, first, jnp.where(row_lane == 2 * row + 1, second, 0.0))
    sub = lax.broadcasted_iota(jnp.int32, (2 * LANES, LANES), 0) % LANES // 64
    pick_lane = lax.broadcasted_iota(jnp.int32, (2 * LANES, LANES), 1)
    per_head = jnp.zeros((3 * TOK, LANES), F32)
    for block in range(BLOCKS):
        rows = block_rows(block)
        lo = block * 2 * TOK

        def both(number):
            start = number * LOCAL + lo
            return all_ref[start : start + TOK, :].astype(F32) + all_ref[start + TOK : start + 2 * TOK, :].astype(F32)

        x = data_ref[rows, :].astype(F32)
        write = data_ref[2 * LOCAL + block * TOK : 2 * LOCAL + block * TOK + TOK, :]
        read = data_ref[3 * LOCAL + block * TOK : 3 * LOCAL + block * TOK + TOK, :]
        carried = nn(twice(write), all_ref[6 * LOCAL + lo : 6 * LOCAL + lo + 2 * TOK, :])
        recalled = nn(twice(read), all_ref[4 * LOCAL + lo : 4 * LOCAL + lo + 2 * TOK, :])
        act = grad_ref[rows, :] + block_lanes(ends, block, TOK) * carried
        wide[pl.ds(2 * block, 64, stride=16), :] = act[:64]
        wide[pl.ds(2 * block + 1, 64, stride=16), :] = act[64:]
        products = jnp.concatenate([both(0) * recalled, both(2) * carried, x * act], axis=0)
        pick = (pick_lane == 2 * block + sub).astype(F32).astype(BF16)
        per_head = per_head + nn(twice_split(products), pick)

    direct = per_head[2 * TOK :]
    read_high, read_low = split(per_head[:TOK].T[: 2 * BLOCKS])
    write_part = per_head[TOK : 2 * TOK].T[: 2 * BLOCKS]
    write_high, write_low = split(write_part)
    vectors = jnp.concatenate([read_high, read_low, write_high, write_low], axis=0)
    log_rows = grad_ref[LOCAL + 2 * TOK : LOCAL + 2 * TOK + 2 * BLOCKS, :]
    log_rows = log_rows + write_part + jnp.sum(write_part, axis=1, keepdims=True)
    owner = lax.broadcasted_iota(jnp.int32, (2 * BLOCKS, LANES), 0) // 2
    for block in range(BLOCKS):
        behind = (pos_cols[:, block : block + 1] >= pos_rows[block : block + 1, :]).astype(F32).astype(BF16)
        sums = nn(vectors, behind)
        added = (sums[0:16] + sums[16:32]) - (sums[32:48] + sums[48:64])
        log_rows = log_rows + jnp.where(owner == block, added, 0.0)
    log_grad = jnp.concatenate([log_rows, jnp.zeros((TOK - 2 * BLOCKS, LANES), F32)], axis=0).T
    log_grad = log_grad + jnp.sum(kept, axis=0, keepdims=True)
    grad_step = direct / steps + slopes * (log_grad - direct)
    grad_step = jnp.where(lane < 2 * BLOCKS, grad_step, 0.0).astype(BF16).astype(F32)
    grad_pre = grad_step * gates
    frames = []
    for frame in range(4):
        low_rows = slice(16 * frame, 16 * frame + 16)
        high_rows = slice(64 + 16 * frame, 80 + 16 * frame)
        frames.append(jnp.sum(grad_pre[low_rows] + grad_pre[high_rows], axis=0, keepdims=True))
    frames = jnp.concatenate(frames + [jnp.zeros((4, LANES), F32)], axis=0)
    frames_high = frames.astype(BF16).astype(F32)
    frames = frames_high + pltpu.roll(frames - frames_high, 64, 1)

    even = lane_iota(64) % 2 == 0
    top, bottom = grad_step[:64], grad_step[64:]
    shift = 16 * part
    row_one = pltpu.roll(jnp.where(even, top, pltpu.roll(bottom, 1, 1)), shift, 1)
    row_two = pltpu.roll(jnp.where(even, pltpu.roll(top, LANES - 1, 1), bottom), shift, 1)
    misc[...] = jnp.zeros((SEQ * 8, LANES), F32)
    misc[pl.ds(0, 64, stride=8), :] = row_one
    misc[pl.ds(1, 64, stride=8), :] = row_two
    for frame in range(4):
        misc[pl.ds(2 + frame, 64, stride=8), :] = jnp.broadcast_to(frames[frame : frame + 1], (SEQ, LANES))
    out_ref[:, 0:16, :] = wide[...].reshape(SEQ, 16, LANES).astype(BF16)
    out_ref[:, 16:32, :] = jnp.zeros((SEQ, 16, LANES), BF16)
    out_ref[:, 32:40, :] = misc[...].reshape(SEQ, 8, LANES).astype(BF16)


def join_kernel(in_ref, keep_ref, got_ref, out_ref):
    out_ref[:, 0:16, :] = in_ref[:, 0:16, :]
    out_ref[:, 16:32, :] = (keep_ref[...] + got_ref[...]).reshape(SEQ, 16, LANES).astype(BF16)
    out_ref[:, 32:40, :] = in_ref[:, 32:40, :]


def proj_kernel(recv_ref, proj_ref, rest_ref):
    for part in range(PARTS):
        for core in range(2):
            total = recv_ref[place(part, core), 16:32, :].astype(F32)
            for high in range(1, 4):
                total = total + recv_ref[place(part, 2 * high + core), 16:32, :].astype(F32)
            proj_ref[16 * part : 16 * part + 16, LANES * core : LANES * core + LANES] = total.astype(BF16)
    rest_ref[:, 0:16, :] = recv_ref[:, 0:16, :]
    rest_ref[:, 16:24, :] = recv_ref[:, 32:40, :]


def finish_kernel(frame_ref, recv_ref, raw_ref, table_ref, act_ref, pre_ref, grad_ref, rows_ref):
    heads = raw_ref.shape[0]
    for pair in range(PAIRS):
        columns = slice(LANES * pair, LANES * pair + LANES)
        for part in range(PARTS):
            act_ref[16 * part : 16 * part + 16, columns] = recv_ref[place(part, pair), 0:16, :]
    lane = lane_iota(8)
    per_frame = jnp.zeros((8, LANES), F32)
    for pair in range(PAIRS):
        rows = recv_ref[place(0, pair), 16:24, :].astype(F32)
        for part in range(1, PARTS):
            rows = rows + recv_ref[place(part, pair), 16:24, :].astype(F32)
        rows_ref[2 * pair : 2 * pair + 2, :] = rows[0:2]
        rows = rows + pltpu.roll(rows, 64, 1)
        for head in range(2):
            inside = (lane < 2 * BLOCKS) & (lane % 2 == head)
            total = jnp.sum(jnp.where(inside, rows, 0.0), axis=1, keepdims=True)
            per_frame = jnp.where(lane == 2 * pair + head, total, per_frame)
    pre = shifted_steps(frame_ref, raw_ref[...], table_ref[...])
    pre_ref[...] = rows_ref[...] * sigmoid(pre)
    per_head = jnp.concatenate([per_frame, jnp.zeros((LANES - 8, LANES), F32)], axis=0).T
    steps = lax.broadcasted_iota(jnp.int32, grad_ref.shape, 1)
    grad = jnp.zeros(grad_ref.shape, F32)
    for frame in range(4):
        grad = grad + jnp.where(steps == frame_ref[frame], per_head[:heads, 2 + frame : 3 + frame], 0.0)
    grad_ref[...] = grad


def total_kernel(own_ref, one_ref, two_ref, three_ref, write_ref, read_ref):
    even = own_ref[...].astype(F32) + two_ref[...].astype(F32)
    odd = one_ref[...].astype(F32) + three_ref[...].astype(F32)
    total = (even + odd).astype(BF16)
    write_ref[...] = total[:, :LANES]
    read_ref[...] = total[:, LANES:]


VMEM = pl.BlockSpec(memory_space=pltpu.VMEM)
SMEM = pl.BlockSpec(memory_space=pltpu.SMEM)


def call(kernel, name, in_specs, out_shape, scratch=(), params=PARAMS):
    shapes = [jax.ShapeDtypeStruct(shape, dtype) for shape, dtype in out_shape]
    return pl.pallas_call(
        kernel,
        out_shape=shapes,
        in_specs=in_specs,
        out_specs=[VMEM] * len(shapes),
        scratch_shapes=list(scratch),
        compiler_params=params,
        name=name,
    )


def shards(
    activations, grad_out, write_proj, read_proj, step_raw, step_table, decay_rate, frame_step, scan_order
):
    raw, table = step_raw.T, step_table.T
    swap_core = [(i, i ^ 1) for i in range(SEQ)]
    hbm = pl.BlockSpec(memory_space=pltpu.HBM)
    sources = (raw, table, write_proj, read_proj, activations, grad_out)
    (send,) = call(
        pack_kernel, "pack", [SMEM, VMEM] + [hbm] * 6, [((SEQ, SLOT_IN, LANES), BF16)],
        [pltpu.VMEM(a.shape, a.dtype) for a in sources] + [pltpu.SemaphoreType.DMA((6,))],
        pltpu.CompilerParams(vmem_limit_bytes=62 * 1024 * 1024),
    )(frame_step, scan_order.reshape(1, TOK), *sources)
    recv = lax.all_to_all(send, "seq", 0, 0, tiled=True)
    swap = lax.ppermute(recv, "seq", swap_core)
    wide = pltpu.VMEM((LOCAL, LANES), F32)
    bundle = ((4 * LOCAL + 4 * TOK, LANES), BF16)
    sums = ((LOCAL, LANES), F32)
    data, mine, weight = call(
        unpack_kernel, "unpack", [SMEM, VMEM],
        [((2 * LOCAL + 4 * TOK, LANES), BF16), ((LOCAL, LANES), BF16), ((2 * LOCAL + 16, LANES), BF16)],
        [wide] * 3 + [pltpu.VMEM((SEQ * 8, LANES), F32)],
    )(decay_rate, recv)
    (data,) = call(gather_kernel, "gather", [VMEM] * 3, [bundle], [wide])(mine, swap, data)
    (states,) = call(states_kernel, "states", [VMEM] * 2, [((PARTS, SLOT_STATE, LANES), BF16)])(data, weight)
    states = lax.all_to_all(states, "seq", 0, 0, tiled=True, axis_index_groups=STATE_GROUPS)
    inner, grad = call(
        inner_kernel, "inner", [SMEM, VMEM],
        [
            ((2 * LOCAL + 8, LANES), F32),
            ((LOCAL + 3 * TOK, LANES), F32),
        ],
    )(decay_rate, data)
    keep, give, pairs = call(
        outer_kernel, "outer", [VMEM] * 4,
        [sums] * 2 + [((8 * LOCAL + 32, LANES), BF16)],
        [pltpu.VMEM((BLOCKS, LANES, LANES), F32)] + [wide] * 2,
    )(states, inner, data, grad)
    got = lax.ppermute(give, "seq", swap_core)
    (out,) = call(
        grads_kernel, "grads", [SMEM] + [VMEM] * 3, [((SEQ, SLOT_OUT, LANES), BF16)],
        [wide, pltpu.VMEM((SEQ * 8, LANES), F32)],
    )(decay_rate, data, pairs, grad)
    (out,) = call(join_kernel, "join", [VMEM] * 3, [((SEQ, SLOT_OUT, LANES), BF16)])(out, keep, got)
    back = lax.all_to_all(out, "seq", 0, 0, tiled=True)
    proj, rest = call(
        proj_kernel, "proj", [VMEM], [((TOK, 2 * LANES), BF16), ((SEQ, 24, LANES), BF16)]
    )(back)
    ring = [lax.ppermute(proj, "head", [(i, (i + k) % 4) for i in range(4)]) for k in (1, 2, 3)]
    act, grad_pre, grad_table = call(
        finish_kernel, "finish", [SMEM] + [VMEM] * 3,
        [(activations.shape, BF16), (raw.shape, F32), (table.shape, F32)],
        [pltpu.VMEM((2 * PAIRS, LANES), F32)],
    )(frame_step, rest, raw, table)
    grad_write, grad_read = call(
        total_kernel, "total", [VMEM] * 4, [(write_proj.shape, BF16), (read_proj.shape, BF16)]
    )(proj, *ring)
    return (act, grad_write, grad_read, grad_pre.T, grad_table.T)


def solution(mesh):
    in_specs = (
        P("seq", "head"),
        P("seq", "head"),
        P("seq", None),
        P("seq", None),
        P("seq", "head"),
        P(None, "head"),
        P("head"),
        P(),
        P("seq"),
    )
    out_specs = (
        P("seq", "head"),
        P("seq", None),
        P("seq", None),
        P("seq", "head"),
        P(None, "head"),
    )
    return jax.shard_map(shards, mesh=mesh, in_specs=in_specs, out_specs=out_specs, check_vma=False)
```

```python
import jax
import jax.numpy as jnp
from jax import lax
from jax.experimental import pallas as pl
from jax.experimental.pallas import tpu as pltpu
from jax.sharding import PartitionSpec as P

F32 = jnp.float32
BF16 = jnp.bfloat16
FRAME_TOK = 2048
TOK = 128
LANES = 128
SEQ = 64
PARTS = 8
PAIRS = 8
BLOCKS = 8
SLOT_IN = 56
SLOT_STATE = 136
SLOT_OUT = 40
LOCAL = BLOCKS * TOK
PARAMS = pltpu.CompilerParams(vmem_limit_bytes=32 * 1024 * 1024)


def place(part, pair):
    y, low = part // 2, part % 2
    high, core = pair // 2, pair % 2
    return y * 16 + (high * 2 + low) * 2 + core


def my_place():
    me = lax.axis_index("seq")
    part = (me // 16) * 2 + (me // 2) % 2
    pair = ((me // 4) % 4) * 2 + me % 2
    return part, pair, me % 2


STATE_GROUPS = [[place(part, pair) for part in range(PARTS)] for pair in range(PAIRS)]


def nn(a, b):
    return lax.dot_general(a, b, (((1,), (0,)), ((), ())), preferred_element_type=F32)


def nt(a, b):
    return lax.dot_general(a, b, (((1,), (1,)), ((), ())), preferred_element_type=F32)


def split(value):
    high = value.astype(BF16)
    return high, (value - high.astype(F32)).astype(BF16)


def lane_iota(rows):
    return lax.broadcasted_iota(jnp.int32, (rows, LANES), 1)


def heads_over_lanes(first, second, rows):
    return jnp.where(lane_iota(rows) < 64, first, second)


def softplus(value):
    return jnp.maximum(value, 0.0) + jnp.log1p(jnp.exp(-jnp.abs(value)))


def sigmoid(value):
    return 1.0 / (1.0 + jnp.exp(-value))


def shifted_steps(frame_ref, raw, table):
    frame_here = lax.axis_index("seq") * TOK // FRAME_TOK
    index = frame_ref[frame_here]
    columns = lax.broadcasted_iota(jnp.int32, table.shape, 1)
    shift = jnp.sum(jnp.where(columns == index, table, 0.0), axis=1, keepdims=True)
    return raw + shift


def pack_kernel(*refs):
    sources, out_ref, targets, sems = refs[:8], refs[8], refs[9:17], refs[17]
    copies = [
        pltpu.make_async_copy(source, target, sems.at[i])
        for i, (source, target) in enumerate(zip(sources, targets))
    ]
    for copy in copies:
        copy.start()
    order_ref, frame_ref, raw_ref, table_ref, b_ref, c_ref, x_ref, dy_ref = targets
    copies[0].wait()
    order = jnp.broadcast_to(order_ref[...].astype(F32), (TOK, TOK)).T
    lane = lane_iota(TOK)
    token = ((lane % 64) * 2 + lane // 64).astype(F32)
    steps = lax.broadcasted_iota(jnp.int32, (TOK, TOK), 0).astype(F32)
    position = jnp.sum(jnp.where(order == token, steps, 0.0), axis=0, keepdims=True)
    for copy in copies[1:4]:
        copy.wait()
    pre = shifted_steps(frame_ref, raw_ref[...], table_ref[...])
    delta = softplus(pre).astype(BF16).astype(F32)
    gate = sigmoid(pre)
    gate_high = gate.astype(BF16).astype(F32)
    gate_low = gate - gate_high
    for copy in copies[4:]:
        copy.wait()
    for pair in range(PAIRS):
        own = slice(2 * pair, 2 * pair + 2)
        rows = jnp.concatenate(
            [position, delta[own], gate_high[own], gate_low[own], jnp.zeros((1, LANES), F32)], axis=0
        ).astype(BF16)
        proj_ref = c_ref if pair % 2 else b_ref
        columns = slice(LANES * pair, LANES * pair + LANES)
        for part in range(PARTS):
            slot = place(part, pair)
            tokens = slice(16 * part, 16 * part + 16)
            out_ref[slot, 0:16, :] = x_ref[tokens, columns]
            out_ref[slot, 16:32, :] = dy_ref[tokens, columns]
            out_ref[slot, 32:48, :] = proj_ref[tokens, :]
            out_ref[slot, 48:56, :] = rows


def to_columns(first, second):
    head_one = jnp.concatenate([first, pltpu.roll(first, LANES - 1, 1)], axis=0)
    head_two = jnp.concatenate([pltpu.roll(second, 1, 1), second], axis=0)
    return jnp.where(lane_iota(TOK) % 2 == 0, head_one, head_two)


def slope_lanes(decay_ref, pair, rows):
    rates = decay_ref[...]
    lane = lax.broadcasted_iota(jnp.int32, rates.shape, 1)
    first = jnp.sum(jnp.where(lane == 2 * pair, rates, 0.0), axis=1, keepdims=True)
    second = jnp.sum(jnp.where(lane == 2 * pair + 1, rates, 0.0), axis=1, keepdims=True)
    return jnp.where(lane_iota(rows) % 2 == 0, -first, -second)


def block_lanes(columns, block, rows):
    j = 2 * block
    return heads_over_lanes(columns[:, j : j + 1], columns[:, j + 1 : j + 2], rows)


def block_rows(block):
    return slice(block * TOK, block * TOK + TOK)


def stack(value):
    return jnp.concatenate(split(value), axis=0)


def twice(value):
    return jnp.concatenate([value, value], axis=1)


def turned(value):
    return value.astype(F32).T.astype(BF16)


def twice_split(value):
    return jnp.concatenate(split(value), axis=1)


def spread(value, wide, target_ref, base):
    wide[...] = value.reshape(SEQ * 16, LANES)
    for row in range(16):
        start = base + row * 64
        target_ref[start : start + 64, :] = wide[pl.ds(row, 64, stride=16), :].astype(BF16)


def cut_kernel(recv_ref, proj_ref):
    proj_ref[...] = recv_ref[:, 32:48, :]


def unpack_kernel(
    decay_ref, recv_ref, data_ref, proj_ref, weight_ref, wide, wide_two, wide_three, misc
):
    part, pair, core = my_place()
    spread(recv_ref[:, 0:16, :].astype(F32), wide, data_ref, 0)
    spread(recv_ref[:, 16:32, :].astype(F32), wide_two, data_ref, LOCAL)
    spread(recv_ref[:, 32:48, :].astype(F32), wide_three, proj_ref, 0)
    misc[...] = recv_ref[:, 48:56, :].astype(F32).reshape(SEQ * 8, LANES)
    shift = (LANES - 16 * part) % LANES

    def own_lanes(row):
        return pltpu.roll(misc[pl.ds(row, 64, stride=8), :], shift, 1)

    steps = to_columns(own_lanes(1), own_lanes(2))
    gates_high = to_columns(own_lanes(3), own_lanes(4))
    gates_low = to_columns(own_lanes(5), own_lanes(6))
    pos_rows = jnp.concatenate(
        [misc[pl.ds(part * 64 + 8 * block, 1), :] for block in range(BLOCKS)], axis=0
    )
    pos_cols = jnp.concatenate([pos_rows, jnp.zeros((LANES - BLOCKS, LANES), F32)], axis=0).T
    lane = lane_iota(TOK)
    steps_bf = steps.astype(BF16)
    sums = jnp.zeros((TOK, LANES), F32)
    for block in range(BLOCKS):
        later = (pos_cols[:, block : block + 1] >= pos_rows[block : block + 1, :]).astype(F32).astype(BF16)
        sums = jnp.where(lane // 2 == block, nn(later, steps_bf), sums)
    slopes = slope_lanes(decay_ref, pair, TOK)
    logs = sums * slopes
    totals = jnp.sum(steps, axis=0, keepdims=True) * slopes[:1]
    short = jnp.where(lane_iota(1) < 2 * BLOCKS, totals, 0.0)
    onward = short
    until = pltpu.roll(short, 2, 1)
    for reach in (2, 4, 8):
        onward = onward + pltpu.roll(onward, LANES - reach, 1)
        until = until + pltpu.roll(until, reach, 1)
    base = 2 * LOCAL
    data_ref[base : base + TOK, :] = steps_bf
    data_ref[base + TOK : base + 2 * TOK, :] = gates_high.astype(BF16)
    data_ref[base + 2 * TOK : base + 3 * TOK, :] = gates_low.astype(BF16)
    data_ref[base + 3 * TOK : base + 4 * TOK, :] = pos_cols.astype(BF16)
    whole = heads_over_lanes(onward[:, 0:1], onward[:, 1:2], 1)
    top = whole.astype(BF16).astype(F32)
    middle = (whole - top).astype(BF16).astype(F32)
    bottom = whole - top - middle
    tail = jnp.concatenate([top, middle, bottom, jnp.zeros((13, LANES), F32)], axis=0).astype(BF16)
    weight_ref[2 * LOCAL : 2 * LOCAL + 16, :] = tail
    weights = steps * jnp.exp(jnp.minimum(onward - logs, 0.0))
    starts = jnp.exp(jnp.minimum(logs + until, 0.0))
    for block in range(BLOCKS):
        rows = block_rows(block)
        later_rows = slice(LOCAL + block * TOK, LOCAL + block * TOK + TOK)
        weight_ref[rows, :] = (
            data_ref[rows, :].astype(F32) * block_lanes(weights, block, TOK)
        ).astype(BF16)
        weight_ref[later_rows, :] = (
            data_ref[later_rows, :].astype(F32) * block_lanes(starts, block, TOK)
        ).astype(BF16)


def gather_kernel(mine_ref, swap_ref, data_ref, all_ref, wide):
    part, pair, core = my_place()
    all_ref[0 : 2 * LOCAL, :] = data_ref[0 : 2 * LOCAL, :]
    all_ref[4 * LOCAL : 4 * LOCAL + 4 * TOK, :] = data_ref[2 * LOCAL : 2 * LOCAL + 4 * TOK, :]

    @pl.when(core == 0)
    def _():
        all_ref[2 * LOCAL : 3 * LOCAL, :] = mine_ref[...]
        spread(swap_ref[...].astype(F32), wide, all_ref, 3 * LOCAL)

    @pl.when(core == 1)
    def _():
        all_ref[3 * LOCAL : 4 * LOCAL, :] = mine_ref[...]
        spread(swap_ref[...].astype(F32), wide, all_ref, 2 * LOCAL)


def states_kernel(all_ref, weight_ref, send_ref):
    part, pair, core = my_place()
    state = jnp.zeros((LANES, LANES), F32)
    adjoint = jnp.zeros((LANES, LANES), F32)
    for block in range(0, BLOCKS, 2):
        rows = slice(block * TOK, block * TOK + 2 * TOK)
        later_rows = slice(LOCAL + block * TOK, LOCAL + block * TOK + 2 * TOK)
        write = all_ref[2 * LOCAL + block * TOK : 2 * LOCAL + block * TOK + 2 * TOK, :]
        read = all_ref[3 * LOCAL + block * TOK : 3 * LOCAL + block * TOK + 2 * TOK, :]
        state = state + nn(turned(write), weight_ref[rows, :])
        adjoint = adjoint + nn(turned(read), weight_ref[later_rows, :])
    state = state.astype(BF16)
    adjoint = adjoint.astype(BF16)
    for slot in range(PARTS):
        after = slot > part

        @pl.when(after)
        def _():
            send_ref[slot, 0:128, :] = state

        @pl.when(jnp.logical_not(after))
        def _():
            send_ref[slot, 0:128, :] = adjoint

        send_ref[slot, 128:136, :] = weight_ref[2 * LOCAL : 2 * LOCAL + 16, :][:8]


def inner_kernel(decay_ref, all_ref, sums_ref, grad_ref):
    part, pair, core = my_place()
    base = 4 * LOCAL
    steps_bf = all_ref[base : base + TOK, :]
    steps = steps_bf.astype(F32)
    pos_cols = all_ref[base + 3 * TOK : base + 4 * TOK, :].astype(F32)
    pos_rows = pos_cols.T[:8]
    grad_ref[LOCAL + 2 * TOK : LOCAL + 3 * TOK, :] = jnp.zeros((TOK, LANES), F32)
    lane = lane_iota(TOK)
    sums = jnp.zeros((TOK, LANES), F32)
    masks = []
    for block in range(BLOCKS):
        behind = pos_cols[:, block : block + 1] >= pos_rows[block : block + 1, :]
        masks.append(behind.astype(F32).astype(BF16))
        sums = jnp.where(lane // 2 == block, nn(masks[block], steps_bf), sums)
    slopes = slope_lanes(decay_ref, pair, TOK)
    logs = sums * slopes
    log_rows = logs.T
    totals = jnp.sum(steps, axis=0, keepdims=True) * slopes[:1]
    starts = jnp.exp(logs)
    ends = steps * jnp.exp(totals - logs)
    grad_ref[LOCAL : LOCAL + TOK, :] = ends
    grad_ref[LOCAL + TOK : LOCAL + 2 * TOK, :] = starts
    for block in range(BLOCKS):
        rows = block_rows(block)

        def piece(number):
            return all_ref[number * LOCAL + block * TOK : number * LOCAL + block * TOK + TOK, :]

        def sums_rows(number):
            return slice(number * LOCAL + block * TOK, number * LOCAL + block * TOK + TOK)

        x, dy, write, read = piece(0), piece(1), piece(2), piece(3)
        sums_ref[2 * LOCAL + block : 2 * LOCAL + block + 1, :] = block_lanes(totals, block, 1)
        ahead = pos_rows[block : block + 1, :] >= pos_cols[:, block : block + 1]
        behind = masks[block]
        cross = nt(write, read)
        zero = jnp.zeros_like(dy)
        x_heads = (jnp.where(lane < 64, x, zero), jnp.where(lane < 64, zero, x))
        dy_stack = jnp.concatenate(
            [jnp.where(lane < 64, dy, zero), jnp.where(lane < 64, zero, dy)], axis=0
        )
        carry, mixed, seen = [], [], []
        for head in range(2):
            j = 2 * block + head
            gap = log_rows[j : j + 1, :] - logs[:, j : j + 1]
            decay = jnp.exp(jnp.where(ahead, gap, -1e30))
            carry.append(decay * cross)
            mixed.append(decay * (nt(x_heads[head], dy) * steps[:, j : j + 1]))
            seen.append(twice_split(mixed[head] * cross))
        crossed = nn(jnp.concatenate(seen, axis=0), jnp.concatenate([behind, behind], axis=0))
        for head in range(2):
            j = LOCAL + 2 * TOK + 2 * block + head
            own = jnp.where(ahead, crossed[head * TOK : head * TOK + TOK], 0.0)
            grad_ref[j : j + 1, :] = jnp.sum(own, axis=0, keepdims=True)
        high, low = split(jnp.concatenate(carry, axis=1))
        grad_ref[rows, :] = block_lanes(steps, block, TOK) * (nn(high, dy_stack) + nn(low, dy_stack))
        both = mixed[0] + mixed[1]
        sums_ref[sums_rows(0), :] = nn(twice_split(both), jnp.concatenate([read, read], axis=0))
        sums_ref[sums_rows(1), :] = nn(twice_split(both.T), jnp.concatenate([write, write], axis=0))


def outer_kernel(recv_ref, sums_ref, data_ref, grad_ref, keep_ref, give_ref, all_ref, adj, wide_w, wide_r):
    part, pair, core = my_place()

    totals = []
    for slot in range(PARTS):
        tail = recv_ref[slot, 128:136, :].astype(F32)
        totals.append(tail[0:1] + tail[1:2] + tail[2:3])
    zero = jnp.zeros((1, LANES), F32)
    state = jnp.zeros((LANES, LANES), F32)
    adjoint = jnp.zeros((LANES, LANES), F32)
    after, before = zero, zero
    weights = [None] * PARTS
    for slot in reversed(range(PARTS)):
        weights[slot] = jnp.where(slot < part, jnp.exp(after), zero)
        after = after + jnp.where(slot < part, totals[slot], zero)
    for slot in range(PARTS):
        weight = jnp.where(slot > part, jnp.exp(before), zero)
        before = before + jnp.where(slot > part, totals[slot], zero)
        sent = recv_ref[slot, 0:128, :].astype(F32)
        state = state + weights[slot] * sent
        adjoint = adjoint + weight * sent
    keeps = jnp.exp(sums_ref[2 * LOCAL : 2 * LOCAL + 8, :])

    def sums_rows(number, block):
        return slice(number * LOCAL + block * TOK, number * LOCAL + block * TOK + TOK)

    ends = grad_ref[LOCAL : LOCAL + TOK, :]
    starts = grad_ref[LOCAL + TOK : LOCAL + 2 * TOK, :]

    def data_rows(number, block):
        return slice(number * LOCAL + block * TOK, number * LOCAL + block * TOK + TOK)

    gains, ds, xe = [], [], []
    for block in range(BLOCKS):
        xe.append(split(data_ref[data_rows(0, block), :].astype(F32) * block_lanes(ends, block, TOK)))
        ds.append(split(data_ref[data_rows(1, block), :].astype(F32) * block_lanes(starts, block, TOK)))
        write = twice(turned(data_ref[data_rows(2, block), :]))
        read = twice(turned(data_ref[data_rows(3, block), :]))
        gains.append((nn(write, jnp.concatenate(xe[block], axis=0)), nn(read, jnp.concatenate(ds[block], axis=0))))
    for block in reversed(range(BLOCKS)):
        adj[block] = adjoint
        adjoint = adjoint * keeps[block : block + 1] + gains[block][1]
    overlaps = []
    for block in range(BLOCKS):
        adjoint = adj[block]
        state_high, state_low = split(state)
        adj_high, adj_low = split(adjoint)
        first = block * 2 * TOK
        all_ref[4 * LOCAL + first : 4 * LOCAL + first + TOK, :] = state_high
        all_ref[4 * LOCAL + first + TOK : 4 * LOCAL + first + 2 * TOK, :] = state_low
        all_ref[6 * LOCAL + first : 6 * LOCAL + first + TOK, :] = adj_high
        all_ref[6 * LOCAL + first + TOK : 6 * LOCAL + first + 2 * TOK, :] = adj_low
        keep = keeps[block : block + 1]
        overlaps.append(jnp.sum(adjoint * state, axis=0, keepdims=True) * keep)
        ds_high, ds_low = ds[block]
        xe_high, xe_low = xe[block]
        all_ref[first : first + TOK, :] = ds_high
        all_ref[first + TOK : first + 2 * TOK, :] = ds_low
        all_ref[2 * LOCAL + first : 2 * LOCAL + first + TOK, :] = xe_high
        all_ref[2 * LOCAL + first + TOK : 2 * LOCAL + first + 2 * TOK, :] = xe_low
        gr = sums_ref[sums_rows(1, block), :] + (
            nt(jnp.concatenate([ds_high, ds_low], axis=1), twice(state_high)) + nt(ds_high, state_low)
        )
        gw = sums_ref[sums_rows(0, block), :] + (
            nt(jnp.concatenate([xe_high, xe_low], axis=1), twice(adj_high)) + nt(xe_high, adj_low)
        )
        for half in range(2):
            out_rows = pl.ds(2 * block + half, 64, stride=16)
            wide_w[out_rows, :] = gw[64 * half : 64 * half + 64]
            wide_r[out_rows, :] = gr[64 * half : 64 * half + 64]
        state = state * keep + gains[block][0]
    overlaps = jnp.concatenate(overlaps, axis=0)
    top = overlaps.astype(BF16).astype(F32)
    middle = (overlaps - top).astype(BF16).astype(F32)
    bottom = overlaps - top - middle
    all_ref[8 * LOCAL : 8 * LOCAL + 32, :] = jnp.concatenate(
        [top, middle, bottom, jnp.zeros((8, LANES), F32)], axis=0
    ).astype(BF16)

    @pl.when(core == 0)
    def _():
        keep_ref[...] = wide_w[...]
        give_ref[...] = wide_r[...]

    @pl.when(core == 1)
    def _():
        keep_ref[...] = wide_r[...]
        give_ref[...] = wide_w[...]


def grads_kernel(decay_ref, data_ref, all_ref, grad_ref, out_ref, wide, misc):
    part, pair, core = my_place()
    slopes = slope_lanes(decay_ref, pair, TOK)
    base = 4 * LOCAL
    steps = data_ref[base : base + TOK, :].astype(F32)
    gates = data_ref[base + TOK : base + 2 * TOK, :].astype(F32) + data_ref[base + 2 * TOK : base + 3 * TOK, :].astype(F32)
    pos_cols = data_ref[base + 3 * TOK : base + 4 * TOK, :].astype(F32)
    pos_rows = pos_cols.T[:8]
    ends = grad_ref[LOCAL : LOCAL + TOK, :]
    lane = lane_iota(TOK)
    tail = all_ref[8 * LOCAL : 8 * LOCAL + 32, :].astype(F32)
    overlaps = tail[0:8] + tail[8:16] + tail[16:24]
    row_lane = lane_iota(8)
    row = lax.broadcasted_iota(jnp.int32, (8, LANES), 0)
    first = jnp.sum(jnp.where(row_lane < 64, overlaps, 0.0), axis=1, keepdims=True)
    second = jnp.sum(jnp.where(row_lane < 64, 0.0, overlaps), axis=1, keepdims=True)
    kept = jnp.where(row_lane == 2 * row, first, jnp.where(row_lane == 2 * row + 1, second, 0.0))
    sub = lax.broadcasted_iota(jnp.int32, (2 * LANES, LANES), 0) % LANES // 64
    pick_lane = lax.broadcasted_iota(jnp.int32, (2 * LANES, LANES), 1)
    per_head = jnp.zeros((3 * TOK, LANES), F32)
    for block in range(BLOCKS):
        rows = block_rows(block)
        lo = block * 2 * TOK

        def both(number):
            start = number * LOCAL + lo
            return all_ref[start : start + TOK, :].astype(F32) + all_ref[start + TOK : start + 2 * TOK, :].astype(F32)

        x = data_ref[rows, :].astype(F32)
        write = data_ref[2 * LOCAL + block * TOK : 2 * LOCAL + block * TOK + TOK, :]
        read = data_ref[3 * LOCAL + block * TOK : 3 * LOCAL + block * TOK + TOK, :]
        carried = nn(twice(write), all_ref[6 * LOCAL + lo : 6 * LOCAL + lo + 2 * TOK, :])
        recalled = nn(twice(read), all_ref[4 * LOCAL + lo : 4 * LOCAL + lo + 2 * TOK, :])
        act = grad_ref[rows, :] + block_lanes(ends, block, TOK) * carried
        wide[pl.ds(2 * block, 64, stride=16), :] = act[:64]
        wide[pl.ds(2 * block + 1, 64, stride=16), :] = act[64:]
        products = jnp.concatenate([both(0) * recalled, both(2) * carried, x * act], axis=0)
        pick = (pick_lane == 2 * block + sub).astype(F32).astype(BF16)
        per_head = per_head + nn(twice_split(products), pick)

    direct = per_head[2 * TOK :]
    read_high, read_low = split(per_head[:TOK].T[: 2 * BLOCKS])
    write_part = per_head[TOK : 2 * TOK].T[: 2 * BLOCKS]
    write_high, write_low = split(write_part)
    vectors = jnp.concatenate([read_high, read_low, write_high, write_low], axis=0)
    log_rows = grad_ref[LOCAL + 2 * TOK : LOCAL + 2 * TOK + 2 * BLOCKS, :]
    log_rows = log_rows + write_part + jnp.sum(write_part, axis=1, keepdims=True)
    owner = lax.broadcasted_iota(jnp.int32, (2 * BLOCKS, LANES), 0) // 2
    for block in range(BLOCKS):
        behind = (pos_cols[:, block : block + 1] >= pos_rows[block : block + 1, :]).astype(F32).astype(BF16)
        sums = nn(vectors, behind)
        added = (sums[0:16] + sums[16:32]) - (sums[32:48] + sums[48:64])
        log_rows = log_rows + jnp.where(owner == block, added, 0.0)
    log_grad = jnp.concatenate([log_rows, jnp.zeros((TOK - 2 * BLOCKS, LANES), F32)], axis=0).T
    log_grad = log_grad + jnp.sum(kept, axis=0, keepdims=True)
    grad_step = direct / steps + slopes * (log_grad - direct)
    grad_step = jnp.where(lane < 2 * BLOCKS, grad_step, 0.0).astype(BF16).astype(F32)
    grad_pre = grad_step * gates
    frames = []
    for frame in range(4):
        low_rows = slice(16 * frame, 16 * frame + 16)
        high_rows = slice(64 + 16 * frame, 80 + 16 * frame)
        frames.append(jnp.sum(grad_pre[low_rows] + grad_pre[high_rows], axis=0, keepdims=True))
    frames = jnp.concatenate(frames + [jnp.zeros((4, LANES), F32)], axis=0)
    frames_high = frames.astype(BF16).astype(F32)
    frames = frames_high + pltpu.roll(frames - frames_high, 64, 1)

    even = lane_iota(64) % 2 == 0
    top, bottom = grad_step[:64], grad_step[64:]
    shift = 16 * part
    row_one = pltpu.roll(jnp.where(even, top, pltpu.roll(bottom, 1, 1)), shift, 1)
    row_two = pltpu.roll(jnp.where(even, pltpu.roll(top, LANES - 1, 1), bottom), shift, 1)
    misc[...] = jnp.zeros((SEQ * 8, LANES), F32)
    misc[pl.ds(0, 64, stride=8), :] = row_one
    misc[pl.ds(1, 64, stride=8), :] = row_two
    for frame in range(4):
        misc[pl.ds(2 + frame, 64, stride=8), :] = jnp.broadcast_to(frames[frame : frame + 1], (SEQ, LANES))
    out_ref[:, 0:16, :] = wide[...].reshape(SEQ, 16, LANES).astype(BF16)
    out_ref[:, 16:32, :] = jnp.zeros((SEQ, 16, LANES), BF16)
    out_ref[:, 32:40, :] = misc[...].reshape(SEQ, 8, LANES).astype(BF16)


def join_kernel(in_ref, keep_ref, got_ref, out_ref):
    out_ref[:, 0:16, :] = in_ref[:, 0:16, :]
    out_ref[:, 16:32, :] = (keep_ref[...] + got_ref[...]).reshape(SEQ, 16, LANES).astype(BF16)
    out_ref[:, 32:40, :] = in_ref[:, 32:40, :]


def proj_kernel(recv_ref, proj_ref, rest_ref):
    for part in range(PARTS):
        for core in range(2):
            total = recv_ref[place(part, core), 16:32, :].astype(F32)
            for high in range(1, 4):
                total = total + recv_ref[place(part, 2 * high + core), 16:32, :].astype(F32)
            proj_ref[16 * part : 16 * part + 16, LANES * core : LANES * core + LANES] = total.astype(BF16)
    rest_ref[:, 0:16, :] = recv_ref[:, 0:16, :]
    rest_ref[:, 16:24, :] = recv_ref[:, 32:40, :]


def finish_kernel(frame_ref, recv_ref, raw_ref, table_ref, act_ref, pre_ref, grad_ref, rows_ref):
    heads = raw_ref.shape[0]
    for pair in range(PAIRS):
        columns = slice(LANES * pair, LANES * pair + LANES)
        for part in range(PARTS):
            act_ref[16 * part : 16 * part + 16, columns] = recv_ref[place(part, pair), 0:16, :]
    lane = lane_iota(8)
    per_frame = jnp.zeros((8, LANES), F32)
    for pair in range(PAIRS):
        rows = recv_ref[place(0, pair), 16:24, :].astype(F32)
        for part in range(1, PARTS):
            rows = rows + recv_ref[place(part, pair), 16:24, :].astype(F32)
        rows_ref[2 * pair : 2 * pair + 2, :] = rows[0:2]
        rows = rows + pltpu.roll(rows, 64, 1)
        for head in range(2):
            inside = (lane < 2 * BLOCKS) & (lane % 2 == head)
            total = jnp.sum(jnp.where(inside, rows, 0.0), axis=1, keepdims=True)
            per_frame = jnp.where(lane == 2 * pair + head, total, per_frame)
    pre = shifted_steps(frame_ref, raw_ref[...], table_ref[...])
    pre_ref[...] = rows_ref[...] * sigmoid(pre)
    per_head = jnp.concatenate([per_frame, jnp.zeros((LANES - 8, LANES), F32)], axis=0).T
    steps = lax.broadcasted_iota(jnp.int32, grad_ref.shape, 1)
    grad = jnp.zeros(grad_ref.shape, F32)
    for frame in range(4):
        grad = grad + jnp.where(steps == frame_ref[frame], per_head[:heads, 2 + frame : 3 + frame], 0.0)
    grad_ref[...] = grad


def total_kernel(own_ref, one_ref, two_ref, three_ref, write_ref, read_ref):
    even = own_ref[...].astype(F32) + two_ref[...].astype(F32)
    odd = one_ref[...].astype(F32) + three_ref[...].astype(F32)
    total = (even + odd).astype(BF16)
    write_ref[...] = total[:, :LANES]
    read_ref[...] = total[:, LANES:]


VMEM = pl.BlockSpec(memory_space=pltpu.VMEM)
SMEM = pl.BlockSpec(memory_space=pltpu.SMEM)


def call(kernel, name, in_specs, out_shape, scratch=(), params=PARAMS):
    shapes = [jax.ShapeDtypeStruct(shape, dtype) for shape, dtype in out_shape]
    return pl.pallas_call(
        kernel,
        out_shape=shapes,
        in_specs=in_specs,
        out_specs=[VMEM] * len(shapes),
        scratch_shapes=list(scratch),
        compiler_params=params,
        name=name,
    )


def shards(
    activations, grad_out, write_proj, read_proj, step_raw, step_table, decay_rate, frame_step, scan_order
):
    raw, table = step_raw.T, step_table.T
    rates = decay_rate.reshape(1, decay_rate.shape[0])
    swap_core = [(i, i ^ 1) for i in range(SEQ)]
    hbm = pl.BlockSpec(memory_space=pltpu.HBM)
    order = scan_order.reshape(1, TOK)
    sources = (order, frame_step, raw, table, write_proj, read_proj, activations, grad_out)
    (send,) = call(
        pack_kernel, "pack", [hbm] * 8, [((SEQ, SLOT_IN, LANES), BF16)],
        [(pltpu.SMEM if a is frame_step else pltpu.VMEM)(a.shape, a.dtype) for a in sources]
        + [pltpu.SemaphoreType.DMA((8,))],
        pltpu.CompilerParams(vmem_limit_bytes=62 * 1024 * 1024),
    )(*sources)
    recv = lax.all_to_all(send, "seq", 0, 0, tiled=True)
    (proj,) = call(cut_kernel, "cut", [VMEM], [((SEQ, 16, LANES), BF16)])(recv)
    swap = lax.ppermute(proj, "seq", swap_core)
    wide = pltpu.VMEM((LOCAL, LANES), F32)
    bundle = ((4 * LOCAL + 4 * TOK, LANES), BF16)
    sums = ((LOCAL, LANES), F32)
    data, mine, weight = call(
        unpack_kernel, "unpack", [VMEM] * 2,
        [((2 * LOCAL + 4 * TOK, LANES), BF16), ((LOCAL, LANES), BF16), ((2 * LOCAL + 16, LANES), BF16)],
        [wide] * 3 + [pltpu.VMEM((SEQ * 8, LANES), F32)],
    )(rates, recv)
    (data,) = call(gather_kernel, "gather", [VMEM] * 3, [bundle], [wide])(mine, swap, data)
    (states,) = call(states_kernel, "states", [VMEM] * 2, [((PARTS, SLOT_STATE, LANES), BF16)])(data, weight)
    states = lax.all_to_all(states, "seq", 0, 0, tiled=True, axis_index_groups=STATE_GROUPS)
    inner, grad = call(
        inner_kernel, "inner", [VMEM] * 2,
        [
            ((2 * LOCAL + 8, LANES), F32),
            ((LOCAL + 3 * TOK, LANES), F32),
        ],
    )(rates, data)
    keep, give, pairs = call(
        outer_kernel, "outer", [VMEM] * 4,
        [sums] * 2 + [((8 * LOCAL + 32, LANES), BF16)],
        [pltpu.VMEM((BLOCKS, LANES, LANES), F32)] + [wide] * 2,
    )(states, inner, data, grad)
    got = lax.ppermute(give, "seq", swap_core)
    (out,) = call(
        grads_kernel, "grads", [VMEM] * 4, [((SEQ, SLOT_OUT, LANES), BF16)],
        [wide, pltpu.VMEM((SEQ * 8, LANES), F32)],
    )(rates, data, pairs, grad)
    (out,) = call(join_kernel, "join", [VMEM] * 3, [((SEQ, SLOT_OUT, LANES), BF16)])(out, keep, got)
    back = lax.all_to_all(out, "seq", 0, 0, tiled=True)
    proj, rest = call(
        proj_kernel, "proj", [VMEM], [((TOK, 2 * LANES), BF16), ((SEQ, 24, LANES), BF16)]
    )(back)
    ring = [lax.ppermute(proj, "head", [(i, (i + k) % 4) for i in range(4)]) for k in (1, 2, 3)]
    act, grad_pre, grad_table = call(
        finish_kernel, "finish", [SMEM] + [VMEM] * 3,
        [(activations.shape, BF16), (raw.shape, F32), (table.shape, F32)],
        [pltpu.VMEM((2 * PAIRS, LANES), F32)],
    )(frame_step, rest, raw, table)
    grad_write, grad_read = call(
        total_kernel, "total", [VMEM] * 4, [(write_proj.shape, BF16), (read_proj.shape, BF16)]
    )(proj, *ring)
    return (act, grad_write, grad_read, grad_pre.T, grad_table.T)


def solution(mesh):
    in_specs = (
        P("seq", "head"),
        P("seq", "head"),
        P("seq", None),
        P("seq", None),
        P("seq", "head"),
        P(None, "head"),
        P("head"),
        P(),
        P("seq"),
    )
    out_specs = (
        P("seq", "head"),
        P("seq", None),
        P("seq", None),
        P("seq", "head"),
        P(None, "head"),
    )
    return jax.shard_map(shards, mesh=mesh, in_specs=in_specs, out_specs=out_specs, check_vma=False)
```

```python
import jax
import jax.numpy as jnp
from jax import lax
from jax.experimental import pallas as pl
from jax.experimental.pallas import tpu as pltpu
from jax.sharding import PartitionSpec as P

F32 = jnp.float32
BF16 = jnp.bfloat16
FRAME_TOK = 2048
TOK = 128
LANES = 128
SEQ = 64
PARTS = 8
PAIRS = 8
BLOCKS = 8
SLOT_IN = 56
SLOT_STATE = 136
SLOT_OUT = 40
LOCAL = BLOCKS * TOK
PARAMS = pltpu.CompilerParams(vmem_limit_bytes=32 * 1024 * 1024)


def place(part, pair):
    y, low = part // 2, part % 2
    high, core = pair // 2, pair % 2
    return y * 16 + (high * 2 + low) * 2 + core


def my_place():
    me = lax.axis_index("seq")
    part = (me // 16) * 2 + (me // 2) % 2
    pair = ((me // 4) % 4) * 2 + me % 2
    return part, pair, me % 2


STATE_GROUPS = [[place(part, pair) for part in range(PARTS)] for pair in range(PAIRS)]


def nn(a, b):
    return lax.dot_general(a, b, (((1,), (0,)), ((), ())), preferred_element_type=F32)


def nt(a, b):
    return lax.dot_general(a, b, (((1,), (1,)), ((), ())), preferred_element_type=F32)


def split(value):
    high = value.astype(BF16)
    return high, (value - high.astype(F32)).astype(BF16)


def lane_iota(rows):
    return lax.broadcasted_iota(jnp.int32, (rows, LANES), 1)


def heads_over_lanes(first, second, rows):
    return jnp.where(lane_iota(rows) < 64, first, second)


def softplus(value):
    return jnp.maximum(value, 0.0) + jnp.log1p(jnp.exp(-jnp.abs(value)))


def sigmoid(value):
    return 1.0 / (1.0 + jnp.exp(-value))


def shifted_steps(frame_ref, raw, table):
    frame_here = lax.axis_index("seq") * TOK // FRAME_TOK
    index = frame_ref[frame_here]
    columns = lax.broadcasted_iota(jnp.int32, table.shape, 1)
    shift = jnp.sum(jnp.where(columns == index, table, 0.0), axis=1, keepdims=True)
    return raw + shift


def pack_kernel(*refs):
    sources, sent_ref, targets, out_ref, sems = refs[:8], refs[8], refs[9:17], refs[17], refs[18]
    copies = [
        pltpu.make_async_copy(source, target, sems.at[i])
        for i, (source, target) in enumerate(zip(sources, targets))
    ]
    for copy in copies:
        copy.start()
    order_ref, frame_ref, raw_ref, table_ref, b_ref, c_ref, x_ref, dy_ref = targets
    copies[0].wait()
    order = jnp.broadcast_to(order_ref[...].astype(F32), (TOK, TOK)).T
    lane = lane_iota(TOK)
    token = ((lane % 64) * 2 + lane // 64).astype(F32)
    steps = lax.broadcasted_iota(jnp.int32, (TOK, TOK), 0).astype(F32)
    position = jnp.sum(jnp.where(order == token, steps, 0.0), axis=0, keepdims=True)
    for copy in copies[1:4]:
        copy.wait()
    pre = shifted_steps(frame_ref, raw_ref[...], table_ref[...])
    delta = softplus(pre).astype(BF16).astype(F32)
    gate = sigmoid(pre)
    gate_high = gate.astype(BF16).astype(F32)
    gate_low = gate - gate_high
    for copy in copies[4:]:
        copy.wait()
    rows = []
    for pair in range(PAIRS):
        own = slice(2 * pair, 2 * pair + 2)
        rows.append(
            jnp.concatenate(
                [position, delta[own], gate_high[own], gate_low[own], jnp.zeros((1, LANES), F32)], axis=0
            ).astype(BF16)
        )
    leaving = []
    for quarter in range(4):
        for part in (2 * quarter, 2 * quarter + 1):
            tokens = slice(16 * part, 16 * part + 16)
            for pair in range(PAIRS):
                proj_ref = c_ref if pair % 2 else b_ref
                columns = slice(LANES * pair, LANES * pair + LANES)
                slot = place(part, pair)
                out_ref[slot, 0:16, :] = x_ref[tokens, columns]
                out_ref[slot, 16:32, :] = dy_ref[tokens, columns]
                out_ref[slot, 32:48, :] = proj_ref[tokens, :]
                out_ref[slot, 48:56, :] = rows[pair]
        slots = pl.ds(16 * quarter, 16)
        leaving.append(pltpu.make_async_copy(out_ref.at[slots], sent_ref.at[slots], sems.at[8 + quarter]))
        leaving[quarter].start()
    for copy in leaving:
        copy.wait()


def to_columns(first, second):
    head_one = jnp.concatenate([first, pltpu.roll(first, LANES - 1, 1)], axis=0)
    head_two = jnp.concatenate([pltpu.roll(second, 1, 1), second], axis=0)
    return jnp.where(lane_iota(TOK) % 2 == 0, head_one, head_two)


def slope_lanes(decay_ref, pair, rows):
    rates = decay_ref[...]
    lane = lax.broadcasted_iota(jnp.int32, rates.shape, 1)
    first = jnp.sum(jnp.where(lane == 2 * pair, rates, 0.0), axis=1, keepdims=True)
    second = jnp.sum(jnp.where(lane == 2 * pair + 1, rates, 0.0), axis=1, keepdims=True)
    return jnp.where(lane_iota(rows) % 2 == 0, -first, -second)


def block_lanes(columns, block, rows):
    j = 2 * block
    return heads_over_lanes(columns[:, j : j + 1], columns[:, j + 1 : j + 2], rows)


def block_rows(block):
    return slice(block * TOK, block * TOK + TOK)


def stack(value):
    return jnp.concatenate(split(value), axis=0)


def twice(value):
    return jnp.concatenate([value, value], axis=1)


def turned(value):
    return value.astype(F32).T.astype(BF16)


def twice_split(value):
    return jnp.concatenate(split(value), axis=1)


def spread(value, wide, target_ref, base):
    wide[...] = value.reshape(SEQ * 16, LANES)
    for row in range(16):
        start = base + row * 64
        target_ref[start : start + 64, :] = wide[pl.ds(row, 64, stride=16), :].astype(BF16)


def cut_kernel(recv_ref, proj_ref):
    proj_ref[...] = recv_ref[:, 32:48, :]


def unpack_kernel(
    decay_ref, recv_ref, data_ref, proj_ref, weight_ref, wide, wide_two, wide_three, misc
):
    part, pair, core = my_place()
    spread(recv_ref[:, 0:16, :].astype(F32), wide, data_ref, 0)
    spread(recv_ref[:, 16:32, :].astype(F32), wide_two, data_ref, LOCAL)
    spread(recv_ref[:, 32:48, :].astype(F32), wide_three, proj_ref, 0)
    misc[...] = recv_ref[:, 48:56, :].astype(F32).reshape(SEQ * 8, LANES)
    shift = (LANES - 16 * part) % LANES

    def own_lanes(row):
        return pltpu.roll(misc[pl.ds(row, 64, stride=8), :], shift, 1)

    steps = to_columns(own_lanes(1), own_lanes(2))
    gates_high = to_columns(own_lanes(3), own_lanes(4))
    gates_low = to_columns(own_lanes(5), own_lanes(6))
    pos_rows = jnp.concatenate(
        [misc[pl.ds(part * 64 + 8 * block, 1), :] for block in range(BLOCKS)], axis=0
    )
    pos_cols = jnp.concatenate([pos_rows, jnp.zeros((LANES - BLOCKS, LANES), F32)], axis=0).T
    lane = lane_iota(TOK)
    steps_bf = steps.astype(BF16)
    sums = jnp.zeros((TOK, LANES), F32)
    for block in range(BLOCKS):
        later = (pos_cols[:, block : block + 1] >= pos_rows[block : block + 1, :]).astype(F32).astype(BF16)
        sums = jnp.where(lane // 2 == block, nn(later, steps_bf), sums)
    slopes = slope_lanes(decay_ref, pair, TOK)
    logs = sums * slopes
    totals = jnp.sum(steps, axis=0, keepdims=True) * slopes[:1]
    short = jnp.where(lane_iota(1) < 2 * BLOCKS, totals, 0.0)
    onward = short
    until = pltpu.roll(short, 2, 1)
    for reach in (2, 4, 8):
        onward = onward + pltpu.roll(onward, LANES - reach, 1)
        until = until + pltpu.roll(until, reach, 1)
    base = 2 * LOCAL
    data_ref[base : base + TOK, :] = steps_bf
    data_ref[base + TOK : base + 2 * TOK, :] = gates_high.astype(BF16)
    data_ref[base + 2 * TOK : base + 3 * TOK, :] = gates_low.astype(BF16)
    data_ref[base + 3 * TOK : base + 4 * TOK, :] = pos_cols.astype(BF16)
    whole = heads_over_lanes(onward[:, 0:1], onward[:, 1:2], 1)
    top = whole.astype(BF16).astype(F32)
    middle = (whole - top).astype(BF16).astype(F32)
    bottom = whole - top - middle
    tail = jnp.concatenate([top, middle, bottom, jnp.zeros((13, LANES), F32)], axis=0).astype(BF16)
    weight_ref[2 * LOCAL : 2 * LOCAL + 16, :] = tail
    weights = steps * jnp.exp(jnp.minimum(onward - logs, 0.0))
    starts = jnp.exp(jnp.minimum(logs + until, 0.0))
    for block in range(BLOCKS):
        rows = block_rows(block)
        later_rows = slice(LOCAL + block * TOK, LOCAL + block * TOK + TOK)
        weight_ref[rows, :] = (
            data_ref[rows, :].astype(F32) * block_lanes(weights, block, TOK)
        ).astype(BF16)
        weight_ref[later_rows, :] = (
            data_ref[later_rows, :].astype(F32) * block_lanes(starts, block, TOK)
        ).astype(BF16)


def gather_kernel(mine_ref, swap_ref, data_ref, all_ref, wide):
    part, pair, core = my_place()
    all_ref[0 : 2 * LOCAL, :] = data_ref[0 : 2 * LOCAL, :]
    all_ref[4 * LOCAL : 4 * LOCAL + 4 * TOK, :] = data_ref[2 * LOCAL : 2 * LOCAL + 4 * TOK, :]

    @pl.when(core == 0)
    def _():
        all_ref[2 * LOCAL : 3 * LOCAL, :] = mine_ref[...]
        spread(swap_ref[...].astype(F32), wide, all_ref, 3 * LOCAL)

    @pl.when(core == 1)
    def _():
        all_ref[3 * LOCAL : 4 * LOCAL, :] = mine_ref[...]
        spread(swap_ref[...].astype(F32), wide, all_ref, 2 * LOCAL)


def states_kernel(all_ref, weight_ref, send_ref):
    part, pair, core = my_place()
    state = jnp.zeros((LANES, LANES), F32)
    adjoint = jnp.zeros((LANES, LANES), F32)
    for block in range(0, BLOCKS, 2):
        rows = slice(block * TOK, block * TOK + 2 * TOK)
        later_rows = slice(LOCAL + block * TOK, LOCAL + block * TOK + 2 * TOK)
        write = all_ref[2 * LOCAL + block * TOK : 2 * LOCAL + block * TOK + 2 * TOK, :]
        read = all_ref[3 * LOCAL + block * TOK : 3 * LOCAL + block * TOK + 2 * TOK, :]
        state = state + nn(turned(write), weight_ref[rows, :])
        adjoint = adjoint + nn(turned(read), weight_ref[later_rows, :])
    state = state.astype(BF16)
    adjoint = adjoint.astype(BF16)
    for slot in range(PARTS):
        after = slot > part

        @pl.when(after)
        def _():
            send_ref[slot, 0:128, :] = state

        @pl.when(jnp.logical_not(after))
        def _():
            send_ref[slot, 0:128, :] = adjoint

        send_ref[slot, 128:136, :] = weight_ref[2 * LOCAL : 2 * LOCAL + 16, :][:8]


def inner_kernel(decay_ref, all_ref, sums_ref, grad_ref):
    part, pair, core = my_place()
    base = 4 * LOCAL
    steps_bf = all_ref[base : base + TOK, :]
    steps = steps_bf.astype(F32)
    pos_cols = all_ref[base + 3 * TOK : base + 4 * TOK, :].astype(F32)
    pos_rows = pos_cols.T[:8]
    grad_ref[LOCAL + 2 * TOK : LOCAL + 3 * TOK, :] = jnp.zeros((TOK, LANES), F32)
    lane = lane_iota(TOK)
    sums = jnp.zeros((TOK, LANES), F32)
    masks = []
    for block in range(BLOCKS):
        behind = pos_cols[:, block : block + 1] >= pos_rows[block : block + 1, :]
        masks.append(behind.astype(F32).astype(BF16))
        sums = jnp.where(lane // 2 == block, nn(masks[block], steps_bf), sums)
    slopes = slope_lanes(decay_ref, pair, TOK)
    logs = sums * slopes
    log_rows = logs.T
    totals = jnp.sum(steps, axis=0, keepdims=True) * slopes[:1]
    starts = jnp.exp(logs)
    ends = steps * jnp.exp(totals - logs)
    grad_ref[LOCAL : LOCAL + TOK, :] = ends
    grad_ref[LOCAL + TOK : LOCAL + 2 * TOK, :] = starts
    for block in range(BLOCKS):
        rows = block_rows(block)

        def piece(number):
            return all_ref[number * LOCAL + block * TOK : number * LOCAL + block * TOK + TOK, :]

        def sums_rows(number):
            return slice(number * LOCAL + block * TOK, number * LOCAL + block * TOK + TOK)

        x, dy, write, read = piece(0), piece(1), piece(2), piece(3)
        sums_ref[2 * LOCAL + block : 2 * LOCAL + block + 1, :] = block_lanes(totals, block, 1)
        ahead = pos_rows[block : block + 1, :] >= pos_cols[:, block : block + 1]
        behind = masks[block]
        cross = nt(write, read)
        zero = jnp.zeros_like(dy)
        x_heads = (jnp.where(lane < 64, x, zero), jnp.where(lane < 64, zero, x))
        dy_stack = jnp.concatenate(
            [jnp.where(lane < 64, dy, zero), jnp.where(lane < 64, zero, dy)], axis=0
        )
        carry, mixed, seen = [], [], []
        for head in range(2):
            j = 2 * block + head
            gap = log_rows[j : j + 1, :] - logs[:, j : j + 1]
            decay = jnp.exp(jnp.where(ahead, gap, -1e30))
            carry.append(decay * cross)
            mixed.append(decay * (nt(x_heads[head], dy) * steps[:, j : j + 1]))
            seen.append(twice_split(mixed[head] * cross))
        crossed = nn(jnp.concatenate(seen, axis=0), jnp.concatenate([behind, behind], axis=0))
        for head in range(2):
            j = LOCAL + 2 * TOK + 2 * block + head
            own = jnp.where(ahead, crossed[head * TOK : head * TOK + TOK], 0.0)
            grad_ref[j : j + 1, :] = jnp.sum(own, axis=0, keepdims=True)
        high, low = split(jnp.concatenate(carry, axis=1))
        grad_ref[rows, :] = block_lanes(steps, block, TOK) * (nn(high, dy_stack) + nn(low, dy_stack))
        both = mixed[0] + mixed[1]
        sums_ref[sums_rows(0), :] = nn(twice_split(both), jnp.concatenate([read, read], axis=0))
        sums_ref[sums_rows(1), :] = nn(twice_split(both.T), jnp.concatenate([write, write], axis=0))


def outer_kernel(recv_ref, sums_ref, data_ref, grad_ref, keep_ref, give_ref, all_ref, adj):
    part, pair, core = my_place()

    totals = []
    for slot in range(PARTS):
        tail = recv_ref[slot, 128:136, :].astype(F32)
        totals.append(tail[0:1] + tail[1:2] + tail[2:3])
    zero = jnp.zeros((1, LANES), F32)
    state = jnp.zeros((LANES, LANES), F32)
    adjoint = jnp.zeros((LANES, LANES), F32)
    after, before = zero, zero
    weights = [None] * PARTS
    for slot in reversed(range(PARTS)):
        weights[slot] = jnp.where(slot < part, jnp.exp(after), zero)
        after = after + jnp.where(slot < part, totals[slot], zero)
    for slot in range(PARTS):
        weight = jnp.where(slot > part, jnp.exp(before), zero)
        before = before + jnp.where(slot > part, totals[slot], zero)
        sent = recv_ref[slot, 0:128, :].astype(F32)
        state = state + weights[slot] * sent
        adjoint = adjoint + weight * sent
    keeps = jnp.exp(sums_ref[2 * LOCAL : 2 * LOCAL + 8, :])

    def sums_rows(number, block):
        return slice(number * LOCAL + block * TOK, number * LOCAL + block * TOK + TOK)

    ends = grad_ref[LOCAL : LOCAL + TOK, :]
    starts = grad_ref[LOCAL + TOK : LOCAL + 2 * TOK, :]

    def data_rows(number, block):
        return slice(number * LOCAL + block * TOK, number * LOCAL + block * TOK + TOK)

    gains, ds, xe = [], [], []
    for block in range(BLOCKS):
        xe.append(split(data_ref[data_rows(0, block), :].astype(F32) * block_lanes(ends, block, TOK)))
        ds.append(split(data_ref[data_rows(1, block), :].astype(F32) * block_lanes(starts, block, TOK)))
        write = twice(turned(data_ref[data_rows(2, block), :]))
        read = twice(turned(data_ref[data_rows(3, block), :]))
        gains.append((nn(write, jnp.concatenate(xe[block], axis=0)), nn(read, jnp.concatenate(ds[block], axis=0))))
    for block in reversed(range(BLOCKS)):
        adj[block] = adjoint
        adjoint = adjoint * keeps[block : block + 1] + gains[block][1]
    overlaps = []
    for block in range(BLOCKS):
        adjoint = adj[block]
        state_high, state_low = split(state)
        adj_high, adj_low = split(adjoint)
        first = block * 2 * TOK
        all_ref[4 * LOCAL + first : 4 * LOCAL + first + TOK, :] = state_high
        all_ref[4 * LOCAL + first + TOK : 4 * LOCAL + first + 2 * TOK, :] = state_low
        all_ref[6 * LOCAL + first : 6 * LOCAL + first + TOK, :] = adj_high
        all_ref[6 * LOCAL + first + TOK : 6 * LOCAL + first + 2 * TOK, :] = adj_low
        keep = keeps[block : block + 1]
        overlaps.append(jnp.sum(adjoint * state, axis=0, keepdims=True) * keep)
        ds_high, ds_low = ds[block]
        xe_high, xe_low = xe[block]
        all_ref[first : first + TOK, :] = ds_high
        all_ref[first + TOK : first + 2 * TOK, :] = ds_low
        all_ref[2 * LOCAL + first : 2 * LOCAL + first + TOK, :] = xe_high
        all_ref[2 * LOCAL + first + TOK : 2 * LOCAL + first + 2 * TOK, :] = xe_low
        gr = sums_ref[sums_rows(1, block), :] + (
            nt(jnp.concatenate([ds_high, ds_low], axis=1), twice(state_high)) + nt(ds_high, state_low)
        )
        gw = sums_ref[sums_rows(0, block), :] + (
            nt(jnp.concatenate([xe_high, xe_low], axis=1), twice(adj_high)) + nt(xe_high, adj_low)
        )
        kept = jnp.where(core == 0, gw, gr)
        given = jnp.where(core == 0, gr, gw)
        for half in range(2):
            out_rows = pl.ds(2 * block + half, 64, stride=16)
            own_rows = slice(64 * half, 64 * half + 64)
            keep_ref[out_rows, :] = kept[own_rows]
            give_ref[out_rows, :] = given[own_rows]
        state = state * keep + gains[block][0]
    overlaps = jnp.concatenate(overlaps, axis=0)
    top = overlaps.astype(BF16).astype(F32)
    middle = (overlaps - top).astype(BF16).astype(F32)
    bottom = overlaps - top - middle
    all_ref[8 * LOCAL : 8 * LOCAL + 32, :] = jnp.concatenate(
        [top, middle, bottom, jnp.zeros((8, LANES), F32)], axis=0
    ).astype(BF16)


def grads_kernel(decay_ref, data_ref, all_ref, grad_ref, out_ref, wide, misc):
    part, pair, core = my_place()
    slopes = slope_lanes(decay_ref, pair, TOK)
    base = 4 * LOCAL
    steps = data_ref[base : base + TOK, :].astype(F32)
    gates = data_ref[base + TOK : base + 2 * TOK, :].astype(F32) + data_ref[base + 2 * TOK : base + 3 * TOK, :].astype(F32)
    pos_cols = data_ref[base + 3 * TOK : base + 4 * TOK, :].astype(F32)
    pos_rows = pos_cols.T[:8]
    ends = grad_ref[LOCAL : LOCAL + TOK, :]
    lane = lane_iota(TOK)
    tail = all_ref[8 * LOCAL : 8 * LOCAL + 32, :].astype(F32)
    overlaps = tail[0:8] + tail[8:16] + tail[16:24]
    row_lane = lane_iota(8)
    row = lax.broadcasted_iota(jnp.int32, (8, LANES), 0)
    first = jnp.sum(jnp.where(row_lane < 64, overlaps, 0.0), axis=1, keepdims=True)
    second = jnp.sum(jnp.where(row_lane < 64, 0.0, overlaps), axis=1, keepdims=True)
    kept = jnp.where(row_lane == 2 * row, first, jnp.where(row_lane == 2 * row + 1, second, 0.0))
    sub = lax.broadcasted_iota(jnp.int32, (2 * LANES, LANES), 0) % LANES // 64
    pick_lane = lax.broadcasted_iota(jnp.int32, (2 * LANES, LANES), 1)
    per_head = jnp.zeros((3 * TOK, LANES), F32)
    for block in range(BLOCKS):
        rows = block_rows(block)
        lo = block * 2 * TOK

        def both(number):
            start = number * LOCAL + lo
            return all_ref[start : start + TOK, :].astype(F32) + all_ref[start + TOK : start + 2 * TOK, :].astype(F32)

        x = data_ref[rows, :].astype(F32)
        write = data_ref[2 * LOCAL + block * TOK : 2 * LOCAL + block * TOK + TOK, :]
        read = data_ref[3 * LOCAL + block * TOK : 3 * LOCAL + block * TOK + TOK, :]
        carried = nn(twice(write), all_ref[6 * LOCAL + lo : 6 * LOCAL + lo + 2 * TOK, :])
        recalled = nn(twice(read), all_ref[4 * LOCAL + lo : 4 * LOCAL + lo + 2 * TOK, :])
        act = grad_ref[rows, :] + block_lanes(ends, block, TOK) * carried
        wide[pl.ds(2 * block, 64, stride=16), :] = act[:64]
        wide[pl.ds(2 * block + 1, 64, stride=16), :] = act[64:]
        products = jnp.concatenate([both(0) * recalled, both(2) * carried, x * act], axis=0)
        pick = (pick_lane == 2 * block + sub).astype(F32).astype(BF16)
        per_head = per_head + nn(twice_split(products), pick)

    direct = per_head[2 * TOK :]
    read_high, read_low = split(per_head[:TOK].T[: 2 * BLOCKS])
    write_part = per_head[TOK : 2 * TOK].T[: 2 * BLOCKS]
    write_high, write_low = split(write_part)
    vectors = jnp.concatenate([read_high, read_low, write_high, write_low], axis=0)
    log_rows = grad_ref[LOCAL + 2 * TOK : LOCAL + 2 * TOK + 2 * BLOCKS, :]
    log_rows = log_rows + write_part + jnp.sum(write_part, axis=1, keepdims=True)
    owner = lax.broadcasted_iota(jnp.int32, (2 * BLOCKS, LANES), 0) // 2
    for block in range(BLOCKS):
        behind = (pos_cols[:, block : block + 1] >= pos_rows[block : block + 1, :]).astype(F32).astype(BF16)
        sums = nn(vectors, behind)
        added = (sums[0:16] + sums[16:32]) - (sums[32:48] + sums[48:64])
        log_rows = log_rows + jnp.where(owner == block, added, 0.0)
    log_grad = jnp.concatenate([log_rows, jnp.zeros((TOK - 2 * BLOCKS, LANES), F32)], axis=0).T
    log_grad = log_grad + jnp.sum(kept, axis=0, keepdims=True)
    grad_step = direct / steps + slopes * (log_grad - direct)
    grad_step = jnp.where(lane < 2 * BLOCKS, grad_step, 0.0).astype(BF16).astype(F32)
    grad_pre = grad_step * gates
    frames = []
    for frame in range(4):
        low_rows = slice(16 * frame, 16 * frame + 16)
        high_rows = slice(64 + 16 * frame, 80 + 16 * frame)
        frames.append(jnp.sum(grad_pre[low_rows] + grad_pre[high_rows], axis=0, keepdims=True))
    frames = sum(pltpu.roll(jnp.where(lane_iota(1) < 16, row, 0.0), 16 * i, 1) for i, row in enumerate(frames))
    frames_high = frames.astype(BF16).astype(F32)
    frames = frames_high + pltpu.roll(frames - frames_high, 64, 1)

    even = lane_iota(64) % 2 == 0
    top, bottom = grad_step[:64], grad_step[64:]
    shift = 16 * part
    row_one = pltpu.roll(jnp.where(even, top, pltpu.roll(bottom, 1, 1)), shift, 1)
    row_two = pltpu.roll(jnp.where(even, pltpu.roll(top, LANES - 1, 1), bottom), shift, 1)
    misc[...] = jnp.zeros((SEQ * 8, LANES), F32)
    misc[pl.ds(0, 64, stride=8), :] = row_one
    misc[pl.ds(1, 64, stride=8), :] = row_two
    misc[pl.ds(2, 64, stride=8), :] = jnp.broadcast_to(frames, (SEQ, LANES))
    out_ref[:, 0:16, :] = wide[...].reshape(SEQ, 16, LANES).astype(BF16)
    out_ref[:, 16:32, :] = jnp.zeros((SEQ, 16, LANES), BF16)
    out_ref[:, 32:40, :] = misc[...].reshape(SEQ, 8, LANES).astype(BF16)


def join_kernel(in_ref, keep_ref, got_ref, out_ref):
    out_ref[:, 0:4] = in_ref[:, 0:16, :].reshape(SEQ, 4, 4, LANES)
    proj = (keep_ref[...] + got_ref[...]).reshape(SEQ, 16, LANES).astype(BF16)
    out_ref[:, 4:8] = proj.reshape(SEQ, 4, 4, LANES)
    out_ref[:, 8:9] = in_ref[:, 32:40, :].reshape(SEQ, 2, 4, LANES)[:, 0:1]


def proj_kernel(recv_ref, proj_ref, rest_ref):
    for part in range(PARTS):
        for core in range(2):
            total = recv_ref[place(part, core), 4:8].reshape(16, LANES).astype(F32)
            for high in range(1, 4):
                total = total + recv_ref[place(part, 2 * high + core), 4:8].reshape(16, LANES).astype(F32)
            proj_ref[16 * part : 16 * part + 16, LANES * core : LANES * core + LANES] = total.astype(BF16)
    rest_ref[:, 0:4] = recv_ref[:, 0:4]
    rest_ref[:, 4:5] = recv_ref[:, 8:9]


def finish_kernel(frame_ref, recv_ref, raw_ref, table_ref, act_ref, pre_ref, grad_ref, rows_ref):
    heads = raw_ref.shape[0]
    for pair in range(PAIRS):
        columns = slice(LANES * pair, LANES * pair + LANES)
        for part in range(PARTS):
            act_ref[16 * part : 16 * part + 16, columns] = recv_ref[place(part, pair), 0:4].reshape(16, LANES)
    lane = lane_iota(8)
    row = lax.broadcasted_iota(jnp.int32, (8, LANES), 0)
    sums = []
    for pair in range(PAIRS):
        rows = recv_ref[place(0, pair), 4:5].reshape(4, LANES).astype(F32)
        for part in range(1, PARTS):
            rows = rows + recv_ref[place(part, pair), 4:5].reshape(4, LANES).astype(F32)
        rows_ref[2 * pair : 2 * pair + 2, :] = rows[0:2]
        sums.append(rows[2:3])
    sums = jnp.concatenate(sums, axis=0)
    sums = sums + pltpu.roll(sums, 64, 1)
    per_frame = []
    for frame in range(4):
        total = jnp.zeros((8, LANES), F32)
        for head in range(2):
            inside = (lane // 16 == frame) & (lane % 2 == head)
            part_sum = jnp.sum(jnp.where(inside, sums, 0.0), axis=1, keepdims=True)
            total = jnp.where(lane == 2 * row + head, part_sum, total)
        per_frame.append(jnp.sum(total, axis=0, keepdims=True))
    pre = shifted_steps(frame_ref, raw_ref[...], table_ref[...])
    pre_ref[...] = rows_ref[...] * sigmoid(pre)
    per_head = jnp.concatenate(per_frame + [jnp.zeros((LANES - 4, LANES), F32)], axis=0).T
    steps = lax.broadcasted_iota(jnp.int32, grad_ref.shape, 1)
    grad = jnp.zeros(grad_ref.shape, F32)
    for frame in range(4):
        grad = grad + jnp.where(steps == frame_ref[frame], per_head[:heads, frame : frame + 1], 0.0)
    grad_ref[...] = grad


def total_kernel(own_ref, one_ref, two_ref, three_ref, write_ref, read_ref):
    even = own_ref[...].astype(F32) + two_ref[...].astype(F32)
    odd = one_ref[...].astype(F32) + three_ref[...].astype(F32)
    total = (even + odd).astype(BF16)
    write_ref[...] = total[:, :LANES]
    read_ref[...] = total[:, LANES:]


VMEM = pl.BlockSpec(memory_space=pltpu.VMEM)
SMEM = pl.BlockSpec(memory_space=pltpu.SMEM)


def call(kernel, name, in_specs, out_shape, scratch=(), params=PARAMS, out=VMEM):
    shapes = [jax.ShapeDtypeStruct(shape, dtype) for shape, dtype in out_shape]
    return pl.pallas_call(
        kernel,
        out_shape=shapes,
        in_specs=in_specs,
        out_specs=[out] * len(shapes),
        scratch_shapes=list(scratch),
        compiler_params=params,
        name=name,
    )


def shards(
    activations, grad_out, write_proj, read_proj, step_raw, step_table, decay_rate, frame_step, scan_order
):
    raw, table = step_raw.T, step_table.T
    rates = decay_rate.reshape(1, decay_rate.shape[0])
    swap_core = [(i, i ^ 1) for i in range(SEQ)]
    hbm = pl.BlockSpec(memory_space=pltpu.HBM)
    order = scan_order.reshape(1, TOK)
    sources = (order, frame_step, raw, table, write_proj, read_proj, activations, grad_out)
    (send,) = call(
        pack_kernel, "pack", [hbm] * 8, [((SEQ, SLOT_IN, LANES), BF16)],
        [(pltpu.SMEM if a is frame_step else pltpu.VMEM)(a.shape, a.dtype) for a in sources]
        + [pltpu.VMEM((SEQ, SLOT_IN, LANES), BF16), pltpu.SemaphoreType.DMA((12,))],
        pltpu.CompilerParams(vmem_limit_bytes=62 * 1024 * 1024), hbm,
    )(*sources)
    recv = lax.all_to_all(send, "seq", 0, 0, tiled=True)
    (proj,) = call(cut_kernel, "cut", [VMEM], [((SEQ, 16, LANES), BF16)])(recv)
    swap = lax.ppermute(proj, "seq", swap_core)
    wide = pltpu.VMEM((LOCAL, LANES), F32)
    bundle = ((4 * LOCAL + 4 * TOK, LANES), BF16)
    sums = ((LOCAL, LANES), F32)
    data, mine, weight = call(
        unpack_kernel, "unpack", [VMEM] * 2,
        [((2 * LOCAL + 4 * TOK, LANES), BF16), ((LOCAL, LANES), BF16), ((2 * LOCAL + 16, LANES), BF16)],
        [wide] * 3 + [pltpu.VMEM((SEQ * 8, LANES), F32)],
    )(rates, recv)
    (data,) = call(gather_kernel, "gather", [VMEM] * 3, [bundle], [wide])(mine, swap, data)
    (states,) = call(states_kernel, "states", [VMEM] * 2, [((PARTS, SLOT_STATE, LANES), BF16)])(data, weight)
    states = lax.all_to_all(states, "seq", 0, 0, tiled=True, axis_index_groups=STATE_GROUPS)
    inner, grad = call(
        inner_kernel, "inner", [VMEM] * 2,
        [
            ((2 * LOCAL + 8, LANES), F32),
            ((LOCAL + 3 * TOK, LANES), F32),
        ],
    )(rates, data)
    keep, give, pairs = call(
        outer_kernel, "outer", [VMEM] * 4,
        [sums] * 2 + [((8 * LOCAL + 32, LANES), BF16)],
        [pltpu.VMEM((BLOCKS, LANES, LANES), F32)],
    )(states, inner, data, grad)
    got = lax.ppermute(give, "seq", swap_core)
    (out,) = call(
        grads_kernel, "grads", [VMEM] * 4, [((SEQ, SLOT_OUT, LANES), BF16)],
        [wide, pltpu.VMEM((SEQ * 8, LANES), F32)],
    )(rates, data, pairs, grad)
    (out,) = call(join_kernel, "join", [VMEM] * 3, [((SEQ, 9, 4, LANES), BF16)])(out, keep, got)
    back = lax.all_to_all(out, "seq", 0, 0, tiled=True)
    proj, rest = call(
        proj_kernel, "proj", [VMEM], [((TOK, 2 * LANES), BF16), ((SEQ, 5, 4, LANES), BF16)]
    )(back)
    ring = [lax.ppermute(proj, "head", [(i, (i + k) % 4) for i in range(4)]) for k in (1, 2, 3)]
    act, grad_pre, grad_table = call(
        finish_kernel, "finish", [SMEM] + [VMEM] * 3,
        [(activations.shape, BF16), (raw.shape, F32), (table.shape, F32)],
        [pltpu.VMEM((2 * PAIRS, LANES), F32)],
    )(frame_step, rest, raw, table)
    grad_write, grad_read = call(
        total_kernel, "total", [VMEM] * 4, [(write_proj.shape, BF16), (read_proj.shape, BF16)]
    )(proj, *ring)
    return (act, grad_write, grad_read, grad_pre.T, grad_table.T)


def solution(mesh):
    in_specs = (
        P("seq", "head"),
        P("seq", "head"),
        P("seq", None),
        P("seq", None),
        P("seq", "head"),
        P(None, "head"),
        P("head"),
        P(),
        P("seq"),
    )
    out_specs = (
        P("seq", "head"),
        P("seq", None),
        P("seq", None),
        P("seq", "head"),
        P(None, "head"),
    )
    return jax.shard_map(shards, mesh=mesh, in_specs=in_specs, out_specs=out_specs, check_vma=False)
```

```python
import jax
import jax.numpy as jnp
from jax import lax
from jax.experimental import pallas as pl
from jax.experimental.pallas import tpu as pltpu
from jax.sharding import PartitionSpec as P

F32 = jnp.float32
BF16 = jnp.bfloat16
FRAME_TOK = 2048
TOK = 128
LANES = 128
SEQ = 64
PARTS = 8
PAIRS = 8
BLOCKS = 8
SLOT_STATE = 136
SLOT_OUT = 40
LOCAL = BLOCKS * TOK
PARAMS = pltpu.CompilerParams(vmem_limit_bytes=32 * 1024 * 1024)


def place(part, pair):
    y, low = part // 2, part % 2
    high, core = pair // 2, pair % 2
    return y * 16 + (high * 2 + low) * 2 + core


def my_place():
    me = lax.axis_index("seq")
    part = (me // 16) * 2 + (me // 2) % 2
    pair = ((me // 4) % 4) * 2 + me % 2
    return part, pair, me % 2


STATE_GROUPS = [[place(part, pair) for part in range(PARTS)] for pair in range(PAIRS)]


def nn(a, b):
    return lax.dot_general(a, b, (((1,), (0,)), ((), ())), preferred_element_type=F32)


def nt(a, b):
    return lax.dot_general(a, b, (((1,), (1,)), ((), ())), preferred_element_type=F32)


def split(value):
    high = value.astype(BF16)
    return high, (value - high.astype(F32)).astype(BF16)


def lane_iota(rows):
    return lax.broadcasted_iota(jnp.int32, (rows, LANES), 1)


def heads_over_lanes(first, second, rows):
    return jnp.where(lane_iota(rows) < 64, first, second)


def softplus(value):
    return jnp.maximum(value, 0.0) + jnp.log1p(jnp.exp(-jnp.abs(value)))


def sigmoid(value):
    return 1.0 / (1.0 + jnp.exp(-value))


def shifted_steps(frame_ref, raw, table):
    frame_here = lax.axis_index("seq") * TOK // FRAME_TOK
    index = frame_ref[frame_here]
    columns = lax.broadcasted_iota(jnp.int32, table.shape, 1)
    shift = jnp.sum(jnp.where(columns == index, table, 0.0), axis=1, keepdims=True)
    return raw + shift


def pack_kernel(*refs):
    sources, sent_ref, targets, out_ref, misc, sems = refs[:8], refs[8], refs[9:17], refs[17], refs[18], refs[19]
    copies = [
        pltpu.make_async_copy(source, target, sems.at[i])
        for i, (source, target) in enumerate(zip(sources, targets))
    ]
    for copy in copies:
        copy.start()
    order_ref, frame_ref, raw_ref, table_ref, b_ref, c_ref, x_ref, dy_ref = targets
    copies[0].wait()
    order = jnp.broadcast_to(order_ref[...].astype(F32), (TOK, TOK)).T
    lane = lane_iota(TOK)
    token = ((lane % 64) * 2 + lane // 64).astype(F32)
    steps = lax.broadcasted_iota(jnp.int32, (TOK, TOK), 0).astype(F32)
    position = jnp.sum(jnp.where(order == token, steps, 0.0), axis=0, keepdims=True)
    for copy in copies[1:4]:
        copy.wait()
    pre = shifted_steps(frame_ref, raw_ref[...], table_ref[...])
    delta = softplus(pre).astype(BF16).astype(F32)
    gate = sigmoid(pre)
    gate_high = gate.astype(BF16).astype(F32)
    gate_low = gate - gate_high
    for copy in copies[4:]:
        copy.wait()
    row = lax.broadcasted_iota(jnp.int32, pre.shape, 0) % 2
    group = lax.broadcasted_iota(jnp.int32, pre.shape, 1) // 16
    turns = []
    for kind, value in enumerate((delta, gate_high, gate_low)):
        first = pltpu.roll(value, 32 * kind, 1) if kind else value
        turns.append(jnp.where(row == 0, first, pltpu.roll(value, 32 * kind + 16, 1)))
    misc[...] = jnp.zeros((SEQ * 4, LANES), F32)
    misc[pl.ds(0, SEQ, stride=4), :] = jnp.broadcast_to(position, (SEQ, LANES))
    for part in range(PARTS):
        mixed = jnp.zeros(pre.shape, F32)
        for kind in range(3):
            mixed = mixed + jnp.where(group == (part + 2 * kind + row) % 8, turns[kind], 0.0)
        mixed = mixed + pltpu.roll(mixed, mixed.shape[0] - 1, 0)
        for pair in range(PAIRS):
            spot = 4 * place(part, pair) + 1
            misc[spot : spot + 1, :] = mixed[2 * pair : 2 * pair + 1]
    out_ref[:, 12:13] = misc[...].astype(BF16).reshape(SEQ, 1, 4, LANES)
    leaving = []
    for quarter in range(4):
        for part in (2 * quarter, 2 * quarter + 1):
            tokens = slice(16 * part, 16 * part + 16)
            for pair in range(PAIRS):
                proj_ref = c_ref if pair % 2 else b_ref
                columns = slice(LANES * pair, LANES * pair + LANES)
                slot = place(part, pair)
                out_ref[slot, 0:4] = x_ref[tokens, columns].reshape(4, 4, LANES)
                out_ref[slot, 4:8] = dy_ref[tokens, columns].reshape(4, 4, LANES)
                out_ref[slot, 8:12] = proj_ref[tokens, :].reshape(4, 4, LANES)
        slots = pl.ds(16 * quarter, 16)
        leaving.append(pltpu.make_async_copy(out_ref.at[slots], sent_ref.at[slots], sems.at[8 + quarter]))
        leaving[quarter].start()
    for copy in leaving:
        copy.wait()


def to_columns(first, second):
    head_one = jnp.concatenate([first, pltpu.roll(first, LANES - 1, 1)], axis=0)
    head_two = jnp.concatenate([pltpu.roll(second, 1, 1), second], axis=0)
    return jnp.where(lane_iota(TOK) % 2 == 0, head_one, head_two)


def slope_lanes(decay_ref, pair, rows):
    rates = decay_ref[...]
    lane = lax.broadcasted_iota(jnp.int32, rates.shape, 1)
    first = jnp.sum(jnp.where(lane == 2 * pair, rates, 0.0), axis=1, keepdims=True)
    second = jnp.sum(jnp.where(lane == 2 * pair + 1, rates, 0.0), axis=1, keepdims=True)
    return jnp.where(lane_iota(rows) % 2 == 0, -first, -second)


def block_lanes(columns, block, rows):
    j = 2 * block
    return heads_over_lanes(columns[:, j : j + 1], columns[:, j + 1 : j + 2], rows)


def block_rows(block):
    return slice(block * TOK, block * TOK + TOK)


def stack(value):
    return jnp.concatenate(split(value), axis=0)


def twice(value):
    return jnp.concatenate([value, value], axis=1)


def turned(value):
    return value.astype(F32).T.astype(BF16)


def twice_split(value):
    return jnp.concatenate(split(value), axis=1)


def spread(value, wide, target_ref, base):
    wide[...] = value.reshape(SEQ * 16, LANES)
    for row in range(16):
        start = base + row * 64
        target_ref[start : start + 64, :] = wide[pl.ds(row, 64, stride=16), :].astype(BF16)


def cut_kernel(recv_ref, proj_ref):
    proj_ref[...] = recv_ref[:, 8:12]


def unpack_kernel(
    decay_ref, recv_ref, data_ref, proj_ref, weight_ref, wide, wide_two, wide_three, misc
):
    part, pair, core = my_place()
    misc[...] = recv_ref[:, 12:13].reshape(SEQ * 4, LANES).astype(F32)
    mixed = pltpu.roll(misc[pl.ds(1, SEQ, stride=4), :], (LANES - 16 * part) % LANES, 1)

    def own_lanes(number):
        return pltpu.roll(mixed, LANES - 16 * number, 1) if number else mixed

    steps = to_columns(own_lanes(0), own_lanes(1))
    gates_high = to_columns(own_lanes(2), own_lanes(3))
    gates_low = to_columns(own_lanes(4), own_lanes(5))
    spread(recv_ref[:, 0:4].reshape(SEQ, 16, LANES).astype(F32), wide, data_ref, 0)
    spread(recv_ref[:, 4:8].reshape(SEQ, 16, LANES).astype(F32), wide_two, data_ref, LOCAL)
    spread(recv_ref[:, 8:12].reshape(SEQ, 16, LANES).astype(F32), wide_three, proj_ref, 0)
    pos_rows = jnp.concatenate(
        [misc[pl.ds(part * 32 + 4 * block, 1), :] for block in range(BLOCKS)], axis=0
    )
    pos_cols = jnp.concatenate([pos_rows, jnp.zeros((LANES - BLOCKS, LANES), F32)], axis=0).T
    lane = lane_iota(TOK)
    steps_bf = steps.astype(BF16)
    sums = jnp.zeros((TOK, LANES), F32)
    for block in range(BLOCKS):
        later = (pos_cols[:, block : block + 1] >= pos_rows[block : block + 1, :]).astype(F32).astype(BF16)
        sums = jnp.where(lane // 2 == block, nn(later, steps_bf), sums)
    slopes = slope_lanes(decay_ref, pair, TOK)
    logs = sums * slopes
    totals = jnp.sum(steps, axis=0, keepdims=True) * slopes[:1]
    short = jnp.where(lane_iota(1) < 2 * BLOCKS, totals, 0.0)
    onward = short
    until = pltpu.roll(short, 2, 1)
    for reach in (2, 4, 8):
        onward = onward + pltpu.roll(onward, LANES - reach, 1)
        until = until + pltpu.roll(until, reach, 1)
    base = 2 * LOCAL
    data_ref[base : base + TOK, :] = steps_bf
    data_ref[base + TOK : base + 2 * TOK, :] = gates_high.astype(BF16)
    data_ref[base + 2 * TOK : base + 3 * TOK, :] = gates_low.astype(BF16)
    data_ref[base + 3 * TOK : base + 4 * TOK, :] = pos_cols.astype(BF16)
    whole = heads_over_lanes(onward[:, 0:1], onward[:, 1:2], 1)
    top = whole.astype(BF16).astype(F32)
    middle = (whole - top).astype(BF16).astype(F32)
    bottom = whole - top - middle
    tail = jnp.concatenate([top, middle, bottom, jnp.zeros((13, LANES), F32)], axis=0).astype(BF16)
    weight_ref[2 * LOCAL : 2 * LOCAL + 16, :] = tail
    weights = steps * jnp.exp(jnp.minimum(onward - logs, 0.0))
    starts = jnp.exp(jnp.minimum(logs + until, 0.0))
    for block in range(BLOCKS):
        rows = block_rows(block)
        later_rows = slice(LOCAL + block * TOK, LOCAL + block * TOK + TOK)
        weight_ref[rows, :] = (
            data_ref[rows, :].astype(F32) * block_lanes(weights, block, TOK)
        ).astype(BF16)
        weight_ref[later_rows, :] = (
            data_ref[later_rows, :].astype(F32) * block_lanes(starts, block, TOK)
        ).astype(BF16)


def gather_kernel(mine_ref, swap_ref, data_ref, all_ref, wide):
    part, pair, core = my_place()
    all_ref[0 : 2 * LOCAL, :] = data_ref[0 : 2 * LOCAL, :]
    all_ref[4 * LOCAL : 4 * LOCAL + 4 * TOK, :] = data_ref[2 * LOCAL : 2 * LOCAL + 4 * TOK, :]

    @pl.when(core == 0)
    def _():
        all_ref[2 * LOCAL : 3 * LOCAL, :] = mine_ref[...]
        spread(swap_ref[...].reshape(SEQ, 16, LANES).astype(F32), wide, all_ref, 3 * LOCAL)

    @pl.when(core == 1)
    def _():
        all_ref[3 * LOCAL : 4 * LOCAL, :] = mine_ref[...]
        spread(swap_ref[...].reshape(SEQ, 16, LANES).astype(F32), wide, all_ref, 2 * LOCAL)


def states_kernel(all_ref, weight_ref, send_ref):
    part, pair, core = my_place()
    state = jnp.zeros((LANES, LANES), F32)
    adjoint = jnp.zeros((LANES, LANES), F32)
    for block in range(0, BLOCKS, 2):
        rows = slice(block * TOK, block * TOK + 2 * TOK)
        later_rows = slice(LOCAL + block * TOK, LOCAL + block * TOK + 2 * TOK)
        write = all_ref[2 * LOCAL + block * TOK : 2 * LOCAL + block * TOK + 2 * TOK, :]
        read = all_ref[3 * LOCAL + block * TOK : 3 * LOCAL + block * TOK + 2 * TOK, :]
        state = state + nn(turned(write), weight_ref[rows, :])
        adjoint = adjoint + nn(turned(read), weight_ref[later_rows, :])
    state = state.astype(BF16)
    adjoint = adjoint.astype(BF16)
    for slot in range(PARTS):
        after = slot > part

        @pl.when(after)
        def _():
            send_ref[slot, 0:128, :] = state

        @pl.when(jnp.logical_not(after))
        def _():
            send_ref[slot, 0:128, :] = adjoint

        send_ref[slot, 128:136, :] = weight_ref[2 * LOCAL : 2 * LOCAL + 16, :][:8]


def inner_kernel(decay_ref, all_ref, sums_ref, grad_ref):
    part, pair, core = my_place()
    base = 4 * LOCAL
    steps_bf = all_ref[base : base + TOK, :]
    steps = steps_bf.astype(F32)
    pos_cols = all_ref[base + 3 * TOK : base + 4 * TOK, :].astype(F32)
    pos_rows = pos_cols.T[:8]
    grad_ref[LOCAL + 2 * TOK : LOCAL + 3 * TOK, :] = jnp.zeros((TOK, LANES), F32)
    lane = lane_iota(TOK)
    sums = jnp.zeros((TOK, LANES), F32)
    masks = []
    for block in range(BLOCKS):
        behind = pos_cols[:, block : block + 1] >= pos_rows[block : block + 1, :]
        masks.append(behind.astype(F32).astype(BF16))
        sums = jnp.where(lane // 2 == block, nn(masks[block], steps_bf), sums)
    slopes = slope_lanes(decay_ref, pair, TOK)
    logs = sums * slopes
    log_rows = logs.T
    totals = jnp.sum(steps, axis=0, keepdims=True) * slopes[:1]
    starts = jnp.exp(logs)
    ends = steps * jnp.exp(totals - logs)
    grad_ref[LOCAL : LOCAL + TOK, :] = ends
    grad_ref[LOCAL + TOK : LOCAL + 2 * TOK, :] = starts
    for block in range(BLOCKS):
        rows = block_rows(block)

        def piece(number):
            return all_ref[number * LOCAL + block * TOK : number * LOCAL + block * TOK + TOK, :]

        def sums_rows(number):
            return slice(number * LOCAL + block * TOK, number * LOCAL + block * TOK + TOK)

        x, dy, write, read = piece(0), piece(1), piece(2), piece(3)
        sums_ref[2 * LOCAL + block : 2 * LOCAL + block + 1, :] = block_lanes(totals, block, 1)
        ahead = pos_rows[block : block + 1, :] >= pos_cols[:, block : block + 1]
        behind = masks[block]
        cross = nt(write, read)
        zero = jnp.zeros_like(dy)
        x_heads = (jnp.where(lane < 64, x, zero), jnp.where(lane < 64, zero, x))
        dy_stack = jnp.concatenate(
            [jnp.where(lane < 64, dy, zero), jnp.where(lane < 64, zero, dy)], axis=0
        )
        carry, mixed, seen = [], [], []
        for head in range(2):
            j = 2 * block + head
            gap = log_rows[j : j + 1, :] - logs[:, j : j + 1]
            decay = jnp.exp(jnp.where(ahead, gap, -1e30))
            carry.append(decay * cross)
            mixed.append(decay * (nt(x_heads[head], dy) * steps[:, j : j + 1]))
            seen.append(twice_split(mixed[head] * cross))
        crossed = nn(jnp.concatenate(seen, axis=0), jnp.concatenate([behind, behind], axis=0))
        for head in range(2):
            j = LOCAL + 2 * TOK + 2 * block + head
            own = jnp.where(ahead, crossed[head * TOK : head * TOK + TOK], 0.0)
            grad_ref[j : j + 1, :] = jnp.sum(own, axis=0, keepdims=True)
        high, low = split(jnp.concatenate(carry, axis=1))
        grad_ref[rows, :] = block_lanes(steps, block, TOK) * (nn(high, dy_stack) + nn(low, dy_stack))
        both = mixed[0] + mixed[1]
        sums_ref[sums_rows(0), :] = nn(twice_split(both), jnp.concatenate([read, read], axis=0))
        sums_ref[sums_rows(1), :] = nn(twice_split(both.T), jnp.concatenate([write, write], axis=0))


def outer_kernel(recv_ref, sums_ref, data_ref, grad_ref, keep_ref, give_ref, all_ref, adj):
    part, pair, core = my_place()

    totals = []
    for slot in range(PARTS):
        tail = recv_ref[slot, 128:136, :].astype(F32)
        totals.append(tail[0:1] + tail[1:2] + tail[2:3])
    zero = jnp.zeros((1, LANES), F32)
    state = jnp.zeros((LANES, LANES), F32)
    adjoint = jnp.zeros((LANES, LANES), F32)
    after, before = zero, zero
    weights = [None] * PARTS
    for slot in reversed(range(PARTS)):
        weights[slot] = jnp.where(slot < part, jnp.exp(after), zero)
        after = after + jnp.where(slot < part, totals[slot], zero)
    for slot in range(PARTS):
        weight = jnp.where(slot > part, jnp.exp(before), zero)
        before = before + jnp.where(slot > part, totals[slot], zero)
        sent = recv_ref[slot, 0:128, :].astype(F32)
        state = state + weights[slot] * sent
        adjoint = adjoint + weight * sent
    keeps = jnp.exp(sums_ref[2 * LOCAL : 2 * LOCAL + 8, :])

    def sums_rows(number, block):
        return slice(number * LOCAL + block * TOK, number * LOCAL + block * TOK + TOK)

    ends = grad_ref[LOCAL : LOCAL + TOK, :]
    starts = grad_ref[LOCAL + TOK : LOCAL + 2 * TOK, :]

    def data_rows(number, block):
        return slice(number * LOCAL + block * TOK, number * LOCAL + block * TOK + TOK)

    gains, ds, xe = [], [], []
    for block in range(BLOCKS):
        xe.append(split(data_ref[data_rows(0, block), :].astype(F32) * block_lanes(ends, block, TOK)))
        ds.append(split(data_ref[data_rows(1, block), :].astype(F32) * block_lanes(starts, block, TOK)))
        write = twice(turned(data_ref[data_rows(2, block), :]))
        read = twice(turned(data_ref[data_rows(3, block), :]))
        gains.append((nn(write, jnp.concatenate(xe[block], axis=0)), nn(read, jnp.concatenate(ds[block], axis=0))))
    for block in reversed(range(BLOCKS)):
        adj[block] = adjoint
        adjoint = adjoint * keeps[block : block + 1] + gains[block][1]
    overlaps = []
    for block in range(BLOCKS):
        adjoint = adj[block]
        state_high, state_low = split(state)
        adj_high, adj_low = split(adjoint)
        first = block * 2 * TOK
        all_ref[4 * LOCAL + first : 4 * LOCAL + first + TOK, :] = state_high
        all_ref[4 * LOCAL + first + TOK : 4 * LOCAL + first + 2 * TOK, :] = state_low
        all_ref[6 * LOCAL + first : 6 * LOCAL + first + TOK, :] = adj_high
        all_ref[6 * LOCAL + first + TOK : 6 * LOCAL + first + 2 * TOK, :] = adj_low
        keep = keeps[block : block + 1]
        overlaps.append(jnp.sum(adjoint * state, axis=0, keepdims=True) * keep)
        ds_high, ds_low = ds[block]
        xe_high, xe_low = xe[block]
        all_ref[first : first + TOK, :] = ds_high
        all_ref[first + TOK : first + 2 * TOK, :] = ds_low
        all_ref[2 * LOCAL + first : 2 * LOCAL + first + TOK, :] = xe_high
        all_ref[2 * LOCAL + first + TOK : 2 * LOCAL + first + 2 * TOK, :] = xe_low
        gr = sums_ref[sums_rows(1, block), :] + (
            nt(jnp.concatenate([ds_high, ds_low], axis=1), twice(state_high)) + nt(ds_high, state_low)
        )
        gw = sums_ref[sums_rows(0, block), :] + (
            nt(jnp.concatenate([xe_high, xe_low], axis=1), twice(adj_high)) + nt(xe_high, adj_low)
        )
        kept = jnp.where(core == 0, gw, gr)
        given = jnp.where(core == 0, gr, gw)
        for half in range(2):
            out_rows = pl.ds(2 * block + half, 64, stride=16)
            own_rows = slice(64 * half, 64 * half + 64)
            keep_ref[out_rows, :] = kept[own_rows]
            give_ref[out_rows, :] = given[own_rows]
        state = state * keep + gains[block][0]
    overlaps = jnp.concatenate(overlaps, axis=0)
    top = overlaps.astype(BF16).astype(F32)
    middle = (overlaps - top).astype(BF16).astype(F32)
    bottom = overlaps - top - middle
    all_ref[8 * LOCAL : 8 * LOCAL + 32, :] = jnp.concatenate(
        [top, middle, bottom, jnp.zeros((8, LANES), F32)], axis=0
    ).astype(BF16)


def grads_kernel(decay_ref, data_ref, all_ref, grad_ref, out_ref, wide, misc):
    part, pair, core = my_place()
    slopes = slope_lanes(decay_ref, pair, TOK)
    base = 4 * LOCAL
    steps = data_ref[base : base + TOK, :].astype(F32)
    gates = data_ref[base + TOK : base + 2 * TOK, :].astype(F32) + data_ref[base + 2 * TOK : base + 3 * TOK, :].astype(F32)
    pos_cols = data_ref[base + 3 * TOK : base + 4 * TOK, :].astype(F32)
    pos_rows = pos_cols.T[:8]
    ends = grad_ref[LOCAL : LOCAL + TOK, :]
    lane = lane_iota(TOK)
    tail = all_ref[8 * LOCAL : 8 * LOCAL + 32, :].astype(F32)
    overlaps = tail[0:8] + tail[8:16] + tail[16:24]
    row_lane = lane_iota(8)
    row = lax.broadcasted_iota(jnp.int32, (8, LANES), 0)
    first = jnp.sum(jnp.where(row_lane < 64, overlaps, 0.0), axis=1, keepdims=True)
    second = jnp.sum(jnp.where(row_lane < 64, 0.0, overlaps), axis=1, keepdims=True)
    kept = jnp.where(row_lane == 2 * row, first, jnp.where(row_lane == 2 * row + 1, second, 0.0))
    sub = lax.broadcasted_iota(jnp.int32, (2 * LANES, LANES), 0) % LANES // 64
    pick_lane = lax.broadcasted_iota(jnp.int32, (2 * LANES, LANES), 1)
    per_head = jnp.zeros((3 * TOK, LANES), F32)
    for block in range(BLOCKS):
        rows = block_rows(block)
        lo = block * 2 * TOK

        def both(number):
            start = number * LOCAL + lo
            return all_ref[start : start + TOK, :].astype(F32) + all_ref[start + TOK : start + 2 * TOK, :].astype(F32)

        x = data_ref[rows, :].astype(F32)
        write = data_ref[2 * LOCAL + block * TOK : 2 * LOCAL + block * TOK + TOK, :]
        read = data_ref[3 * LOCAL + block * TOK : 3 * LOCAL + block * TOK + TOK, :]
        carried = nn(twice(write), all_ref[6 * LOCAL + lo : 6 * LOCAL + lo + 2 * TOK, :])
        recalled = nn(twice(read), all_ref[4 * LOCAL + lo : 4 * LOCAL + lo + 2 * TOK, :])
        act = grad_ref[rows, :] + block_lanes(ends, block, TOK) * carried
        wide[pl.ds(2 * block, 64, stride=16), :] = act[:64]
        wide[pl.ds(2 * block + 1, 64, stride=16), :] = act[64:]
        products = jnp.concatenate([both(0) * recalled, both(2) * carried, x * act], axis=0)
        pick = (pick_lane == 2 * block + sub).astype(F32).astype(BF16)
        per_head = per_head + nn(twice_split(products), pick)

    direct = per_head[2 * TOK :]
    read_high, read_low = split(per_head[:TOK].T[: 2 * BLOCKS])
    write_part = per_head[TOK : 2 * TOK].T[: 2 * BLOCKS]
    write_high, write_low = split(write_part)
    vectors = jnp.concatenate([read_high, read_low, write_high, write_low], axis=0)
    log_rows = grad_ref[LOCAL + 2 * TOK : LOCAL + 2 * TOK + 2 * BLOCKS, :]
    log_rows = log_rows + write_part + jnp.sum(write_part, axis=1, keepdims=True)
    owner = lax.broadcasted_iota(jnp.int32, (2 * BLOCKS, LANES), 0) // 2
    for block in range(BLOCKS):
        behind = (pos_cols[:, block : block + 1] >= pos_rows[block : block + 1, :]).astype(F32).astype(BF16)
        sums = nn(vectors, behind)
        added = (sums[0:16] + sums[16:32]) - (sums[32:48] + sums[48:64])
        log_rows = log_rows + jnp.where(owner == block, added, 0.0)
    log_grad = jnp.concatenate([log_rows, jnp.zeros((TOK - 2 * BLOCKS, LANES), F32)], axis=0).T
    log_grad = log_grad + jnp.sum(kept, axis=0, keepdims=True)
    grad_step = direct / steps + slopes * (log_grad - direct)
    grad_step = jnp.where(lane < 2 * BLOCKS, grad_step, 0.0).astype(BF16).astype(F32)
    grad_pre = grad_step * gates
    frames = []
    for frame in range(4):
        low_rows = slice(16 * frame, 16 * frame + 16)
        high_rows = slice(64 + 16 * frame, 80 + 16 * frame)
        frames.append(jnp.sum(grad_pre[low_rows] + grad_pre[high_rows], axis=0, keepdims=True))
    frames = sum(pltpu.roll(jnp.where(lane_iota(1) < 16, row, 0.0), 16 * i, 1) for i, row in enumerate(frames))
    frames_high = frames.astype(BF16).astype(F32)
    frames = frames_high + pltpu.roll(frames - frames_high, 64, 1)

    even = lane_iota(64) % 2 == 0
    top, bottom = grad_step[:64], grad_step[64:]
    shift = 16 * part
    row_one = pltpu.roll(jnp.where(even, top, pltpu.roll(bottom, 1, 1)), shift, 1)
    row_two = pltpu.roll(jnp.where(even, pltpu.roll(top, LANES - 1, 1), bottom), shift, 1)
    misc[...] = jnp.zeros((SEQ * 8, LANES), F32)
    misc[pl.ds(0, 64, stride=8), :] = row_one
    misc[pl.ds(1, 64, stride=8), :] = row_two
    misc[pl.ds(2, 64, stride=8), :] = jnp.broadcast_to(frames, (SEQ, LANES))
    out_ref[:, 0:16, :] = wide[...].reshape(SEQ, 16, LANES).astype(BF16)
    out_ref[:, 16:32, :] = jnp.zeros((SEQ, 16, LANES), BF16)
    out_ref[:, 32:40, :] = misc[...].reshape(SEQ, 8, LANES).astype(BF16)


def join_kernel(in_ref, keep_ref, got_ref, out_ref):
    out_ref[:, 0:4] = in_ref[:, 0:16, :].reshape(SEQ, 4, 4, LANES)
    proj = (keep_ref[...] + got_ref[...]).reshape(SEQ, 16, LANES).astype(BF16)
    out_ref[:, 4:8] = proj.reshape(SEQ, 4, 4, LANES)
    out_ref[:, 8:9] = in_ref[:, 32:40, :].reshape(SEQ, 2, 4, LANES)[:, 0:1]


def proj_kernel(recv_ref, proj_ref, rest_ref):
    for part in range(PARTS):
        for core in range(2):
            total = recv_ref[place(part, core), 4:8].reshape(16, LANES).astype(F32)
            for high in range(1, 4):
                total = total + recv_ref[place(part, 2 * high + core), 4:8].reshape(16, LANES).astype(F32)
            proj_ref[16 * part : 16 * part + 16, LANES * core : LANES * core + LANES] = total.astype(BF16)
    rest_ref[:, 0:4] = recv_ref[:, 0:4]
    rest_ref[:, 4:5] = recv_ref[:, 8:9]


def finish_kernel(frame_ref, recv_ref, raw_ref, table_ref, act_ref, pre_ref, grad_ref, rows_ref):
    heads = raw_ref.shape[0]
    for pair in range(PAIRS):
        columns = slice(LANES * pair, LANES * pair + LANES)
        for part in range(PARTS):
            act_ref[16 * part : 16 * part + 16, columns] = recv_ref[place(part, pair), 0:4].reshape(16, LANES)
    lane = lane_iota(8)
    row = lax.broadcasted_iota(jnp.int32, (8, LANES), 0)
    sums = []
    for pair in range(PAIRS):
        rows = recv_ref[place(0, pair), 4:5].reshape(4, LANES).astype(F32)
        for part in range(1, PARTS):
            rows = rows + recv_ref[place(part, pair), 4:5].reshape(4, LANES).astype(F32)
        rows_ref[2 * pair : 2 * pair + 2, :] = rows[0:2]
        sums.append(rows[2:3])
    sums = jnp.concatenate(sums, axis=0)
    sums = sums + pltpu.roll(sums, 64, 1)
    per_frame = []
    for frame in range(4):
        total = jnp.zeros((8, LANES), F32)
        for head in range(2):
            inside = (lane // 16 == frame) & (lane % 2 == head)
            part_sum = jnp.sum(jnp.where(inside, sums, 0.0), axis=1, keepdims=True)
            total = jnp.where(lane == 2 * row + head, part_sum, total)
        per_frame.append(jnp.sum(total, axis=0, keepdims=True))
    pre = shifted_steps(frame_ref, raw_ref[...], table_ref[...])
    pre_ref[...] = rows_ref[...] * sigmoid(pre)
    per_head = jnp.concatenate(per_frame + [jnp.zeros((LANES - 4, LANES), F32)], axis=0).T
    steps = lax.broadcasted_iota(jnp.int32, grad_ref.shape, 1)
    grad = jnp.zeros(grad_ref.shape, F32)
    for frame in range(4):
        grad = grad + jnp.where(steps == frame_ref[frame], per_head[:heads, frame : frame + 1], 0.0)
    grad_ref[...] = grad


def total_kernel(own_ref, one_ref, two_ref, three_ref, write_ref, read_ref):
    even = own_ref[...].astype(F32) + two_ref[...].astype(F32)
    odd = one_ref[...].astype(F32) + three_ref[...].astype(F32)
    total = (even + odd).astype(BF16)
    write_ref[...] = total[:, :LANES]
    read_ref[...] = total[:, LANES:]


VMEM = pl.BlockSpec(memory_space=pltpu.VMEM)
SMEM = pl.BlockSpec(memory_space=pltpu.SMEM)


def call(kernel, name, in_specs, out_shape, scratch=(), params=PARAMS, out=VMEM):
    shapes = [jax.ShapeDtypeStruct(shape, dtype) for shape, dtype in out_shape]
    return pl.pallas_call(
        kernel,
        out_shape=shapes,
        in_specs=in_specs,
        out_specs=[out] * len(shapes),
        scratch_shapes=list(scratch),
        compiler_params=params,
        name=name,
    )


def shards(
    activations, grad_out, write_proj, read_proj, step_raw, step_table, decay_rate, frame_step, scan_order
):
    raw, table = step_raw.T, step_table.T
    rates = decay_rate.reshape(1, decay_rate.shape[0])
    swap_core = [(i, i ^ 1) for i in range(SEQ)]
    hbm = pl.BlockSpec(memory_space=pltpu.HBM)
    order = scan_order.reshape(1, TOK)
    sources = (order, frame_step, raw, table, write_proj, read_proj, activations, grad_out)
    (send,) = call(
        pack_kernel, "pack", [hbm] * 8, [((SEQ, 13, 4, LANES), BF16)],
        [(pltpu.SMEM if a is frame_step else pltpu.VMEM)(a.shape, a.dtype) for a in sources]
        + [
            pltpu.VMEM((SEQ, 13, 4, LANES), BF16),
            pltpu.VMEM((SEQ * 4, LANES), F32),
            pltpu.SemaphoreType.DMA((12,)),
        ],
        pltpu.CompilerParams(vmem_limit_bytes=62 * 1024 * 1024), hbm,
    )(*sources)
    recv = lax.all_to_all(send, "seq", 0, 0, tiled=True)
    (proj,) = call(cut_kernel, "cut", [VMEM], [((SEQ, 4, 4, LANES), BF16)])(recv)
    swap = lax.ppermute(proj, "seq", swap_core)
    wide = pltpu.VMEM((LOCAL, LANES), F32)
    bundle = ((4 * LOCAL + 4 * TOK, LANES), BF16)
    sums = ((LOCAL, LANES), F32)
    data, mine, weight = call(
        unpack_kernel, "unpack", [VMEM] * 2,
        [((2 * LOCAL + 4 * TOK, LANES), BF16), ((LOCAL, LANES), BF16), ((2 * LOCAL + 16, LANES), BF16)],
        [wide] * 3 + [pltpu.VMEM((SEQ * 4, LANES), F32)],
    )(rates, recv)
    (data,) = call(gather_kernel, "gather", [VMEM] * 3, [bundle], [wide])(mine, swap, data)
    (states,) = call(states_kernel, "states", [VMEM] * 2, [((PARTS, SLOT_STATE, LANES), BF16)])(data, weight)
    states = lax.all_to_all(states, "seq", 0, 0, tiled=True, axis_index_groups=STATE_GROUPS)
    inner, grad = call(
        inner_kernel, "inner", [VMEM] * 2,
        [
            ((2 * LOCAL + 8, LANES), F32),
            ((LOCAL + 3 * TOK, LANES), F32),
        ],
    )(rates, data)
    keep, give, pairs = call(
        outer_kernel, "outer", [VMEM] * 4,
        [sums] * 2 + [((8 * LOCAL + 32, LANES), BF16)],
        [pltpu.VMEM((BLOCKS, LANES, LANES), F32)],
    )(states, inner, data, grad)
    got = lax.ppermute(give, "seq", swap_core)
    (out,) = call(
        grads_kernel, "grads", [VMEM] * 4, [((SEQ, SLOT_OUT, LANES), BF16)],
        [wide, pltpu.VMEM((SEQ * 8, LANES), F32)],
    )(rates, data, pairs, grad)
    (out,) = call(join_kernel, "join", [VMEM] * 3, [((SEQ, 9, 4, LANES), BF16)])(out, keep, got)
    back = lax.all_to_all(out, "seq", 0, 0, tiled=True)
    proj, rest = call(
        proj_kernel, "proj", [VMEM], [((TOK, 2 * LANES), BF16), ((SEQ, 5, 4, LANES), BF16)]
    )(back)
    ring = [lax.ppermute(proj, "head", [(i, (i + k) % 4) for i in range(4)]) for k in (1, 2, 3)]
    act, grad_pre, grad_table = call(
        finish_kernel, "finish", [SMEM] + [VMEM] * 3,
        [(activations.shape, BF16), (raw.shape, F32), (table.shape, F32)],
        [pltpu.VMEM((2 * PAIRS, LANES), F32)],
    )(frame_step, rest, raw, table)
    grad_write, grad_read = call(
        total_kernel, "total", [VMEM] * 4, [(write_proj.shape, BF16), (read_proj.shape, BF16)]
    )(proj, *ring)
    return (act, grad_write, grad_read, grad_pre.T, grad_table.T)


def solution(mesh):
    in_specs = (
        P("seq", "head"),
        P("seq", "head"),
        P("seq", None),
        P("seq", None),
        P("seq", "head"),
        P(None, "head"),
        P("head"),
        P(),
        P("seq"),
    )
    out_specs = (
        P("seq", "head"),
        P("seq", None),
        P("seq", None),
        P("seq", "head"),
        P(None, "head"),
    )
    return jax.shard_map(shards, mesh=mesh, in_specs=in_specs, out_specs=out_specs, check_vma=False)
```

```python
import jax
import jax.numpy as jnp
from jax import lax
from jax.experimental import pallas as pl
from jax.experimental.pallas import tpu as pltpu
from jax.sharding import PartitionSpec as P

F32 = jnp.float32
BF16 = jnp.bfloat16
FRAME_TOK = 2048
TOK = 128
LANES = 128
SEQ = 64
PARTS = 8
PAIRS = 8
BLOCKS = 8
SLOT_STATE = 136
SLOT_OUT = 40
LOCAL = BLOCKS * TOK
PARAMS = pltpu.CompilerParams(vmem_limit_bytes=32 * 1024 * 1024)


def place(part, pair):
    y, low = part // 2, part % 2
    high, core = pair // 2, pair % 2
    return y * 16 + (high * 2 + low) * 2 + core


def my_place():
    me = lax.axis_index("seq")
    part = (me // 16) * 2 + (me // 2) % 2
    pair = ((me // 4) % 4) * 2 + me % 2
    return part, pair, me % 2


STATE_GROUPS = [[place(part, pair) for part in range(PARTS)] for pair in range(PAIRS)]


def nn(a, b):
    return lax.dot_general(a, b, (((1,), (0,)), ((), ())), preferred_element_type=F32)


def nt(a, b):
    return lax.dot_general(a, b, (((1,), (1,)), ((), ())), preferred_element_type=F32)


def split(value):
    high = value.astype(BF16)
    return high, (value - high.astype(F32)).astype(BF16)


def lane_iota(rows):
    return lax.broadcasted_iota(jnp.int32, (rows, LANES), 1)


def heads_over_lanes(first, second, rows):
    return jnp.where(lane_iota(rows) < 64, first, second)


def softplus(value):
    return jnp.maximum(value, 0.0) + jnp.log1p(jnp.exp(-jnp.abs(value)))


def sigmoid(value):
    return 1.0 / (1.0 + jnp.exp(-value))


def shifted_steps(frame_ref, raw, table):
    frame_here = lax.axis_index("seq") * TOK // FRAME_TOK
    index = frame_ref[frame_here]
    columns = lax.broadcasted_iota(jnp.int32, table.shape, 1)
    shift = jnp.sum(jnp.where(columns == index, table, 0.0), axis=1, keepdims=True)
    return raw + shift


def pack_kernel(*refs):
    sources, sent_ref, targets, out_ref, misc, sems = refs[:8], refs[8], refs[9:17], refs[17], refs[18], refs[19]
    copies = [
        pltpu.make_async_copy(source, target, sems.at[i])
        for i, (source, target) in enumerate(zip(sources, targets))
    ]
    for copy in copies:
        copy.start()
    order_ref, frame_ref, raw_ref, table_ref, b_ref, c_ref, x_ref, dy_ref = targets
    copies[0].wait()
    order = jnp.broadcast_to(order_ref[...].astype(F32), (TOK, TOK)).T
    lane = lane_iota(TOK)
    token = ((lane % 64) * 2 + lane // 64).astype(F32)
    steps = lax.broadcasted_iota(jnp.int32, (TOK, TOK), 0).astype(F32)
    position = jnp.sum(jnp.where(order == token, steps, 0.0), axis=0, keepdims=True)
    for copy in copies[1:4]:
        copy.wait()
    pre = shifted_steps(frame_ref, raw_ref[...], table_ref[...])
    delta = softplus(pre).astype(BF16).astype(F32)
    gate = sigmoid(pre)
    gate_high = gate.astype(BF16).astype(F32)
    gate_low = gate - gate_high
    for copy in copies[4:]:
        copy.wait()
    row = lax.broadcasted_iota(jnp.int32, pre.shape, 0) % 2
    group = lax.broadcasted_iota(jnp.int32, pre.shape, 1) // 16
    turns = []
    for kind, value in enumerate((delta, gate_high, gate_low)):
        first = pltpu.roll(value, 32 * kind, 1) if kind else value
        turns.append(jnp.where(row == 0, first, pltpu.roll(value, 32 * kind + 16, 1)))
    misc[...] = jnp.zeros((SEQ * 4, LANES), F32)
    misc[pl.ds(0, SEQ, stride=4), :] = jnp.broadcast_to(position, (SEQ, LANES))
    for part in range(PARTS):
        mixed = jnp.zeros(pre.shape, F32)
        for kind in range(3):
            mixed = mixed + jnp.where(group == (part + 2 * kind + row) % 8, turns[kind], 0.0)
        mixed = mixed + pltpu.roll(mixed, mixed.shape[0] - 1, 0)
        for pair in range(PAIRS):
            spot = 4 * place(part, pair) + 1
            misc[spot : spot + 1, :] = mixed[2 * pair : 2 * pair + 1]
    out_ref[:, 12:13] = misc[...].astype(BF16).reshape(SEQ, 1, 4, LANES)
    leaving = []
    for quarter in range(4):
        for part in (2 * quarter, 2 * quarter + 1):
            tokens = slice(16 * part, 16 * part + 16)
            for pair in range(PAIRS):
                proj_ref = c_ref if pair % 2 else b_ref
                columns = slice(LANES * pair, LANES * pair + LANES)
                slot = place(part, pair)
                out_ref[slot, 0:4] = x_ref[tokens, columns].reshape(4, 4, LANES)
                out_ref[slot, 4:8] = dy_ref[tokens, columns].reshape(4, 4, LANES)
                out_ref[slot, 8:12] = proj_ref[tokens, :].reshape(4, 4, LANES)
        slots = pl.ds(16 * quarter, 16)
        leaving.append(pltpu.make_async_copy(out_ref.at[slots], sent_ref.at[slots], sems.at[8 + quarter]))
        leaving[quarter].start()
    for copy in leaving:
        copy.wait()


def to_columns(first, second):
    head_one = jnp.concatenate([first, pltpu.roll(first, LANES - 1, 1)], axis=0)
    head_two = jnp.concatenate([pltpu.roll(second, 1, 1), second], axis=0)
    return jnp.where(lane_iota(TOK) % 2 == 0, head_one, head_two)


def slope_lanes(decay_ref, pair, rows):
    rates = decay_ref[...]
    lane = lax.broadcasted_iota(jnp.int32, rates.shape, 1)
    first = jnp.sum(jnp.where(lane == 2 * pair, rates, 0.0), axis=1, keepdims=True)
    second = jnp.sum(jnp.where(lane == 2 * pair + 1, rates, 0.0), axis=1, keepdims=True)
    return jnp.where(lane_iota(rows) % 2 == 0, -first, -second)


def block_lanes(columns, block, rows):
    j = 2 * block
    return heads_over_lanes(columns[:, j : j + 1], columns[:, j + 1 : j + 2], rows)


def block_rows(block):
    return slice(block * TOK, block * TOK + TOK)


def stack(value):
    return jnp.concatenate(split(value), axis=0)


def twice(value):
    return jnp.concatenate([value, value], axis=1)


def turned(value):
    return value.astype(F32).T.astype(BF16)


def twice_split(value):
    return jnp.concatenate(split(value), axis=1)


def spread(value, wide, target_ref, base):
    wide[...] = value.reshape(SEQ * 16, LANES)
    for row in range(16):
        start = base + row * 64
        target_ref[start : start + 64, :] = wide[pl.ds(row, 64, stride=16), :].astype(BF16)


def cut_kernel(recv_ref, proj_ref):
    proj_ref[...] = recv_ref[:, 8:12]


def unpack_kernel(
    decay_ref, recv_ref, data_ref, proj_ref, weight_ref, wide, wide_two, wide_three, misc
):
    part, pair, core = my_place()
    misc[...] = recv_ref[:, 12:13].reshape(SEQ * 4, LANES).astype(F32)
    mixed = pltpu.roll(misc[pl.ds(1, SEQ, stride=4), :], (LANES - 16 * part) % LANES, 1)

    def own_lanes(number):
        return pltpu.roll(mixed, LANES - 16 * number, 1) if number else mixed

    steps = to_columns(own_lanes(0), own_lanes(1))
    gates_high = to_columns(own_lanes(2), own_lanes(3))
    gates_low = to_columns(own_lanes(4), own_lanes(5))
    spread(recv_ref[:, 0:4].reshape(SEQ, 16, LANES).astype(F32), wide, data_ref, 0)
    spread(recv_ref[:, 4:8].reshape(SEQ, 16, LANES).astype(F32), wide_two, data_ref, LOCAL)
    spread(recv_ref[:, 8:12].reshape(SEQ, 16, LANES).astype(F32), wide_three, proj_ref, 0)
    pos_rows = jnp.concatenate(
        [misc[pl.ds(part * 32 + 4 * block, 1), :] for block in range(BLOCKS)], axis=0
    )
    pos_cols = jnp.concatenate([pos_rows, jnp.zeros((LANES - BLOCKS, LANES), F32)], axis=0).T
    lane = lane_iota(TOK)
    steps_bf = steps.astype(BF16)
    sums = jnp.zeros((TOK, LANES), F32)
    for block in range(BLOCKS):
        later = (pos_cols[:, block : block + 1] >= pos_rows[block : block + 1, :]).astype(F32).astype(BF16)
        sums = jnp.where(lane // 2 == block, nn(later, steps_bf), sums)
    slopes = slope_lanes(decay_ref, pair, TOK)
    logs = sums * slopes
    totals = jnp.sum(steps, axis=0, keepdims=True) * slopes[:1]
    short = jnp.where(lane_iota(1) < 2 * BLOCKS, totals, 0.0)
    onward = short
    until = pltpu.roll(short, 2, 1)
    for reach in (2, 4, 8):
        onward = onward + pltpu.roll(onward, LANES - reach, 1)
        until = until + pltpu.roll(until, reach, 1)
    base = 2 * LOCAL
    data_ref[base : base + TOK, :] = steps_bf
    data_ref[base + TOK : base + 2 * TOK, :] = gates_high.astype(BF16)
    data_ref[base + 2 * TOK : base + 3 * TOK, :] = gates_low.astype(BF16)
    data_ref[base + 3 * TOK : base + 4 * TOK, :] = pos_cols.astype(BF16)
    whole = heads_over_lanes(onward[:, 0:1], onward[:, 1:2], 1)
    top = whole.astype(BF16).astype(F32)
    middle = (whole - top).astype(BF16).astype(F32)
    bottom = whole - top - middle
    tail = jnp.concatenate([top, middle, bottom, jnp.zeros((13, LANES), F32)], axis=0).astype(BF16)
    weight_ref[2 * LOCAL : 2 * LOCAL + 16, :] = tail
    weights = steps * jnp.exp(jnp.minimum(onward - logs, 0.0))
    starts = jnp.exp(jnp.minimum(logs + until, 0.0))
    for block in range(BLOCKS):
        rows = block_rows(block)
        later_rows = slice(LOCAL + block * TOK, LOCAL + block * TOK + TOK)
        weight_ref[rows, :] = (
            data_ref[rows, :].astype(F32) * block_lanes(weights, block, TOK)
        ).astype(BF16)
        weight_ref[later_rows, :] = (
            data_ref[later_rows, :].astype(F32) * block_lanes(starts, block, TOK)
        ).astype(BF16)


def gather_kernel(mine_ref, swap_ref, data_ref, all_ref, wide):
    part, pair, core = my_place()
    all_ref[0 : 2 * LOCAL, :] = data_ref[0 : 2 * LOCAL, :]
    all_ref[4 * LOCAL : 4 * LOCAL + 4 * TOK, :] = data_ref[2 * LOCAL : 2 * LOCAL + 4 * TOK, :]

    @pl.when(core == 0)
    def _():
        all_ref[2 * LOCAL : 3 * LOCAL, :] = mine_ref[...]
        spread(swap_ref[...].reshape(SEQ, 16, LANES).astype(F32), wide, all_ref, 3 * LOCAL)

    @pl.when(core == 1)
    def _():
        all_ref[3 * LOCAL : 4 * LOCAL, :] = mine_ref[...]
        spread(swap_ref[...].reshape(SEQ, 16, LANES).astype(F32), wide, all_ref, 2 * LOCAL)


def states_kernel(all_ref, weight_ref, send_ref):
    part, pair, core = my_place()
    state = jnp.zeros((LANES, LANES), F32)
    adjoint = jnp.zeros((LANES, LANES), F32)
    for block in range(0, BLOCKS, 2):
        rows = slice(block * TOK, block * TOK + 2 * TOK)
        later_rows = slice(LOCAL + block * TOK, LOCAL + block * TOK + 2 * TOK)
        write = all_ref[2 * LOCAL + block * TOK : 2 * LOCAL + block * TOK + 2 * TOK, :]
        read = all_ref[3 * LOCAL + block * TOK : 3 * LOCAL + block * TOK + 2 * TOK, :]
        state = state + nn(turned(write), weight_ref[rows, :])
        adjoint = adjoint + nn(turned(read), weight_ref[later_rows, :])
    state = state.astype(BF16)
    adjoint = adjoint.astype(BF16)
    for slot in range(PARTS):
        after = slot > part

        @pl.when(after)
        def _():
            send_ref[slot, 0:128, :] = state

        @pl.when(jnp.logical_not(after))
        def _():
            send_ref[slot, 0:128, :] = adjoint

        send_ref[slot, 128:136, :] = weight_ref[2 * LOCAL : 2 * LOCAL + 16, :][:8]


def inner_kernel(decay_ref, all_ref, sums_ref, grad_ref):
    part, pair, core = my_place()
    base = 4 * LOCAL
    steps_bf = all_ref[base : base + TOK, :]
    steps = steps_bf.astype(F32)
    pos_cols = all_ref[base + 3 * TOK : base + 4 * TOK, :].astype(F32)
    pos_rows = pos_cols.T[:8]
    grad_ref[LOCAL + 2 * TOK : LOCAL + 3 * TOK, :] = jnp.zeros((TOK, LANES), F32)
    lane = lane_iota(TOK)
    sums = jnp.zeros((TOK, LANES), F32)
    masks = []
    for block in range(BLOCKS):
        behind = pos_cols[:, block : block + 1] >= pos_rows[block : block + 1, :]
        masks.append(behind.astype(F32).astype(BF16))
        sums = jnp.where(lane // 2 == block, nn(masks[block], steps_bf), sums)
    slopes = slope_lanes(decay_ref, pair, TOK)
    logs = sums * slopes
    log_rows = logs.T
    totals = jnp.sum(steps, axis=0, keepdims=True) * slopes[:1]
    starts = jnp.exp(logs)
    ends = steps * jnp.exp(totals - logs)
    grad_ref[LOCAL : LOCAL + TOK, :] = ends
    grad_ref[LOCAL + TOK : LOCAL + 2 * TOK, :] = starts
    for block in range(BLOCKS):
        rows = block_rows(block)

        def piece(number):
            return all_ref[number * LOCAL + block * TOK : number * LOCAL + block * TOK + TOK, :]

        def sums_rows(number):
            return slice(number * LOCAL + block * TOK, number * LOCAL + block * TOK + TOK)

        x, dy, write, read = piece(0), piece(1), piece(2), piece(3)
        sums_ref[2 * LOCAL + block : 2 * LOCAL + block + 1, :] = block_lanes(totals, block, 1)
        ahead = pos_rows[block : block + 1, :] >= pos_cols[:, block : block + 1]
        behind = masks[block]
        cross = nt(write, read)
        zero = jnp.zeros_like(dy)
        x_heads = (jnp.where(lane < 64, x, zero), jnp.where(lane < 64, zero, x))
        dy_stack = jnp.concatenate(
            [jnp.where(lane < 64, dy, zero), jnp.where(lane < 64, zero, dy)], axis=0
        )
        carry, mixed, seen = [], [], []
        for head in range(2):
            j = 2 * block + head
            gap = log_rows[j : j + 1, :] - logs[:, j : j + 1]
            decay = jnp.exp(jnp.where(ahead, gap, -1e30))
            carry.append(decay * cross)
            mixed.append(decay * (nt(x_heads[head], dy) * steps[:, j : j + 1]))
            seen.append(twice_split(mixed[head] * cross))
        crossed = nn(jnp.concatenate(seen, axis=0), jnp.concatenate([behind, behind], axis=0))
        for head in range(2):
            j = LOCAL + 2 * TOK + 2 * block + head
            own = jnp.where(ahead, crossed[head * TOK : head * TOK + TOK], 0.0)
            grad_ref[j : j + 1, :] = jnp.sum(own, axis=0, keepdims=True)
        high, low = split(jnp.concatenate(carry, axis=1))
        grad_ref[rows, :] = block_lanes(steps, block, TOK) * (nn(high, dy_stack) + nn(low, dy_stack))
        both = mixed[0] + mixed[1]
        sums_ref[sums_rows(0), :] = nn(twice_split(both), jnp.concatenate([read, read], axis=0))
        sums_ref[sums_rows(1), :] = nn(twice_split(both.T), jnp.concatenate([write, write], axis=0))


def outer_kernel(recv_ref, sums_ref, data_ref, grad_ref, keep_ref, give_ref, all_ref, adj):
    part, pair, core = my_place()

    totals = []
    for slot in range(PARTS):
        tail = recv_ref[slot, 128:136, :].astype(F32)
        totals.append(tail[0:1] + tail[1:2] + tail[2:3])
    zero = jnp.zeros((1, LANES), F32)
    state = jnp.zeros((LANES, LANES), F32)
    adjoint = jnp.zeros((LANES, LANES), F32)
    after, before = zero, zero
    weights = [None] * PARTS
    for slot in reversed(range(PARTS)):
        weights[slot] = jnp.where(slot < part, jnp.exp(after), zero)
        after = after + jnp.where(slot < part, totals[slot], zero)
    for slot in range(PARTS):
        weight = jnp.where(slot > part, jnp.exp(before), zero)
        before = before + jnp.where(slot > part, totals[slot], zero)
        sent = recv_ref[slot, 0:128, :].astype(F32)
        state = state + weights[slot] * sent
        adjoint = adjoint + weight * sent
    keeps = jnp.exp(sums_ref[2 * LOCAL : 2 * LOCAL + 8, :])

    def sums_rows(number, block):
        return slice(number * LOCAL + block * TOK, number * LOCAL + block * TOK + TOK)

    ends = grad_ref[LOCAL : LOCAL + TOK, :]
    starts = grad_ref[LOCAL + TOK : LOCAL + 2 * TOK, :]

    def data_rows(number, block):
        return slice(number * LOCAL + block * TOK, number * LOCAL + block * TOK + TOK)

    gains, ds, xe = [], [], []
    for block in range(BLOCKS):
        xe.append(split(data_ref[data_rows(0, block), :].astype(F32) * block_lanes(ends, block, TOK)))
        ds.append(split(data_ref[data_rows(1, block), :].astype(F32) * block_lanes(starts, block, TOK)))
        write = twice(turned(data_ref[data_rows(2, block), :]))
        read = twice(turned(data_ref[data_rows(3, block), :]))
        gains.append((nn(write, jnp.concatenate(xe[block], axis=0)), nn(read, jnp.concatenate(ds[block], axis=0))))
    for block in reversed(range(BLOCKS)):
        adj[block] = adjoint
        adjoint = adjoint * keeps[block : block + 1] + gains[block][1]
    overlaps = []
    for block in range(BLOCKS):
        adjoint = adj[block]
        state_high, state_low = split(state)
        adj_high, adj_low = split(adjoint)
        first = block * 2 * TOK
        all_ref[4 * LOCAL + first : 4 * LOCAL + first + TOK, :] = state_high
        all_ref[4 * LOCAL + first + TOK : 4 * LOCAL + first + 2 * TOK, :] = state_low
        all_ref[6 * LOCAL + first : 6 * LOCAL + first + TOK, :] = adj_high
        all_ref[6 * LOCAL + first + TOK : 6 * LOCAL + first + 2 * TOK, :] = adj_low
        keep = keeps[block : block + 1]
        overlaps.append(jnp.sum(adjoint * state, axis=0, keepdims=True) * keep)
        ds_high, ds_low = ds[block]
        xe_high, xe_low = xe[block]
        all_ref[first : first + TOK, :] = ds_high
        all_ref[first + TOK : first + 2 * TOK, :] = ds_low
        all_ref[2 * LOCAL + first : 2 * LOCAL + first + TOK, :] = xe_high
        all_ref[2 * LOCAL + first + TOK : 2 * LOCAL + first + 2 * TOK, :] = xe_low
        gr = sums_ref[sums_rows(1, block), :] + (
            nt(jnp.concatenate([ds_high, ds_low], axis=1), twice(state_high)) + nt(ds_high, state_low)
        )
        gw = sums_ref[sums_rows(0, block), :] + (
            nt(jnp.concatenate([xe_high, xe_low], axis=1), twice(adj_high)) + nt(xe_high, adj_low)
        )
        kept = jnp.where(core == 0, gw, gr)
        given = jnp.where(core == 0, gr, gw)
        for half in range(2):
            out_rows = pl.ds(2 * block + half, 64, stride=16)
            own_rows = slice(64 * half, 64 * half + 64)
            keep_ref[out_rows, :] = kept[own_rows]
            give_ref[out_rows, :] = given[own_rows]
        state = state * keep + gains[block][0]
    overlaps = jnp.concatenate(overlaps, axis=0)
    top = overlaps.astype(BF16).astype(F32)
    middle = (overlaps - top).astype(BF16).astype(F32)
    bottom = overlaps - top - middle
    all_ref[8 * LOCAL : 8 * LOCAL + 32, :] = jnp.concatenate(
        [top, middle, bottom, jnp.zeros((8, LANES), F32)], axis=0
    ).astype(BF16)


def grads_kernel(decay_ref, data_ref, all_ref, grad_ref, out_ref, wide, misc):
    part, pair, core = my_place()
    slopes = slope_lanes(decay_ref, pair, TOK)
    base = 4 * LOCAL
    steps = data_ref[base : base + TOK, :].astype(F32)
    gates = data_ref[base + TOK : base + 2 * TOK, :].astype(F32) + data_ref[base + 2 * TOK : base + 3 * TOK, :].astype(F32)
    pos_cols = data_ref[base + 3 * TOK : base + 4 * TOK, :].astype(F32)
    pos_rows = pos_cols.T[:8]
    ends = grad_ref[LOCAL : LOCAL + TOK, :]
    lane = lane_iota(TOK)
    tail = all_ref[8 * LOCAL : 8 * LOCAL + 32, :].astype(F32)
    overlaps = tail[0:8] + tail[8:16] + tail[16:24]
    row_lane = lane_iota(8)
    row = lax.broadcasted_iota(jnp.int32, (8, LANES), 0)
    first = jnp.sum(jnp.where(row_lane < 64, overlaps, 0.0), axis=1, keepdims=True)
    second = jnp.sum(jnp.where(row_lane < 64, 0.0, overlaps), axis=1, keepdims=True)
    kept = jnp.where(row_lane == 2 * row, first, jnp.where(row_lane == 2 * row + 1, second, 0.0))
    sub = lax.broadcasted_iota(jnp.int32, (2 * LANES, LANES), 0) % LANES // 64
    pick_lane = lax.broadcasted_iota(jnp.int32, (2 * LANES, LANES), 1)
    per_head = jnp.zeros((3 * TOK, LANES), F32)
    for block in range(BLOCKS):
        rows = block_rows(block)
        lo = block * 2 * TOK

        def both(number):
            start = number * LOCAL + lo
            return all_ref[start : start + TOK, :].astype(F32) + all_ref[start + TOK : start + 2 * TOK, :].astype(F32)

        x = data_ref[rows, :].astype(F32)
        write = data_ref[2 * LOCAL + block * TOK : 2 * LOCAL + block * TOK + TOK, :]
        read = data_ref[3 * LOCAL + block * TOK : 3 * LOCAL + block * TOK + TOK, :]
        carried = nn(twice(write), all_ref[6 * LOCAL + lo : 6 * LOCAL + lo + 2 * TOK, :])
        recalled = nn(twice(read), all_ref[4 * LOCAL + lo : 4 * LOCAL + lo + 2 * TOK, :])
        act = grad_ref[rows, :] + block_lanes(ends, block, TOK) * carried
        wide[pl.ds(2 * block, 64, stride=16), :] = act[:64]
        wide[pl.ds(2 * block + 1, 64, stride=16), :] = act[64:]
        products = jnp.concatenate([both(0) * recalled, both(2) * carried, x * act], axis=0)
        pick = (pick_lane == 2 * block + sub).astype(F32).astype(BF16)
        per_head = per_head + nn(twice_split(products), pick)

    direct = per_head[2 * TOK :]
    read_high, read_low = split(per_head[:TOK].T[: 2 * BLOCKS])
    write_part = per_head[TOK : 2 * TOK].T[: 2 * BLOCKS]
    write_high, write_low = split(write_part)
    vectors = jnp.concatenate([read_high, read_low, write_high, write_low], axis=0)
    log_rows = grad_ref[LOCAL + 2 * TOK : LOCAL + 2 * TOK + 2 * BLOCKS, :]
    log_rows = log_rows + write_part + jnp.sum(write_part, axis=1, keepdims=True)
    owner = lax.broadcasted_iota(jnp.int32, (2 * BLOCKS, LANES), 0) // 2
    for block in range(BLOCKS):
        behind = (pos_cols[:, block : block + 1] >= pos_rows[block : block + 1, :]).astype(F32).astype(BF16)
        sums = nn(vectors, behind)
        added = (sums[0:16] + sums[16:32]) - (sums[32:48] + sums[48:64])
        log_rows = log_rows + jnp.where(owner == block, added, 0.0)
    log_grad = jnp.concatenate([log_rows, jnp.zeros((TOK - 2 * BLOCKS, LANES), F32)], axis=0).T
    log_grad = log_grad + jnp.sum(kept, axis=0, keepdims=True)
    grad_step = direct / steps + slopes * (log_grad - direct)
    grad_step = jnp.where(lane < 2 * BLOCKS, grad_step, 0.0).astype(BF16).astype(F32)
    grad_pre = grad_step * gates
    frames = []
    for frame in range(4):
        low_rows = slice(16 * frame, 16 * frame + 16)
        high_rows = slice(64 + 16 * frame, 80 + 16 * frame)
        frames.append(jnp.sum(grad_pre[low_rows] + grad_pre[high_rows], axis=0, keepdims=True))
    frames = sum(pltpu.roll(jnp.where(lane_iota(1) < 16, row, 0.0), 16 * i, 1) for i, row in enumerate(frames))
    frames_high = frames.astype(BF16).astype(F32)
    frames = frames_high + pltpu.roll(frames - frames_high, 64, 1)

    even = lane_iota(64) % 2 == 0
    top, bottom = grad_step[:64], grad_step[64:]
    shift = 16 * part
    row_one = pltpu.roll(jnp.where(even, top, pltpu.roll(bottom, 1, 1)), shift, 1)
    row_two = pltpu.roll(jnp.where(even, pltpu.roll(top, LANES - 1, 1), bottom), shift, 1)
    misc[...] = jnp.zeros((SEQ * 8, LANES), F32)
    misc[pl.ds(0, 64, stride=8), :] = row_one
    misc[pl.ds(1, 64, stride=8), :] = row_two
    misc[pl.ds(2, 64, stride=8), :] = jnp.broadcast_to(frames, (SEQ, LANES))
    out_ref[:, 0:16, :] = wide[...].reshape(SEQ, 16, LANES).astype(BF16)
    out_ref[:, 32:40, :] = misc[...].reshape(SEQ, 8, LANES).astype(BF16)


def join_kernel(in_ref, keep_ref, got_ref, out_ref):
    out_ref[:, 0:4] = in_ref[:, 0:16, :].reshape(SEQ, 4, 4, LANES)
    proj = (keep_ref[...] + got_ref[...]).reshape(SEQ, 16, LANES).astype(BF16)
    out_ref[:, 4:8] = proj.reshape(SEQ, 4, 4, LANES)
    out_ref[:, 8:9] = in_ref[:, 32:40, :].reshape(SEQ, 2, 4, LANES)[:, 0:1]


def proj_kernel(recv_ref, proj_ref, rest_ref):
    for part in range(PARTS):
        for core in range(2):
            total = recv_ref[place(part, core), 4:8].reshape(16, LANES).astype(F32)
            for high in range(1, 4):
                total = total + recv_ref[place(part, 2 * high + core), 4:8].reshape(16, LANES).astype(F32)
            proj_ref[16 * part : 16 * part + 16, LANES * core : LANES * core + LANES] = total.astype(BF16)
    rest_ref[:, 0:4] = recv_ref[:, 0:4]
    rest_ref[:, 4:5] = recv_ref[:, 8:9]


def finish_kernel(frame_ref, recv_ref, raw_ref, table_ref, act_ref, pre_ref, grad_ref, rows_ref):
    heads = raw_ref.shape[0]
    for pair in range(PAIRS):
        columns = slice(LANES * pair, LANES * pair + LANES)
        for part in range(PARTS):
            act_ref[16 * part : 16 * part + 16, columns] = recv_ref[place(part, pair), 0:4].reshape(16, LANES)
    lane = lane_iota(8)
    row = lax.broadcasted_iota(jnp.int32, (8, LANES), 0)
    sums = []
    for pair in range(PAIRS):
        rows = recv_ref[place(0, pair), 4:5].reshape(4, LANES).astype(F32)
        for part in range(1, PARTS):
            rows = rows + recv_ref[place(part, pair), 4:5].reshape(4, LANES).astype(F32)
        rows_ref[2 * pair : 2 * pair + 2, :] = rows[0:2]
        sums.append(rows[2:3])
    sums = jnp.concatenate(sums, axis=0)
    sums = sums + pltpu.roll(sums, 64, 1)
    per_frame = []
    for frame in range(4):
        total = jnp.zeros((8, LANES), F32)
        for head in range(2):
            inside = (lane // 16 == frame) & (lane % 2 == head)
            part_sum = jnp.sum(jnp.where(inside, sums, 0.0), axis=1, keepdims=True)
            total = jnp.where(lane == 2 * row + head, part_sum, total)
        per_frame.append(jnp.sum(total, axis=0, keepdims=True))
    pre = shifted_steps(frame_ref, raw_ref[...], table_ref[...])
    pre_ref[...] = rows_ref[...] * sigmoid(pre)
    per_head = jnp.concatenate(per_frame + [jnp.zeros((LANES - 4, LANES), F32)], axis=0).T
    steps = lax.broadcasted_iota(jnp.int32, grad_ref.shape, 1)
    grad = jnp.zeros(grad_ref.shape, F32)
    for frame in range(4):
        grad = grad + jnp.where(steps == frame_ref[frame], per_head[:heads, frame : frame + 1], 0.0)
    grad_ref[...] = grad


def total_kernel(own_ref, one_ref, two_ref, three_ref, write_ref, read_ref):
    even = own_ref[...].astype(F32) + two_ref[...].astype(F32)
    odd = one_ref[...].astype(F32) + three_ref[...].astype(F32)
    total = (even + odd).astype(BF16)
    write_ref[...] = total[:, :LANES]
    read_ref[...] = total[:, LANES:]


VMEM = pl.BlockSpec(memory_space=pltpu.VMEM)
SMEM = pl.BlockSpec(memory_space=pltpu.SMEM)


def call(kernel, name, in_specs, out_shape, scratch=(), params=PARAMS, out=VMEM):
    shapes = [jax.ShapeDtypeStruct(shape, dtype) for shape, dtype in out_shape]
    return pl.pallas_call(
        kernel,
        out_shape=shapes,
        in_specs=in_specs,
        out_specs=[out] * len(shapes),
        scratch_shapes=list(scratch),
        compiler_params=params,
        name=name,
    )


def shards(
    activations, grad_out, write_proj, read_proj, step_raw, step_table, decay_rate, frame_step, scan_order
):
    raw, table = step_raw.T, step_table.T
    rates = decay_rate.reshape(1, decay_rate.shape[0])
    swap_core = [(i, i ^ 1) for i in range(SEQ)]
    hbm = pl.BlockSpec(memory_space=pltpu.HBM)
    order = scan_order.reshape(1, TOK)
    sources = (order, frame_step, raw, table, write_proj, read_proj, activations, grad_out)
    (send,) = call(
        pack_kernel, "pack", [hbm] * 8, [((SEQ, 13, 4, LANES), BF16)],
        [(pltpu.SMEM if a is frame_step else pltpu.VMEM)(a.shape, a.dtype) for a in sources]
        + [
            pltpu.VMEM((SEQ, 13, 4, LANES), BF16),
            pltpu.VMEM((SEQ * 4, LANES), F32),
            pltpu.SemaphoreType.DMA((12,)),
        ],
        pltpu.CompilerParams(vmem_limit_bytes=62 * 1024 * 1024), hbm,
    )(*sources)
    recv = lax.all_to_all(send, "seq", 0, 0, tiled=True)
    (proj,) = call(cut_kernel, "cut", [VMEM], [((SEQ, 4, 4, LANES), BF16)])(recv)
    swap = lax.ppermute(proj, "seq", swap_core)
    wide = pltpu.VMEM((LOCAL, LANES), F32)
    bundle = ((4 * LOCAL + 4 * TOK, LANES), BF16)
    sums = ((LOCAL, LANES), F32)
    data, mine, weight = call(
        unpack_kernel, "unpack", [VMEM] * 2,
        [((2 * LOCAL + 4 * TOK, LANES), BF16), ((LOCAL, LANES), BF16), ((2 * LOCAL + 16, LANES), BF16)],
        [wide] * 3 + [pltpu.VMEM((SEQ * 4, LANES), F32)],
    )(rates, recv)
    (data,) = call(gather_kernel, "gather", [VMEM] * 3, [bundle], [wide])(mine, swap, data)
    (states,) = call(states_kernel, "states", [VMEM] * 2, [((PARTS, SLOT_STATE, LANES), BF16)])(data, weight)
    states = lax.all_to_all(states, "seq", 0, 0, tiled=True, axis_index_groups=STATE_GROUPS)
    inner, grad = call(
        inner_kernel, "inner", [VMEM] * 2,
        [
            ((2 * LOCAL + 8, LANES), F32),
            ((LOCAL + 3 * TOK, LANES), F32),
        ],
    )(rates, data)
    keep, give, pairs = call(
        outer_kernel, "outer", [VMEM] * 4,
        [sums] * 2 + [((8 * LOCAL + 32, LANES), BF16)],
        [pltpu.VMEM((BLOCKS, LANES, LANES), F32)],
    )(states, inner, data, grad)
    got = lax.ppermute(give, "seq", swap_core)
    (out,) = call(
        grads_kernel, "grads", [VMEM] * 4, [((SEQ, SLOT_OUT, LANES), BF16)],
        [wide, pltpu.VMEM((SEQ * 8, LANES), F32)],
    )(rates, data, pairs, grad)
    (out,) = call(join_kernel, "join", [VMEM] * 3, [((SEQ, 9, 4, LANES), BF16)])(out, keep, got)
    back = lax.all_to_all(out, "seq", 0, 0, tiled=True)
    proj, rest = call(
        proj_kernel, "proj", [VMEM], [((TOK, 2 * LANES), BF16), ((SEQ, 5, 4, LANES), BF16)]
    )(back)
    one, three, two = [lax.ppermute(proj, "head", [(i, (i + k) % 4) for i in range(4)]) for k in (1, 3, 2)]
    act, grad_pre, grad_table = call(
        finish_kernel, "finish", [SMEM] + [VMEM] * 3,
        [(activations.shape, BF16), (raw.shape, F32), (table.shape, F32)],
        [pltpu.VMEM((2 * PAIRS, LANES), F32)],
    )(frame_step, rest, raw, table)
    grad_write, grad_read = call(
        total_kernel, "total", [VMEM] * 4, [(write_proj.shape, BF16), (read_proj.shape, BF16)]
    )(proj, one, two, three)
    return (act, grad_write, grad_read, grad_pre.T, grad_table.T)


def solution(mesh):
    in_specs = (
        P("seq", "head"),
        P("seq", "head"),
        P("seq", None),
        P("seq", None),
        P("seq", "head"),
        P(None, "head"),
        P("head"),
        P(),
        P("seq"),
    )
    out_specs = (
        P("seq", "head"),
        P("seq", None),
        P("seq", None),
        P("seq", "head"),
        P(None, "head"),
    )
    return jax.shard_map(shards, mesh=mesh, in_specs=in_specs, out_specs=out_specs, check_vma=False)
```
